512 devices in a mesh: cells: 128 (over x, y_hi, z, core), vel: 4 (over y_lo).
Axes of the slice: x: 4, y: 8 (y_hi: 2, y_lo: 4; y = y_hi * 4 + y_lo), z: 8, core: 2. Of those that a mesh axis runs over, the one named last changes fastest.
Arguments:
- populations: float32 [2744, 128, 256], P('vel', 'cells'), may hold values from -6 to 6
- solid_mask: int32 [128, 256], P('cells'), may hold values 0 or 1
- collision: bfloat16 [2744, 2744], P('vel'), may hold values from -1 to 1
Outputs:
- evolved: float32 [2744, 128, 256], P('vel', 'cells')
The draws below stay inside these ranges and needn't reach their ends.
All inputs are finite; a program needn't handle non-finite values. No bound on the sum of `solid_mask` on one device may be relied on, other than what follows from the above.
Results may differ from the reference program's by a relative error of at most 0.0031.
Values may be sent and summed in bfloat16 or wider, within the bound.
No kernel may reach another device: no remote copies, remote signals or barrier semaphores. Data moves between devices by JAX's collectives and lax.ppermute only.
A program may use at most 128 MiB of HBM per device.

```python
import math
import jax
import jax.numpy as jnp
from jax import lax

K = 14
STEPS = 2
NY = 16
NZ = 16
Q = 2744
NX = 128


def draw_collision(key, part):
    first_key, second_key = jax.random.split(jax.random.fold_in(key, 11))
    diagonal = jax.random.uniform(first_key, (Q,), jnp.float32, 0.4, 0.9)
    spread = jax.random.normal(second_key, (Q, Q), jnp.float32) * (0.6 / math.sqrt(Q))
    velocity_ids = jnp.arange(Q)
    identity = (velocity_ids[:, None] == velocity_ids[None, :]).astype(jnp.float32)
    matrix = spread * (1.0 - identity) + identity * diagonal[:, None]
    return matrix.astype(jnp.bfloat16)


def plant(drawn, own_key, smallest, largest):
    longest = drawn.shape.index(max(drawn.shape))
    spots = []
    for shift in (0, 1):
        where = [jax.random.randint(jax.random.fold_in(own_key, axis), (), 0, length) for axis, length in enumerate(drawn.shape)]
        where[longest] = (where[longest] + shift) % drawn.shape[longest]
        spots.append(tuple(where))
    return drawn.at[spots[0]].set(smallest).at[spots[1]].set(largest)


def shard_levels(stream_key, shape, cuts, least, top_value):
    def one(position, parts):
        draws = jax.random.uniform(jax.random.fold_in(jax.random.fold_in(stream_key, 6), position), (parts,), jnp.float32, least / len(cuts), top_value / len(cuts))
        return jnp.repeat(jnp.exp(draws), shape[position] // parts).reshape((-1,) + (1,) * (len(shape) - position - 1))

    level = one(*cuts[0])
    for cut in cuts[1:]:
        level = level * one(*cut)
    return level


def noise(rng, dims, deviation, bound, shards=(), kind=jnp.bfloat16):
    drawn = deviation * jax.random.normal(rng, dims, jnp.float32)
    if shards:
        drawn = drawn * shard_levels(rng, dims, shards, -0.22, 0.18)
    return jnp.clip(drawn, -bound, bound).astype(kind)


def setup_inputs(seed: int = 0) -> dict:
    key_list = jax.random.split(jax.random.key(seed), 4)
    populations = noise(key_list[0], (Q, NX, NY * NZ), 1.0, 6.0, ((0, 4), (1, 128)), jnp.float32)
    solid_mask = plant((jax.random.randint(key_list[1], (NX, NY * NZ), 0, 10) < 3).astype(jnp.int32), jax.random.fold_in(key_list[1], 1), 0, 1)
    collision = draw_collision(jax.random.fold_in(key_list[3], 71), 0)
    return dict(populations=populations, solid_mask=solid_mask, collision=collision)


def velocity_terms(first_row, row_count):
    velocity_ids = first_row + lax.iota(jnp.int32, row_count)
    components = (velocity_ids // (K * K), (velocity_ids // K) % K, velocity_ids % K)
    centre = (K - 1) / 2.0
    result = []
    for component in components:
        shifted = component.astype(jnp.float32) - centre
        factor = (0.3 * jnp.abs(shifted) / centre)[:, None, None]
        result.append((factor, (shifted > 0)[:, None, None]))
    return result


def lower_y(values):
    return jnp.roll(values, NZ, axis=-1)


def upper_y(values):
    return jnp.roll(values, -NZ, axis=-1)


def lower_z(values):
    z_place = lax.iota(jnp.int32, values.shape[-1]) % NZ
    return jnp.where(z_place == 0, jnp.roll(values, 1 - NZ, axis=-1), jnp.roll(values, 1, axis=-1))


def upper_z(values):
    z_place = lax.iota(jnp.int32, values.shape[-1]) % NZ
    return jnp.where(z_place == NZ - 1, jnp.roll(values, NZ - 1, axis=-1), jnp.roll(values, -1, axis=-1))


def stream(tile_rows, fluid_cells):
    mirror = jnp.flip(tile_rows, axis=0)
    neighbours = (
        (jnp.roll(tile_rows, 1, axis=1), jnp.roll(tile_rows, -1, axis=1),
         jnp.roll(fluid_cells, 1, axis=0), jnp.roll(fluid_cells, -1, axis=0)),
        (lower_y(tile_rows), upper_y(tile_rows), lower_y(fluid_cells), upper_y(fluid_cells)),
        (lower_z(tile_rows), upper_z(tile_rows), lower_z(fluid_cells), upper_z(fluid_cells)),
    )
    outflow = None
    for (factor, positive), (lower_side, upper_side, open_lower, open_upper) in zip(velocity_terms(0, tile_rows.shape[0]), neighbours):
        upwind = jnp.where(positive, jnp.where(open_lower > 0, lower_side, mirror), jnp.where(open_upper > 0, upper_side, mirror))
        flux_term = factor * (tile_rows - upwind)
        outflow = flux_term if outflow is None else outflow + flux_term
    return (tile_rows - outflow) * fluid_cells


def collide(collision, lowered):
    slabs = jnp.moveaxis(lowered, 1, 0)

    def one_slab(slab):
        return jnp.dot(collision, slab, preferred_element_type=jnp.float32)

    return jnp.moveaxis(lax.map(one_slab, slabs), 0, 1)


def reference(populations, solid_mask, collision):
    fluid_cells = (solid_mask == 0).astype(jnp.float32)
    state = populations
    for step_index in range(STEPS):
        read = stream(state, fluid_cells)
        lowered = read.astype(jnp.bfloat16)
        collided = collide(collision, lowered)
        state = stream(collided, fluid_cells)
    return state
```

```python
import jax
import jax.numpy as jnp
from jax import lax
from jax.sharding import PartitionSpec as P

K = 14
STEPS = 2
NZ = 16
BOTH = ("cells", "vel")


def velocity_terms(first_row, row_count):
    velocity_ids = first_row + lax.iota(jnp.int32, row_count)
    components = (velocity_ids // (K * K), velocity_ids // K % K, velocity_ids % K)
    centre = (K - 1) / 2.0
    result = []
    for component in components:
        shifted = component.astype(jnp.float32) - centre
        factor = (0.3 * jnp.abs(shifted) / centre)[:, None]
        result.append((factor, (shifted > 0)[:, None]))
    return result


def lower_y(values):
    return jnp.roll(values, NZ, axis=-1)


def upper_y(values):
    return jnp.roll(values, -NZ, axis=-1)


def lower_z(values):
    z_place = lax.iota(jnp.int32, values.shape[-1]) % NZ
    return jnp.where(z_place == 0, jnp.roll(values, 1 - NZ, axis=-1), jnp.roll(values, 1, axis=-1))


def upper_z(values):
    z_place = lax.iota(jnp.int32, values.shape[-1]) % NZ
    return jnp.where(
        z_place == NZ - 1, jnp.roll(values, NZ - 1, axis=-1), jnp.roll(values, -1, axis=-1)
    )


def upwind_layer(array):
    cells, vel = lax.axis_size("cells"), lax.axis_size("vel")
    pairs = []
    for cell in range(cells):
        for part in range(vel):
            target = (cell + (1 if 2 * part >= vel else -1)) % cells
            pairs.append((cell * vel + part, target * vel + part))
    return lax.ppermute(array, BOTH, pairs)


def from_mirror(array):
    vel = lax.axis_size("vel")
    return lax.ppermute(array, "vel", [(i, vel - 1 - i) for i in range(vel)])


def gathered(array):
    vel = lax.axis_size("vel")
    mine = lax.axis_index("vel")
    parts = [array]
    for step in range(1, vel):
        parts.append(lax.ppermute(array, "vel", [(i, i ^ step) for i in range(vel)]))
    return [lax.select_n(mine, *[parts[i ^ j] for i in range(vel)]) for j in range(vel)]


def stream(rows, terms, fluid, open_x):
    low = rows.astype(jnp.bfloat16)
    mirror = jnp.flip(from_mirror(low), axis=0).astype(jnp.float32)
    layer = upwind_layer(low).astype(jnp.float32)
    upwind = [jnp.where(open_x > 0, layer, mirror)]
    for (factor, positive), (lower, upper) in zip(terms[1:], ((lower_y, upper_y), (lower_z, upper_z))):
        upwind.append(
            jnp.where(
                positive,
                jnp.where(lower(fluid) > 0, lower(rows), mirror),
                jnp.where(upper(fluid) > 0, upper(rows), mirror),
            )
        )
    outflow = 0.0
    for (factor, _), value in zip(terms, upwind):
        outflow = outflow + factor * (rows - value)
    return (rows - outflow) * fluid


def per_device(populations, solid_mask, collision):
    row_count = populations.shape[0]
    terms = velocity_terms(lax.axis_index("vel") * row_count, row_count)
    open_x = (upwind_layer(solid_mask) == 0).astype(jnp.float32)
    fluid = (solid_mask == 0).astype(jnp.float32)
    state = populations[:, 0, :]
    for _ in range(STEPS):
        read = stream(state, terms, fluid, open_x)
        blocks = gathered(read.astype(jnp.bfloat16))
        collided = jnp.dot(
            collision, jnp.concatenate(blocks, axis=0), preferred_element_type=jnp.float32
        )
        state = stream(collided, terms, fluid, open_x)
    return state[:, None, :]


def solution(mesh):
    in_specs = (P("vel", "cells", None), P("cells", None), P("vel", None))
    out_specs = P("vel", "cells", None)
    return jax.shard_map(
        per_device, mesh=mesh, in_specs=in_specs, out_specs=out_specs, check_vma=False
    )
```

```python
import jax
import jax.numpy as jnp
from jax import lax
from jax.experimental import pallas as pl
from jax.experimental.pallas import tpu as pltpu
from jax.sharding import PartitionSpec as P


K = 14
STEPS = 2
NZ = 16
BOTH = ("cells", "vel")
ROWS = 686
PAD = 704
CHUNK = 88
PART = 2 * CHUNK
EDGE = 96
LANES = 128
RING = 16
F32 = jnp.float32
BF16 = jnp.bfloat16
PARAMS = pltpu.CompilerParams(vmem_limit_bytes=40 * 1024 * 1024)


def pairs_of(target):
    pairs = []
    for cell in range(128):
        for part in range(4):
            to_cell, to_part = target(cell, part)
            pairs.append((cell * 4 + part, to_cell * 4 + to_part))
    return pairs


def to_sibling(array):
    return lax.ppermute(array, BOTH, pairs_of(lambda cell, part: (cell ^ 1, part)))


def to_neighbour(array):
    def target(cell, part):
        other = (cell - 1 if cell % 2 == 0 else cell + 1) % 128
        return other, part if (other // RING) % 2 == (cell // RING) % 2 else 3 - part

    return lax.ppermute(array, BOTH, pairs_of(target))


def to_mirror(array):
    return lax.ppermute(array, "vel", [(i, 3 - i) for i in range(4)])


def to_side(array):
    return lax.ppermute(array, "vel", [(i, i ^ 1) for i in range(4)])


def call(kernel, outs, flags, *arrays, flops=0):
    moved = sum(x.size * x.dtype.itemsize for x in arrays)
    moved += sum(s[0] * s[1] * jnp.dtype(d).itemsize for s, d in outs)
    vmem = pl.BlockSpec(memory_space=pltpu.VMEM)
    result = pl.pallas_call(
        kernel,
        out_shape=[jax.ShapeDtypeStruct(shape, dtype) for shape, dtype in outs],
        in_specs=[pl.BlockSpec(memory_space=pltpu.SMEM)] + [vmem] * len(arrays),
        out_specs=[vmem] * len(outs),
        compiler_params=PARAMS,
        cost_estimate=pl.CostEstimate(flops=flops, bytes_accessed=moved, transcendentals=0),
    )(flags, *arrays)
    return result


def roll(values, shift):
    return pltpu.roll(values, shift % values.shape[1], 1)


def order_matrix(low):
    row = lax.broadcasted_iota(jnp.int32, (PAD, PAD), 0)
    column = lax.broadcasted_iota(jnp.int32, (PAD, PAD), 1)
    wanted = jnp.where(low, row, ROWS - 1 - row)
    return jnp.where((column == wanted) & (row < ROWS), 1.0, 0.0).astype(BF16)


def reordered(order, values):
    total = jnp.zeros(values.shape, F32)
    for _ in range(3):
        part = values.astype(BF16)
        total += jnp.dot(order, part, preferred_element_type=F32)
        values = values - part.astype(F32)
    return total


def terms(block, chunk):
    row = CHUNK * chunk + lax.broadcasted_iota(jnp.int32, (CHUNK, LANES), 0)
    ids = ROWS * block + row
    upper = (ids * 4682) >> 16
    k_z = ids - K * upper
    k_x = (upper * 4682) >> 16
    k_y = upper - K * k_x
    centre = (K - 1) / 2.0

    def factor(k):
        return jnp.abs(k.astype(F32) - centre) * (0.3 / centre)

    return (factor(k_x), factor(k_y), factor(k_z)), k_y >= K // 2, k_z >= K // 2


def lanes_of(rows):
    return lax.broadcasted_iota(jnp.int32, (rows, LANES), 1)


def lower_z(values):
    z_place = lax.broadcasted_iota(jnp.int32, values.shape, 1) % NZ
    return jnp.where(z_place == 0, roll(values, 1 - NZ), roll(values, 1))


def upper_z(values):
    z_place = lax.broadcasted_iota(jnp.int32, values.shape, 1) % NZ
    return jnp.where(z_place == NZ - 1, roll(values, NZ - 1), roll(values, -1))


def pack_edge(values, positive, chunk):
    edge = jnp.where(positive, roll(values, NZ), values)
    return jnp.where(lanes_of(CHUNK) // NZ == chunk, roll(edge, NZ * chunk), 0.0)


def edge_block(packed):
    return jnp.concatenate([packed, jnp.zeros((EDGE - CHUNK, LANES), F32)], axis=0).astype(BF16)


def prepare_kernel(flags, populations, solid, own, own_edge, message, masks):
    low, block, half = flags[0] == 1, flags[2], flags[3]
    ordered = reordered(order_matrix(low), populations[...])
    left, right = ordered[:, :LANES], ordered[:, LANES:]
    mine = jnp.where(half == 0, left, right)
    rest = jnp.where(half == 0, right, left)
    own[...] = mine
    edges = jnp.zeros((CHUNK, LANES), F32)
    sent = jnp.zeros((CHUNK, LANES), F32)
    for chunk in range(PAD // CHUNK):
        rows = slice(CHUNK * chunk, CHUNK * (chunk + 1))
        _, positive, _ = terms(block, chunk)
        positive = jnp.where(positive, 1, 0) == flags[0]
        edges += pack_edge(rest[rows], positive, chunk)
        sent += pack_edge(mine[rows], positive, chunk)
    own_edge[...] = edges
    message[:PAD] = rest.astype(BF16)
    message[PAD:] = edge_block(sent)
    fluid = jnp.where(jnp.broadcast_to(solid[...], (8, 2 * LANES)) == 0, 1.0, 0.0)
    place = lax.broadcasted_iota(jnp.int32, (8, 2 * LANES), 0)
    found = jnp.zeros((8, 2 * LANES), F32)
    near = (fluid, roll(fluid, NZ), roll(fluid, -NZ), lower_z(fluid), upper_z(fluid))
    for index, value in enumerate(near):
        found = jnp.where(place == index, value, found)
    masks[...] = jnp.where(half == 0, found[:, :LANES], found[:, LANES:])


def faces_kernel(flags, own, received, masks, sibling, neighbour):
    same = flags[0] == flags[1]
    row = lax.broadcasted_iota(jnp.int32, (16, LANES), 0)
    fluid = jnp.where(row == 0, jnp.broadcast_to(masks[0:1, :], (16, LANES)), 0.0).astype(BF16)
    mine, theirs = own[...], received[:PAD].astype(F32)
    sibling[:PAD] = jnp.where(same, theirs, mine).astype(BF16)
    neighbour[:PAD] = jnp.where(same, mine, theirs).astype(BF16)
    sibling[PAD:] = fluid
    neighbour[PAD:] = fluid


def half_stream(flags, a, b, sibling, neighbour, edge_a, edge_b, masks, emit):
    even = flags[1] == 1
    wide = [jnp.broadcast_to(masks[i : i + 1], (CHUNK, LANES)) for i in range(7)]
    fluid, open_y, open_z, open_x = wide[0], wide[1:3], wide[3:5], wide[5:7]
    lane = lanes_of(CHUNK)
    for part in range(PAD // PART):
        span = slice(PART * part, PART * (part + 1))
        part_a, part_b = a(span), b(span)
        near, far = sibling[span].astype(F32), neighbour[span].astype(F32)
        above, below = jnp.where(even, near, far), jnp.where(even, far, near)
        results = []
        for index in range(2):
            chunk = 2 * part + index
            rows = slice(CHUNK * index, CHUNK * (index + 1))
            factors, up_y, up_z = terms(flags[2], chunk)

            def one(values, mirror, layer, edge, up_y, up_z, open_here):
                put = jnp.where(up_y, roll(edge, -NZ * chunk), roll(edge, -NZ * (chunk + 1)))
                outside = (up_y & (lane < NZ)) | (~up_y & (lane >= LANES - NZ))
                near_y = jnp.where(up_y, roll(values, NZ), roll(values, -NZ))
                near_y = jnp.where(outside, put, near_y)
                near_z = jnp.where(up_z, lower_z(values), upper_z(values))
                upwind_x = jnp.where(open_here > 0, layer, mirror)
                upwind_y = jnp.where(jnp.where(up_y, *open_y) > 0, near_y, mirror)
                upwind_z = jnp.where(jnp.where(up_z, *open_z) > 0, near_z, mirror)
                outflow = factors[0] * (values - upwind_x)
                outflow += factors[1] * (values - upwind_y)
                outflow += factors[2] * (values - upwind_z)
                return (values - outflow) * fluid

            here_a, here_b = part_a[rows], part_b[rows]
            results.append(
                (
                    one(here_a, here_b, above[rows], edge_a, up_y, up_z, open_x[1]),
                    one(here_b, here_a, below[rows], edge_b, ~up_y, ~up_z, open_x[0]),
                    up_y,
                )
            )
        emit(part, results)


def joined(results, index):
    return jnp.concatenate([result[index] for result in results], axis=0)


def first_kernel(flags, own, own_edge, received, sibling, neighbour, masks_in, lowered, masks_out):
    low, even = flags[0] == 1, flags[1] == 1
    near, far = sibling[PAD:].astype(F32)[:1], neighbour[PAD:].astype(F32)[:1]
    place = lax.broadcasted_iota(jnp.int32, (8, LANES), 0)
    masks = masks_in[...]
    masks = jnp.where(place == 5, jnp.where(even, far, near), masks)
    masks = jnp.where(place == 6, jnp.where(even, near, far), masks)
    masks_out[...] = masks
    edge_own, edge_other = own_edge[...], received[PAD:].astype(F32)[:CHUNK]

    def emit(part, results):
        span = PART * part
        lowered[span : span + PART] = joined(results, 0).astype(BF16)
        lowered[PAD + span : PAD + span + PART] = joined(results, 1).astype(BF16)

    half_stream(
        flags,
        lambda span: jnp.where(low, own[span], received[span].astype(F32)),
        lambda span: jnp.where(low, received[span].astype(F32), own[span]),
        sibling,
        neighbour,
        jnp.where(low, edge_own, edge_other),
        jnp.where(low, edge_other, edge_own),
        masks,
        emit,
    )


class Sender:
    def __init__(self, flags, a, b, sibling, neighbour, edges):
        self.even = flags[1] == 1
        self.refs = a, b, sibling, neighbour
        self.edges = edges
        self.packed = [jnp.zeros((CHUNK, LANES), F32)] * 2

    def __call__(self, part, results):
        span = slice(PART * part, PART * (part + 1))
        a, b, sibling, neighbour = self.refs
        rows_a, rows_b = joined(results, 0), joined(results, 1)
        a[span], b[span] = rows_a, rows_b
        sibling[span] = jnp.where(self.even, rows_b, rows_a).astype(BF16)
        neighbour[span] = jnp.where(self.even, rows_a, rows_b).astype(BF16)
        for index, (chunk_a, chunk_b, up_y) in enumerate(results):
            self.packed[0] += pack_edge(chunk_a, up_y, 2 * part + index)
            self.packed[1] += pack_edge(chunk_b, ~up_y, 2 * part + index)
        if part == PAD // PART - 1:
            self.edges[:EDGE] = edge_block(self.packed[0])
            self.edges[EDGE:] = edge_block(self.packed[1])


def received_edges(edges):
    values = edges[...].astype(F32)
    return values[:CHUNK], values[EDGE : EDGE + CHUNK]


def between_kernel(flags, a, b, sibling, neighbour, edges, masks, *outs):
    emit = Sender(flags, *outs)
    half_stream(
        flags, lambda s: a[s], lambda s: b[s], sibling, neighbour, *received_edges(edges), masks[...], emit
    )


def lower_kernel(flags, a, b, sibling, neighbour, edges, masks, lowered):
    def emit(part, results):
        span = PART * part
        lowered[span : span + PART] = joined(results, 0).astype(BF16)
        lowered[PAD + span : PAD + span + PART] = joined(results, 1).astype(BF16)

    half_stream(
        flags, lambda s: a[s], lambda s: b[s], sibling, neighbour, *received_edges(edges), masks[...], emit
    )


def last_kernel(flags, a, b, sibling, neighbour, edges, masks, kept, message):
    low = flags[0] == 1

    def emit(part, results):
        span = slice(PART * part, PART * (part + 1))
        rows_a, rows_b = joined(results, 0), joined(results, 1)
        kept[span] = jnp.where(low, rows_a, rows_b)
        message[span] = jnp.where(low, rows_b, rows_a).astype(BF16)

    half_stream(
        flags, lambda s: a[s], lambda s: b[s], sibling, neighbour, *received_edges(edges), masks[...], emit
    )


def collide_kernel(flags, matrix, lowered, other, rows_out):
    swapped = flags[2] == 1
    first = jnp.where(swapped, other[...], lowered[...])
    second = jnp.where(swapped, lowered[...], other[...])
    for part in range(PAD // PART):
        span = slice(PART * part, PART * (part + 1))
        total = jnp.dot(matrix[span, : 2 * PAD], first, preferred_element_type=F32)
        total += jnp.dot(matrix[span, 2 * PAD :], second, preferred_element_type=F32)
        rows_out[span] = total


def collide_send_kernel(flags, own, mine, theirs, lowered, other, *outs):
    low = flags[0] == 1
    swapped = flags[2] != flags[4]
    first = jnp.where(swapped, other[...], lowered[...])
    second = jnp.where(swapped, lowered[...], other[...])
    emit = Sender(flags, *outs)
    for part in range(PAD // PART):
        span = slice(PART * part, PART * (part + 1))
        total = jnp.dot(mine[span], first, preferred_element_type=F32)
        total += jnp.dot(theirs[span], second, preferred_element_type=F32)
        own_rows = own[span]
        rows_a, rows_b = jnp.where(low, own_rows, total), jnp.where(low, total, own_rows)
        results = []
        for index in range(2):
            rows = slice(CHUNK * index, CHUNK * (index + 1))
            results.append((rows_a[rows], rows_b[rows], terms(flags[2], 2 * part + index)[1]))
        emit(part, results)


def reorder_kernel(flags, kept, ordered):
    ordered[...] = reordered(order_matrix(flags[0] == 1), kept[...])


def finish_kernel(flags, kept, received, evolved):
    order = order_matrix(flags[0] == 1)
    rest = jnp.dot(order, received[...], preferred_element_type=F32)
    mine = kept[...]
    half = flags[3]
    evolved[:, :LANES] = jnp.where(half == 0, mine, rest)[:ROWS]
    evolved[:, LANES:] = jnp.where(half == 0, rest, mine)[:ROWS]


def place(rows, columns, wanted):
    return (lax.broadcasted_iota(jnp.int32, (rows, columns), 0) == wanted[None, :]).astype(BF16)


def chosen(left, right):
    return jnp.dot(left, right, preferred_element_type=BF16)


def column_half(wide, block):
    column = lax.iota(jnp.int32, PAD)
    inside = column < ROWS
    start_a, start_b = 640 * block, jnp.where(block == 1, 1280, 2048)
    part_a = lax.dynamic_slice(wide, (0, start_a), (wide.shape[0], 768))
    part_b = lax.dynamic_slice(wide, (0, start_b), (wide.shape[0], 896))
    wanted_a = jnp.where(inside, ROWS * block + column - start_a, -1)
    wanted_b = jnp.where(inside, 4 * ROWS - 1 - ROWS * block - column - start_b + 768, -1)
    return chosen(
        jnp.concatenate([part_a, part_b], axis=1),
        place(768 + 896, 2 * PAD, jnp.concatenate([wanted_a, wanted_b])),
    )


def padded_columns(matrix):
    return jnp.pad(matrix, ((0, 0), (0, 2944 - matrix.shape[1])))


def per_device(populations, solid_mask, collision):
    cell, vel = lax.axis_index("cells"), lax.axis_index("vel")
    low = (vel < 2).astype(jnp.int32)
    core, z = cell % 2, cell // 2 % 8
    block = jnp.minimum(vel, 3 - vel)
    half = (1 - low) ^ (cell // RING % 2)
    flags = jnp.stack([low, 1 - core, block, half, core]).astype(jnp.int32)

    row = CHUNK * z + lax.iota(jnp.int32, CHUNK)
    wanted = jnp.where(row < ROWS, jnp.where(low == 1, row, ROWS - 1 - row), -1)
    window = chosen(place(ROWS, CHUNK, wanted).T, collision)
    piece = to_mirror(column_half(padded_columns(window), core))
    rings = [
        [(line * 8 + step) * 2 + side for step in range(8)] for line in range(8) for side in range(2)
    ]
    mine = lax.all_gather(piece, "cells", axis=0, tiled=True, axis_index_groups=rings)
    theirs = to_sibling(mine)

    padded = jnp.pad(populations[:, 0, :], ((0, PAD - ROWS), (0, 0)))
    own, own_edge, message, masks = call(
        prepare_kernel,
        [((PAD, LANES), F32), ((CHUNK, LANES), F32), ((PAD + EDGE, LANES), BF16), ((8, LANES), F32)],
        flags, padded, solid_mask, flops=2 * 3 * PAD * PAD * 256,
    )
    received = to_mirror(message)
    faces = [((PAD + 16, LANES), BF16)] * 2
    sibling, neighbour = call(faces_kernel, faces, flags, own, received, masks)
    neighbour, sibling = to_neighbour(neighbour), to_sibling(sibling)

    row = lax.iota(jnp.int32, PAD)
    wanted = jnp.where(row < ROWS, jnp.where(low == 1, row, ROWS - 1 - row), -1)
    ordered = padded_columns(chosen(place(ROWS, PAD, wanted).T, collision))
    matrix = jnp.concatenate([column_half(ordered, 0), column_half(ordered, 1)], axis=1)

    lowered, masks = call(
        first_kernel,
        [((2 * PAD, LANES), BF16), ((8, LANES), F32)],
        flags, own, own_edge, received, sibling, neighbour, masks, flops=100 * PAD * 256,
    )
    sends = [((PAD, LANES), F32)] * 2 + [((PAD, LANES), BF16)] * 2 + [((2 * EDGE, LANES), BF16)]
    multiply = 2 * PAD * 4 * PAD * LANES
    for step in range(STEPS):
        other = to_side(lowered)
        (own,) = call(
            collide_kernel, [((PAD, LANES), F32)], flags, matrix, lowered, other, flops=multiply
        )
        a, b, sibling, neighbour, edges = call(
            collide_send_kernel, sends, flags, own, mine, theirs, lowered, other, flops=multiply
        )
        near = to_neighbour(neighbour), to_mirror(edges), to_sibling(sibling)
        if step == STEPS - 1:
            break
        a, b, sibling, neighbour, edges = call(
            between_kernel, sends, flags, a, b, near[2], near[0], near[1], masks, flops=100 * PAD * 256
        )
        near = to_neighbour(neighbour), to_mirror(edges), to_sibling(sibling)
        (lowered,) = call(
            lower_kernel, [((2 * PAD, LANES), BF16)],
            flags, a, b, near[2], near[0], near[1], masks, flops=100 * PAD * 256,
        )
    kept, message = call(
        last_kernel, [((PAD, LANES), F32), ((PAD, LANES), BF16)],
        flags, a, b, near[2], near[0], near[1], masks, flops=100 * PAD * 256,
    )
    received = to_mirror(message)
    (kept,) = call(
        reorder_kernel, [((PAD, LANES), F32)], flags, kept, flops=2 * 3 * PAD * PAD * LANES
    )
    (evolved,) = call(
        finish_kernel, [((ROWS, 2 * LANES), F32)], flags, kept, received, flops=2 * PAD * PAD * LANES
    )
    return evolved[:, None, :]


def solution(mesh):
    in_specs = (P("vel", "cells", None), P("cells", None), P("vel", None))
    out_specs = P("vel", "cells", None)
    return jax.shard_map(
        per_device, mesh=mesh, in_specs=in_specs, out_specs=out_specs, check_vma=False
    )
```

```python
import math

import jax
import jax.numpy as jnp
from jax import lax
from jax.experimental import pallas as pl
from jax.experimental.pallas import tpu as pltpu
from jax.sharding import PartitionSpec as P


K = 14
STEPS = 2
NZ = 16
BOTH = ("cells", "vel")
ROWS = 686
PAD = 704
CHUNK = 88
PART = 2 * CHUNK
EDGE = 96
LANES = 128
RING = 16
F32 = jnp.float32
BF16 = jnp.bfloat16
PARAMS = pltpu.CompilerParams(vmem_limit_bytes=40 * 1024 * 1024)


def pairs_of(target):
    pairs = []
    for cell in range(128):
        for part in range(4):
            to_cell, to_part = target(cell, part)
            pairs.append((cell * 4 + part, to_cell * 4 + to_part))
    return pairs


def to_sibling(array):
    return lax.ppermute(array, BOTH, pairs_of(lambda cell, part: (cell ^ 1, part)))


def to_neighbour(array):
    def target(cell, part):
        other = (cell - 1 if cell % 2 == 0 else cell + 1) % 128
        return other, part if (other // RING) % 2 == (cell // RING) % 2 else 3 - part

    return lax.ppermute(array, BOTH, pairs_of(target))


def to_mirror(array):
    return lax.ppermute(array, "vel", [(i, 3 - i) for i in range(4)])


def to_side(array):
    return lax.ppermute(array, "vel", [(i, i ^ 1) for i in range(4)])


def call(kernel, outs, flags, *arrays, flops=0):
    moved = sum(x.size * x.dtype.itemsize for x in arrays)
    moved += sum(math.prod(shape) * jnp.dtype(dtype).itemsize for shape, dtype in outs)
    vmem = pl.BlockSpec(memory_space=pltpu.VMEM)
    result = pl.pallas_call(
        kernel,
        out_shape=[jax.ShapeDtypeStruct(shape, dtype) for shape, dtype in outs],
        in_specs=[pl.BlockSpec(memory_space=pltpu.SMEM)] + [vmem] * len(arrays),
        out_specs=[vmem] * len(outs),
        compiler_params=PARAMS,
        cost_estimate=pl.CostEstimate(flops=flops, bytes_accessed=moved, transcendentals=0),
    )(flags, *arrays)
    return result


def roll(values, shift):
    return pltpu.roll(values, shift % values.shape[1], 1)


def order_matrix(low):
    row = lax.broadcasted_iota(jnp.int32, (PAD, PAD), 0)
    column = lax.broadcasted_iota(jnp.int32, (PAD, PAD), 1)
    wanted = jnp.where(low, row, ROWS - 1 - row)
    return jnp.where((column == wanted) & (row < ROWS), 1.0, 0.0).astype(BF16)


def reordered(order, values):
    total = jnp.zeros(values.shape, F32)
    for _ in range(3):
        part = values.astype(BF16)
        total += jnp.dot(order, part, preferred_element_type=F32)
        values = values - part.astype(F32)
    return total


def signed_factors(block, chunk):
    row = CHUNK * chunk + lax.broadcasted_iota(jnp.int32, (CHUNK, LANES), 0)
    ids = ROWS * block + row
    upper = (ids * 4682) >> 16
    k_z = ids - K * upper
    k_x = (upper * 4682) >> 16
    k_y = upper - K * k_x
    centre = (K - 1) / 2.0
    x, y, z = ((k.astype(F32) - centre) * (0.3 / centre) for k in (k_x, k_y, k_z))
    return jnp.abs(x), y, z


def lanes_of(rows):
    return lax.broadcasted_iota(jnp.int32, (rows, LANES), 1)


def lower_z(values):
    z_place = lax.broadcasted_iota(jnp.int32, values.shape, 1) % NZ
    return jnp.where(z_place == 0, roll(values, 1 - NZ), roll(values, 1))


def upper_z(values):
    z_place = lax.broadcasted_iota(jnp.int32, values.shape, 1) % NZ
    return jnp.where(z_place == NZ - 1, roll(values, NZ - 1), roll(values, -1))


def picked(values, lanes):
    return jnp.take_along_axis(values, lanes, axis=1, mode="promise_in_bounds")


def pack_edge(packed, values, positive, chunk, lane):
    place = lane & (NZ - 1)
    edge = picked(values, jnp.where(positive, place + LANES - NZ, place))
    return jnp.where((lane >> 4) == chunk, edge, packed)


def edge_block(packed):
    return jnp.concatenate([packed, jnp.zeros((EDGE - CHUNK, LANES), F32)], axis=0).astype(BF16)


def prepare_kernel(flags, populations, solid, own, own_edge, message, masks, factors):
    low, block, half = flags[0] == 1, flags[2], flags[3]
    ordered = reordered(order_matrix(low), populations[...])
    left, right = ordered[:, :LANES], ordered[:, LANES:]
    mine = jnp.where(half == 0, left, right)
    rest = jnp.where(half == 0, right, left)
    own[...] = mine
    edges = jnp.zeros((CHUNK, LANES), F32)
    sent = jnp.zeros((CHUNK, LANES), F32)
    lane = lanes_of(CHUNK)
    for chunk in range(PAD // CHUNK):
        rows = slice(CHUNK * chunk, CHUNK * (chunk + 1))
        x, y, z = signed_factors(block, chunk)
        factors[0, rows], factors[1, rows], factors[2, rows] = x, y, z
        positive = jnp.where(low, y, -y) > 0
        edges = pack_edge(edges, rest[rows], positive, chunk, lane)
        sent = pack_edge(sent, mine[rows], positive, chunk, lane)
    own_edge[...] = edges
    message[:PAD] = rest.astype(BF16)
    message[PAD:] = edge_block(sent)
    fluid = jnp.where(jnp.broadcast_to(solid[...], (8, 2 * LANES)) == 0, 1.0, 0.0)
    place = lax.broadcasted_iota(jnp.int32, (8, 2 * LANES), 0)
    found = jnp.zeros((8, 2 * LANES), F32)
    near = (fluid, roll(fluid, NZ), roll(fluid, -NZ), lower_z(fluid), upper_z(fluid))
    for index, value in enumerate(near):
        found = jnp.where(place == index, value, found)
    masks[...] = jnp.where(half == 0, found[:, :LANES], found[:, LANES:])


def faces_kernel(flags, own, received, masks, sibling, neighbour):
    same = flags[0] == flags[1]
    row = lax.broadcasted_iota(jnp.int32, (16, LANES), 0)
    fluid = jnp.where(row == 0, jnp.broadcast_to(masks[0:1, :], (16, LANES)), 0.0).astype(BF16)
    mine, theirs = own[...], received[:PAD].astype(F32)
    sibling[:PAD] = jnp.where(same, theirs, mine).astype(BF16)
    neighbour[:PAD] = jnp.where(same, mine, theirs).astype(BF16)
    sibling[PAD:] = fluid
    neighbour[PAD:] = fluid


def half_stream(flags, a, b, sibling, neighbour, edge_a, edge_b, masks, factors, emit):
    even = flags[1] == 1
    wide = [jnp.broadcast_to(masks[i : i + 1], (CHUNK, LANES)) for i in range(7)]
    fluid, open_y, open_z, open_x = wide[0], wide[1:3], wide[3:5], wide[5:7]
    lane = lanes_of(CHUNK)
    z_place = lane & (NZ - 1)
    below_z = jnp.where(z_place == 0, lane + NZ - 1, lane - 1)
    above_z = jnp.where(z_place == NZ - 1, lane + 1 - NZ, lane + 1)
    below_y, above_y = (lane + LANES - NZ) & (LANES - 1), (lane + NZ) & (LANES - 1)
    first_y, last_y = lane < NZ, lane >= LANES - NZ

    def one(values, mirror, layer, edge, chunk, up_y, up_z, sizes, open_here):
        lane_y = jnp.where(up_y, below_y, above_y)
        lane_z = jnp.where(up_z, below_z, above_z)
        at_edge = jnp.where(up_y, lane, lane + NZ)
        put = picked(edge, (at_edge + NZ * chunk) & (LANES - 1))
        outside = (up_y & first_y) | (~up_y & last_y)
        near_y = jnp.where(outside, put, picked(values, lane_y))
        near_z = picked(values, lane_z)
        upwind_x = jnp.where(open_here > 0, layer, mirror)
        upwind_y = jnp.where(jnp.where(up_y, *open_y) > 0, near_y, mirror)
        upwind_z = jnp.where(jnp.where(up_z, *open_z) > 0, near_z, mirror)
        outflow = sizes[0] * (values - upwind_x)
        outflow += sizes[1] * (values - upwind_y)
        outflow += sizes[2] * (values - upwind_z)
        return (values - outflow) * fluid

    for part in range(PAD // PART):
        span = slice(PART * part, PART * (part + 1))
        part_a, part_b = a(span), b(span)
        near, far = sibling[span].astype(F32), neighbour[span].astype(F32)
        above, below = jnp.where(even, near, far), jnp.where(even, far, near)
        results = []
        for index in range(2):
            chunk = 2 * part + index
            rows = slice(CHUNK * index, CHUNK * (index + 1))
            x, y, z = (factors[i, CHUNK * chunk : CHUNK * (chunk + 1)] for i in range(3))
            sizes = x, jnp.abs(y), jnp.abs(z)
            here_a, here_b = part_a[rows], part_b[rows]
            results.append(
                (
                    one(here_a, here_b, above[rows], edge_a, chunk, y > 0, z > 0, sizes, open_x[1]),
                    one(here_b, here_a, below[rows], edge_b, chunk, y < 0, z < 0, sizes, open_x[0]),
                    y,
                )
            )
        emit(part, results)


def joined(results, index):
    return jnp.concatenate([result[index] for result in results], axis=0)


def first_kernel(
    flags, own, own_edge, received, sibling, neighbour, masks_in, factors, lowered, masks_out
):
    low, even = flags[0] == 1, flags[1] == 1
    near, far = sibling[PAD:].astype(F32)[:1], neighbour[PAD:].astype(F32)[:1]
    place = lax.broadcasted_iota(jnp.int32, (8, LANES), 0)
    masks = masks_in[...]
    masks = jnp.where(place == 5, jnp.where(even, far, near), masks)
    masks = jnp.where(place == 6, jnp.where(even, near, far), masks)
    masks_out[...] = masks
    edge_own, edge_other = own_edge[...], received[PAD:].astype(F32)[:CHUNK]

    def emit(part, results):
        span = PART * part
        lowered[span : span + PART] = joined(results, 0).astype(BF16)
        lowered[PAD + span : PAD + span + PART] = joined(results, 1).astype(BF16)

    half_stream(
        flags,
        lambda span: jnp.where(low, own[span], received[span].astype(F32)),
        lambda span: jnp.where(low, received[span].astype(F32), own[span]),
        sibling,
        neighbour,
        jnp.where(low, edge_own, edge_other),
        jnp.where(low, edge_other, edge_own),
        masks,
        factors,
        emit,
    )


class Sender:
    def __init__(self, flags, a, b, sibling, neighbour, edges):
        self.even = flags[1] == 1
        self.refs = a, b, sibling, neighbour
        self.edges = edges
        self.packed = [jnp.zeros((CHUNK, LANES), F32)] * 2

    def __call__(self, part, results):
        span = slice(PART * part, PART * (part + 1))
        a, b, sibling, neighbour = self.refs
        rows_a, rows_b = joined(results, 0), joined(results, 1)
        a[span], b[span] = rows_a, rows_b
        sibling[span] = jnp.where(self.even, rows_b, rows_a).astype(BF16)
        neighbour[span] = jnp.where(self.even, rows_a, rows_b).astype(BF16)
        lane = lanes_of(CHUNK)
        for index, (chunk_a, chunk_b, y) in enumerate(results):
            chunk = 2 * part + index
            self.packed[0] = pack_edge(self.packed[0], chunk_a, y > 0, chunk, lane)
            self.packed[1] = pack_edge(self.packed[1], chunk_b, y < 0, chunk, lane)
        if part == PAD // PART - 1:
            self.edges[:EDGE] = edge_block(self.packed[0])
            self.edges[EDGE:] = edge_block(self.packed[1])


def received_edges(edges):
    values = edges[...].astype(F32)
    return values[:CHUNK], values[EDGE : EDGE + CHUNK]


def between_kernel(flags, a, b, sibling, neighbour, edges, masks, factors, *outs):
    emit = Sender(flags, *outs)
    half_stream(
        flags, lambda s: a[s], lambda s: b[s], sibling, neighbour, *received_edges(edges), masks[...],
        factors, emit,
    )


def lower_kernel(flags, a, b, sibling, neighbour, edges, masks, factors, lowered):
    def emit(part, results):
        span = PART * part
        lowered[span : span + PART] = joined(results, 0).astype(BF16)
        lowered[PAD + span : PAD + span + PART] = joined(results, 1).astype(BF16)

    half_stream(
        flags, lambda s: a[s], lambda s: b[s], sibling, neighbour, *received_edges(edges), masks[...],
        factors, emit,
    )


def last_kernel(flags, a, b, sibling, neighbour, edges, masks, factors, kept, message):
    low = flags[0] == 1

    def emit(part, results):
        span = slice(PART * part, PART * (part + 1))
        rows_a, rows_b = joined(results, 0), joined(results, 1)
        kept[span] = jnp.where(low, rows_a, rows_b)
        message[span] = jnp.where(low, rows_b, rows_a).astype(BF16)

    half_stream(
        flags, lambda s: a[s], lambda s: b[s], sibling, neighbour, *received_edges(edges), masks[...],
        factors, emit,
    )


def collide_kernel(flags, matrix, lowered, other, rows_out):
    swapped = flags[2] == 1
    first = jnp.where(swapped, other[...], lowered[...])
    second = jnp.where(swapped, lowered[...], other[...])
    for part in range(PAD // PART):
        span = slice(PART * part, PART * (part + 1))
        total = jnp.dot(matrix[span, : 2 * PAD], first, preferred_element_type=F32)
        total += jnp.dot(matrix[span, 2 * PAD :], second, preferred_element_type=F32)
        rows_out[span] = total


def collide_send_kernel(flags, own, mine, theirs, lowered, other, factors, *outs):
    low = flags[0] == 1
    swapped = flags[2] != flags[4]
    first = jnp.where(swapped, other[...], lowered[...])
    second = jnp.where(swapped, lowered[...], other[...])
    emit = Sender(flags, *outs)
    for part in range(PAD // PART):
        span = slice(PART * part, PART * (part + 1))
        total = jnp.dot(mine[span], first, preferred_element_type=F32)
        total += jnp.dot(theirs[span], second, preferred_element_type=F32)
        own_rows = own[span]
        rows_a, rows_b = jnp.where(low, own_rows, total), jnp.where(low, total, own_rows)
        results = []
        for index in range(2):
            rows = slice(CHUNK * index, CHUNK * (index + 1))
            chunk = 2 * part + index
            y = factors[1, CHUNK * chunk : CHUNK * (chunk + 1)]
            results.append((rows_a[rows], rows_b[rows], y))
        emit(part, results)


def reorder_kernel(flags, kept, ordered):
    ordered[...] = reordered(order_matrix(flags[0] == 1), kept[...])


def finish_kernel(flags, kept, received, evolved):
    order = order_matrix(flags[0] == 1)
    rest = jnp.dot(order, received[...], preferred_element_type=F32)
    mine = kept[...]
    half = flags[3]
    evolved[:, :LANES] = jnp.where(half == 0, mine, rest)[:ROWS]
    evolved[:, LANES:] = jnp.where(half == 0, rest, mine)[:ROWS]


def place(rows, columns, wanted):
    return (lax.broadcasted_iota(jnp.int32, (rows, columns), 0) == wanted[None, :]).astype(BF16)


def chosen(left, right):
    return jnp.dot(left, right, preferred_element_type=BF16)


def column_half(wide, block):
    column = lax.iota(jnp.int32, PAD)
    inside = column < ROWS
    start_a, start_b = 640 * block, jnp.where(block == 1, 1280, 2048)
    part_a = lax.dynamic_slice(wide, (0, start_a), (wide.shape[0], 768))
    part_b = lax.dynamic_slice(wide, (0, start_b), (wide.shape[0], 896))
    wanted_a = jnp.where(inside, ROWS * block + column - start_a, -1)
    wanted_b = jnp.where(inside, 4 * ROWS - 1 - ROWS * block - column - start_b, -1)
    halves = chosen(part_a, place(768, PAD, wanted_a)), chosen(part_b, place(896, PAD, wanted_b))
    return jnp.concatenate(halves, axis=1)


def padded_columns(matrix):
    return jnp.pad(matrix, ((0, 0), (0, 2944 - matrix.shape[1])))


def per_device(populations, solid_mask, collision):
    cell, vel = lax.axis_index("cells"), lax.axis_index("vel")
    low = (vel < 2).astype(jnp.int32)
    core, z = cell % 2, cell // 2 % 8
    block = jnp.minimum(vel, 3 - vel)
    half = (1 - low) ^ (cell // RING % 2)
    flags = jnp.stack([low, 1 - core, block, half, core]).astype(jnp.int32)

    row = CHUNK * z + lax.iota(jnp.int32, CHUNK)
    start = jnp.clip(jnp.where(low == 1, CHUNK * z, ROWS - CHUNK - CHUNK * z), 0, ROWS - CHUNK)
    wanted = jnp.where(row < ROWS, jnp.where(low == 1, row, ROWS - 1 - row) - start, -1)
    window = lax.dynamic_slice(collision, (start, 0), (CHUNK, collision.shape[1]))
    window = padded_columns(chosen(place(CHUNK, CHUNK, wanted).T, window))
    piece = column_half(window, core)
    populations, piece = lax.optimization_barrier((populations, piece))
    piece = to_mirror(piece)
    rings = [
        [(line * 8 + step) * 2 + side for step in range(8)] for line in range(8) for side in range(2)
    ]
    mine = lax.all_gather(piece, "cells", axis=0, tiled=True, axis_index_groups=rings)

    padded = jnp.pad(populations[:, 0, :], ((0, PAD - ROWS), (0, 0)))
    own, own_edge, message, masks, factors = call(
        prepare_kernel,
        [((PAD, LANES), F32), ((CHUNK, LANES), F32), ((PAD + EDGE, LANES), BF16), ((8, LANES), F32),
         ((3, PAD, LANES), F32)],
        flags, padded, solid_mask, flops=2 * 3 * PAD * PAD * 256,
    )
    received = to_mirror(message)
    faces = [((PAD + 16, LANES), BF16)] * 2
    sibling, neighbour = call(faces_kernel, faces, flags, own, received, masks)
    neighbour, sibling = to_neighbour(neighbour), to_sibling(sibling)

    row = lax.iota(jnp.int32, PAD)
    wanted = jnp.where(row < ROWS, jnp.where(low == 1, row, ROWS - 1 - row), -1)
    received, collision = lax.optimization_barrier((received, collision))
    ordered = padded_columns(chosen(place(ROWS, PAD, wanted).T, collision))

    lowered, masks = call(
        first_kernel,
        [((2 * PAD, LANES), BF16), ((8, LANES), F32)],
        flags, own, own_edge, received, sibling, neighbour, masks, factors, flops=100 * PAD * 256,
    )
    lowered, ordered = lax.optimization_barrier((lowered, ordered))
    matrix = jnp.concatenate([column_half(ordered, 0), column_half(ordered, 1)], axis=1)
    sends = [((PAD, LANES), F32)] * 2 + [((PAD, LANES), BF16)] * 2 + [((2 * EDGE, LANES), BF16)]
    multiply = 2 * PAD * 4 * PAD * LANES
    for step in range(STEPS):
        other = to_side(lowered)
        (own,) = call(
            collide_kernel, [((PAD, LANES), F32)], flags, matrix, lowered, other, flops=multiply
        )
        if step == 0:
            mine, own = lax.optimization_barrier((mine, own))
            theirs = to_sibling(mine)
        a, b, sibling, neighbour, edges = call(
            collide_send_kernel, sends, flags, own, mine, theirs, lowered, other, factors, flops=multiply
        )
        near = to_neighbour(neighbour), to_mirror(edges), to_sibling(sibling)
        if step == STEPS - 1:
            break
        a, b, sibling, neighbour, edges = call(
            between_kernel, sends, flags, a, b, near[2], near[0], near[1], masks, factors, flops=100 * PAD * 256
        )
        near = to_neighbour(neighbour), to_mirror(edges), to_sibling(sibling)
        (lowered,) = call(
            lower_kernel, [((2 * PAD, LANES), BF16)],
            flags, a, b, near[2], near[0], near[1], masks, factors, flops=100 * PAD * 256,
        )
    kept, message = call(
        last_kernel, [((PAD, LANES), F32), ((PAD, LANES), BF16)],
        flags, a, b, near[2], near[0], near[1], masks, factors, flops=100 * PAD * 256,
    )
    received = to_mirror(message)
    (kept,) = call(
        reorder_kernel, [((PAD, LANES), F32)], flags, kept, flops=2 * 3 * PAD * PAD * LANES
    )
    (evolved,) = call(
        finish_kernel, [((ROWS, 2 * LANES), F32)], flags, kept, received, flops=2 * PAD * PAD * LANES
    )
    return evolved[:, None, :]


def solution(mesh):
    in_specs = (P("vel", "cells", None), P("cells", None), P("vel", None))
    out_specs = P("vel", "cells", None)
    return jax.shard_map(
        per_device, mesh=mesh, in_specs=in_specs, out_specs=out_specs, check_vma=False
    )
```

```python
import math

import jax
import jax.numpy as jnp
from jax import lax
from jax.experimental import pallas as pl
from jax.experimental.pallas import tpu as pltpu
from jax.sharding import PartitionSpec as P


K = 14
STEPS = 2
NZ = 16
BOTH = ("cells", "vel")
ROWS = 686
PAD = 704
CHUNK = 88
PART = 2 * CHUNK
EDGE = 96
LANES = 128
RING = 16
F32 = jnp.float32
BF16 = jnp.bfloat16
PARAMS = pltpu.CompilerParams(vmem_limit_bytes=40 * 1024 * 1024)


def pairs_of(target):
    pairs = []
    for cell in range(128):
        for part in range(4):
            to_cell, to_part = target(cell, part)
            pairs.append((cell * 4 + part, to_cell * 4 + to_part))
    return pairs


def to_sibling(array):
    return lax.ppermute(array, BOTH, pairs_of(lambda cell, part: (cell ^ 1, part)))


def neighbour_of(cell, part):
    other = (cell - 1 if cell % 2 == 0 else cell + 1) % 128
    return other, part if (other // RING) % 2 == (cell // RING) % 2 else 3 - part


def to_neighbour(array):
    return lax.ppermute(array, BOTH, pairs_of(neighbour_of))


def with_neighbour(array):
    pairs = pairs_of(neighbour_of)
    groups = [list(pair) for pair in pairs if pair[0] // 4 % 2 == 1]
    return lax.all_gather(array, BOTH, axis=0, tiled=True, axis_index_groups=groups)


def to_mirror(array):
    return lax.ppermute(array, "vel", [(i, 3 - i) for i in range(4)])


def to_side(array):
    return lax.ppermute(array, "vel", [(i, i ^ 1) for i in range(4)])


def call(kernel, outs, flags, *arrays, flops=0, scratch=()):
    moved = sum(x.size * x.dtype.itemsize for x in arrays)
    moved += sum(math.prod(shape) * jnp.dtype(dtype).itemsize for shape, dtype in outs)
    vmem = pl.BlockSpec(memory_space=pltpu.VMEM)
    result = pl.pallas_call(
        kernel,
        out_shape=[jax.ShapeDtypeStruct(shape, dtype) for shape, dtype in outs],
        in_specs=[pl.BlockSpec(memory_space=pltpu.SMEM)] + [vmem] * len(arrays),
        out_specs=[vmem] * len(outs),
        scratch_shapes=[pltpu.VMEM(shape, dtype) for shape, dtype in scratch],
        compiler_params=PARAMS,
        cost_estimate=pl.CostEstimate(flops=flops, bytes_accessed=moved, transcendentals=0),
    )(flags, *arrays)
    return result


def roll(values, shift):
    return pltpu.roll(values, shift % values.shape[1], 1)


def order_matrix(low):
    row = lax.broadcasted_iota(jnp.int32, (PAD, PAD), 0)
    column = lax.broadcasted_iota(jnp.int32, (PAD, PAD), 1)
    wanted = jnp.where(low, row, ROWS - 1 - row)
    return jnp.where((column == wanted) & (row < ROWS), 1.0, 0.0).astype(BF16)


def reordered(order, values):
    total = jnp.zeros(values.shape, F32)
    for _ in range(3):
        part = values.astype(BF16)
        total += jnp.dot(order, part, preferred_element_type=F32)
        values = values - part.astype(F32)
    return total


def signed_factors(block, chunk):
    row = CHUNK * chunk + lax.broadcasted_iota(jnp.int32, (CHUNK, LANES), 0)
    ids = ROWS * block + row
    upper = (ids * 4682) >> 16
    k_z = ids - K * upper
    k_x = (upper * 4682) >> 16
    k_y = upper - K * k_x
    centre = (K - 1) / 2.0
    x, y, z = ((k.astype(F32) - centre) * (0.3 / centre) for k in (k_x, k_y, k_z))
    return jnp.abs(x), y, z


def lanes_of(rows):
    return lax.broadcasted_iota(jnp.int32, (rows, LANES), 1)


def lower_z(values):
    z_place = lax.broadcasted_iota(jnp.int32, values.shape, 1) % NZ
    return jnp.where(z_place == 0, roll(values, 1 - NZ), roll(values, 1))


def upper_z(values):
    z_place = lax.broadcasted_iota(jnp.int32, values.shape, 1) % NZ
    return jnp.where(z_place == NZ - 1, roll(values, NZ - 1), roll(values, -1))


def picked(values, lanes):
    return jnp.take_along_axis(values, lanes, axis=1, mode="promise_in_bounds")


def pack_edge(packed, values, positive, chunk, lane):
    place = lane & (NZ - 1)
    edge = picked(values, jnp.where(positive, place + LANES - NZ, place))
    return jnp.where((lane >> 4) == chunk, edge, packed)


def edge_block(packed):
    return jnp.concatenate([packed, jnp.zeros((EDGE - CHUNK, LANES), F32)], axis=0).astype(BF16)


def prepare_kernel(flags, populations, solid, own, own_edge, message, masks, factors):
    low, block, half = flags[0] == 1, flags[2], flags[3]
    ordered = reordered(order_matrix(low), populations[...])
    left, right = ordered[:, :LANES], ordered[:, LANES:]
    mine = jnp.where(half == 0, left, right)
    rest = jnp.where(half == 0, right, left)
    own[...] = mine
    edges = jnp.zeros((CHUNK, LANES), F32)
    sent = jnp.zeros((CHUNK, LANES), F32)
    lane = lanes_of(CHUNK)
    for chunk in range(PAD // CHUNK):
        rows = slice(CHUNK * chunk, CHUNK * (chunk + 1))
        x, y, z = signed_factors(block, chunk)
        factors[0, rows], factors[1, rows], factors[2, rows] = x, y, z
        positive = jnp.where(low, y, -y) > 0
        edges = pack_edge(edges, rest[rows], positive, chunk, lane)
        sent = pack_edge(sent, mine[rows], positive, chunk, lane)
    own_edge[...] = edges
    message[:PAD] = rest.astype(BF16)
    message[PAD:] = edge_block(sent)
    fluid = jnp.where(jnp.broadcast_to(solid[...], (8, 2 * LANES)) == 0, 1.0, 0.0)
    place = lax.broadcasted_iota(jnp.int32, (8, 2 * LANES), 0)
    found = jnp.zeros((8, 2 * LANES), F32)
    near = (fluid, roll(fluid, NZ), roll(fluid, -NZ), lower_z(fluid), upper_z(fluid))
    for index, value in enumerate(near):
        found = jnp.where(place == index, value, found)
    masks[...] = jnp.where(half == 0, found[:, :LANES], found[:, LANES:])


def faces_kernel(flags, own, received, masks, sibling, neighbour):
    same = flags[4] == 1
    row = lax.broadcasted_iota(jnp.int32, (16, LANES), 0)
    fluid = jnp.where(row == 0, jnp.broadcast_to(masks[0:1, :], (16, LANES)), 0.0).astype(BF16)
    mine, theirs = own[...], received[:PAD].astype(F32)
    sibling[:PAD] = jnp.where(same, theirs, mine).astype(BF16)
    neighbour[:PAD] = jnp.where(same, mine, theirs).astype(BF16)
    sibling[PAD:] = fluid
    neighbour[PAD:] = fluid


def rows_of(index, size):
    return slice(size * index, size * (index + 1))


def stream_part(part, sign, values, mirror, layer, edge, masks, open_x, factors):
    fluid, below_open_y, above_open_y, below_open_z, above_open_z = (
        jnp.broadcast_to(masks[i : i + 1], (CHUNK, LANES)) for i in range(5)
    )
    open_x = jnp.broadcast_to(open_x, (CHUNK, LANES))
    lane = lanes_of(CHUNK)
    z_place = lane & (NZ - 1)
    below_z = jnp.where(z_place == 0, lane + NZ - 1, lane - 1)
    above_z = jnp.where(z_place == NZ - 1, lane + 1 - NZ, lane + 1)
    below_y, above_y = (lane + LANES - NZ) & (LANES - 1), (lane + NZ) & (LANES - 1)
    results = []
    for index in range(2):
        chunk = 2 * part + index
        x, y, z = (factors[i, rows_of(chunk, CHUNK)] for i in range(3))
        up_y, up_z = y * sign > 0, z * sign > 0
        here, back = values[rows_of(index, CHUNK)], mirror[rows_of(index, CHUNK)]
        at_edge = jnp.where(up_y, lane, lane + NZ)
        put = picked(edge, (at_edge + NZ * chunk) & (LANES - 1))
        outside = (up_y & (lane < NZ)) | (~up_y & (lane >= LANES - NZ))
        near_y = jnp.where(outside, put, picked(here, jnp.where(up_y, below_y, above_y)))
        near_z = picked(here, jnp.where(up_z, below_z, above_z))
        upwind_x = jnp.where(open_x > 0, layer[rows_of(index, CHUNK)], back)
        upwind_y = jnp.where(jnp.where(up_y, below_open_y, above_open_y) > 0, near_y, back)
        upwind_z = jnp.where(jnp.where(up_z, below_open_z, above_open_z) > 0, near_z, back)
        outflow = x * (here - upwind_x)
        outflow += jnp.abs(y) * (here - upwind_y)
        outflow += jnp.abs(z) * (here - upwind_z)
        results.append((here - outflow) * fluid)
    return jnp.concatenate(results, axis=0)


def pack_part(packed, part, sign, values, factors):
    lane = lanes_of(CHUNK)
    for index in range(2):
        chunk = 2 * part + index
        positive = factors[1, rows_of(chunk, CHUNK)] * sign > 0
        packed = pack_edge(packed, values[rows_of(index, CHUNK)], positive, chunk, lane)
    return packed


def signs(flags):
    near = jnp.where(flags[1] == 1, 1.0, -1.0)
    return near, -near


def place_of_near(flags):
    return pl.multiple_of(PAD * (1 - flags[1]), 16), pl.multiple_of(PAD * flags[1], 16)


def first_kernel(
    flags, own, own_edge, received, sibling, neighbour, masks_in, factors, lowered, masks_out
):
    same = flags[4] == 1
    place = lax.broadcasted_iota(jnp.int32, (8, LANES), 0)
    open_near = sibling[PAD:].astype(F32)[:1]
    open_far = neighbour[PAD:].astype(F32)[:1]
    masks = masks_in[...]
    masks = jnp.where(place == 5, open_near, masks)
    masks = jnp.where(place == 6, open_far, masks)
    masks_out[...] = masks
    edge_own, edge_other = own_edge[...], received[PAD:].astype(F32)[:CHUNK]
    edge_near = jnp.where(same, edge_own, edge_other)
    edge_far = jnp.where(same, edge_other, edge_own)
    sign_near, sign_far = signs(flags)
    at_near, at_far = place_of_near(flags)
    for part in range(PAD // PART):
        span = rows_of(part, PART)
        mine, theirs = own[span], received[span].astype(F32)
        near, far = jnp.where(same, mine, theirs), jnp.where(same, theirs, mine)
        new_near = stream_part(
            part, sign_near, near, far, sibling[span].astype(F32), edge_near, masks, open_near, factors
        )
        new_far = stream_part(
            part, sign_far, far, near, neighbour[span].astype(F32), edge_far, masks, open_far, factors
        )
        lowered[pl.ds(at_near + PART * part, PART)] = new_near.astype(BF16)
        lowered[pl.ds(at_far + PART * part, PART)] = new_far.astype(BF16)


def stream_near(flags, near, far, sibling, edges, masks, factors):
    values = masks[...]
    edge = edges[:EDGE].astype(F32)[:CHUNK]
    for part in range(PAD // PART):
        span = rows_of(part, PART)
        yield part, span, stream_part(
            part, signs(flags)[0], near[span], far[span], sibling[span].astype(F32), edge, values,
            values[5:6], factors,
        )


def stream_far(flags, near, far, neighbour, edges, masks, factors):
    values = masks[...]
    edge = edges[EDGE:].astype(F32)[:CHUNK]
    start = pl.multiple_of(PAD * (1 - flags[1]), 16)
    for part in range(PAD // PART):
        span = rows_of(part, PART)
        layer = neighbour[pl.ds(start + PART * part, PART)].astype(F32)
        yield part, span, stream_part(
            part, signs(flags)[1], far[span], near[span], layer, edge, values, values[6:7], factors
        )


def between_near_kernel(flags, near, far, sibling, edges, masks, factors, rows_out, sent, packed_out):
    packed = jnp.zeros((CHUNK, LANES), F32)
    for part, span, rows in stream_near(flags, near, far, sibling, edges, masks, factors):
        rows_out[span] = rows
        sent[span] = rows.astype(BF16)
        packed = pack_part(packed, part, signs(flags)[0], rows, factors)
    packed_out[...] = edge_block(packed)


def between_far_kernel(
    flags, near, far, neighbour, edges, masks, factors, packed_near, rows_out, sent, packed_out
):
    packed = jnp.zeros((CHUNK, LANES), F32)
    for part, span, rows in stream_far(flags, near, far, neighbour, edges, masks, factors):
        rows_out[span] = rows
        sent[span] = rows.astype(BF16)
        packed = pack_part(packed, part, signs(flags)[1], rows, factors)
    packed_out[:EDGE] = packed_near[...]
    packed_out[EDGE:] = edge_block(packed)


def lower_near_kernel(flags, near, far, sibling, edges, masks, factors, lowered):
    for _, span, rows in stream_near(flags, near, far, sibling, edges, masks, factors):
        lowered[span] = rows.astype(BF16)


def lower_far_kernel(flags, near, far, neighbour, edges, masks, factors, low_near, lowered):
    at_near, at_far = place_of_near(flags)
    for part, span, rows in stream_far(flags, near, far, neighbour, edges, masks, factors):
        lowered[pl.ds(at_far + PART * part, PART)] = rows.astype(BF16)
        lowered[pl.ds(at_near + PART * part, PART)] = low_near[span]


def last_near_kernel(flags, near, far, sibling, edges, masks, factors, rows_out):
    for _, span, rows in stream_near(flags, near, far, sibling, edges, masks, factors):
        rows_out[span] = rows


def last_far_kernel(flags, near, far, neighbour, edges, masks, factors, new_near, kept, message):
    same = flags[4] == 1
    for _, span, rows in stream_far(flags, near, far, neighbour, edges, masks, factors):
        done = new_near[span]
        kept[span] = jnp.where(same, done, rows)
        message[span] = jnp.where(same, rows, done).astype(BF16)


def dot(left, right):
    return jnp.dot(left, right, preferred_element_type=F32)


def own_product(parts, half, values, span):
    return dot(parts[2 * half][span], values[:PAD]) + dot(parts[2 * half + 1][span], values[PAD:])


def collide_kernel(flags, m0, m1, m2, m3, lowered, other, rows_out):
    swapped = flags[2] == 1
    first = jnp.where(swapped, other[...], lowered[...])
    second = jnp.where(swapped, lowered[...], other[...])
    for part in range(PAD // PART):
        span = rows_of(part, PART)
        parts = m0, m1, m2, m3
        rows_out[span] = own_product(parts, 0, first, span) + own_product(parts, 1, second, span)


def give_rows(flags, part, own, partner, factors, packed, outs):
    near, far, to_other_core, to_neighbour_chip = outs
    same = flags[4] == 1
    span = rows_of(part, PART)
    rows_near, rows_far = jnp.where(same, own, partner), jnp.where(same, partner, own)
    near[span], far[span] = rows_near, rows_far
    to_neighbour_chip[span] = rows_near.astype(BF16)
    to_other_core[span] = rows_far.astype(BF16)
    sign_near, sign_far = signs(flags)
    return (
        pack_part(packed[0], part, sign_near, rows_near, factors),
        pack_part(packed[1], part, sign_far, rows_far, factors),
    )


def collide_partner_kernel(flags, own, matrix, lowered, other, factors, *outs):
    swapped = flags[2] == 1
    first = jnp.where(swapped, other[...], lowered[...])
    second = jnp.where(swapped, lowered[...], other[...])
    packed = (jnp.zeros((CHUNK, LANES), F32),) * 2
    for part in range(PAD // PART):
        span = rows_of(part, PART)
        partner = dot(matrix[span], first) + dot(matrix[PAD + PART * part : PAD + PART * (part + 1)], second)
        packed = give_rows(flags, part, own[span], partner, factors, packed, outs[:4])
    outs[4][:EDGE], outs[4][EDGE:] = edge_block(packed[0]), edge_block(packed[1])


def early_kernel(flags, m0, m1, m2, m3, matrix, lowered, own_out, partner_out):
    values = lowered[...]
    for half in range(2):

        @pl.when(flags[2] == half)
        def _():
            for part in range(PAD // PART):
                span = rows_of(part, PART)
                start = PAD * half + PART * part
                own_out[span] = own_product((m0, m1, m2, m3), half, values, span)
                partner_out[span] = dot(matrix[start : start + PART], values)


def late_kernel(flags, m0, m1, m2, m3, matrix, other, own, partner, factors, *outs):
    *outs, total_own, total_partner = outs
    values = other[...]
    for half in range(2):

        @pl.when(flags[2] != half)
        def _():
            for part in range(PAD // PART):
                span = rows_of(part, PART)
                start = PAD * half + PART * part
                total_own[span] = own[span] + own_product((m0, m1, m2, m3), half, values, span)
                total_partner[span] = partner[span] + dot(matrix[start : start + PART], values)

    packed = (jnp.zeros((CHUNK, LANES), F32),) * 2
    for part in range(PAD // PART):
        span = rows_of(part, PART)
        packed = give_rows(flags, part, total_own[span], total_partner[span], factors, packed, outs[:4])
    outs[4][:EDGE], outs[4][EDGE:] = edge_block(packed[0]), edge_block(packed[1])


def reorder_kernel(flags, kept, ordered):
    ordered[...] = reordered(order_matrix(flags[0] == 1), kept[...])


def finish_kernel(flags, kept, received, evolved):
    order = order_matrix(flags[0] == 1)
    rest = jnp.dot(order, received[...], preferred_element_type=F32)
    mine = kept[...]
    half = flags[3]
    evolved[:, :LANES] = jnp.where(half == 0, mine, rest)[:ROWS]
    evolved[:, LANES:] = jnp.where(half == 0, rest, mine)[:ROWS]


def place(rows, columns, wanted):
    return (lax.broadcasted_iota(jnp.int32, (rows, columns), 0) == wanted[None, :]).astype(BF16)


def chosen(left, right):
    return jnp.dot(left, right, preferred_element_type=BF16)


def column_half(wide, block):
    column = lax.iota(jnp.int32, PAD)
    inside = column < ROWS
    start_a, start_b = 640 * block, jnp.where(block == 1, 1280, 2048)
    part_a = lax.dynamic_slice(wide, (0, start_a), (wide.shape[0], 768))
    part_b = lax.dynamic_slice(wide, (0, start_b), (wide.shape[0], 896))
    wanted_a = jnp.where(inside, ROWS * block + column - start_a, -1)
    wanted_b = jnp.where(inside, 4 * ROWS - 1 - ROWS * block - column - start_b, -1)
    halves = chosen(part_a, place(768, PAD, wanted_a)), chosen(part_b, place(896, PAD, wanted_b))
    return halves


def padded_columns(matrix):
    return jnp.pad(matrix, ((0, 0), (0, 2944 - matrix.shape[1])))


def per_device(populations, solid_mask, collision):
    cell, vel = lax.axis_index("cells"), lax.axis_index("vel")
    low = (vel < 2).astype(jnp.int32)
    core, z = cell % 2, cell // 2 % 8
    block = jnp.minimum(vel, 3 - vel)
    half = (1 - low) ^ (cell // RING % 2)
    flags = jnp.stack([low, 1 - core, block, half, (low != core).astype(jnp.int32)])
    flags = flags.astype(jnp.int32)

    row = CHUNK * z + lax.iota(jnp.int32, CHUNK)
    start = jnp.clip(jnp.where(low == 1, CHUNK * z, ROWS - CHUNK - CHUNK * z), 0, ROWS - CHUNK)
    wanted = jnp.where(row < ROWS, jnp.where(low == 1, row, ROWS - 1 - row) - start, -1)
    window = lax.dynamic_slice(collision, (start, 0), (CHUNK, collision.shape[1]))
    window = padded_columns(chosen(place(CHUNK, CHUNK, wanted).T, window))
    piece = jnp.concatenate(column_half(window, core), axis=1)
    populations, piece = lax.optimization_barrier((populations, piece))
    piece = to_mirror(piece)

    padded = jnp.pad(populations[:, 0, :], ((0, PAD - ROWS), (0, 0)))
    rows = (PAD, LANES)
    own, own_edge, message, masks, factors = call(
        prepare_kernel,
        [(rows, F32), ((CHUNK, LANES), F32), ((PAD + EDGE, LANES), BF16), ((8, LANES), F32), ((3, *rows), F32)],
        flags, padded, solid_mask, flops=2 * 3 * PAD * PAD * 256,
    )
    piece, _ = lax.optimization_barrier((piece, message))
    groups = [
        [(line * 8 + step) * 2 + side for side in range(2) for step in range(8)] for line in range(8)
    ]
    partner_matrix = lax.all_gather(piece, "cells", axis=0, tiled=True, axis_index_groups=groups)
    received = to_mirror(message)
    faces = [((PAD + 16, LANES), BF16)] * 2
    sibling, neighbour = call(faces_kernel, faces, flags, own, received, masks)
    neighbour, sibling = to_neighbour(neighbour), to_sibling(sibling)

    row = lax.iota(jnp.int32, PAD)
    wanted = jnp.where(row < ROWS, jnp.where(low == 1, row, ROWS - 1 - row), -1)
    received, collision = lax.optimization_barrier((received, collision))
    ordered = padded_columns(chosen(place(ROWS, PAD, wanted).T, collision))

    lowered, masks = call(
        first_kernel,
        [((2 * PAD, LANES), BF16), ((8, LANES), F32)],
        flags, own, own_edge, received, sibling, neighbour, masks, factors, flops=100 * PAD * 256,
    )
    lowered, ordered = lax.optimization_barrier((lowered, ordered))
    matrix = *column_half(ordered, 0), *column_half(ordered, 1)
    edges_shape = ((2 * EDGE, LANES), BF16)
    sends = [(rows, F32)] * 2 + [(rows, BF16)] * 2 + [edges_shape]
    multiply = 2 * PAD * 4 * PAD * LANES
    work = 60 * PAD * LANES

    other = to_side(lowered)
    (own,) = call(collide_kernel, [(rows, F32)], flags, *matrix, lowered, other, flops=multiply)
    partner_matrix, own = lax.optimization_barrier((partner_matrix, own))
    near, far, for_sibling, for_neighbour, edges = call(
        collide_partner_kernel, sends, flags, own, partner_matrix, lowered, other, factors, flops=multiply
    )

    for step in range(1, STEPS):
        neighbour = with_neighbour(for_neighbour)
        sibling, edges = to_sibling(for_sibling), to_mirror(edges)
        new_near, for_neighbour, packed = call(
            between_near_kernel, [(rows, F32), (rows, BF16), ((EDGE, LANES), BF16)],
            flags, near, far, sibling, edges, masks, factors, flops=work,
        )
        new_far, for_sibling, new_edges = call(
            between_far_kernel, [(rows, F32), (rows, BF16), edges_shape],
            flags, near, far, neighbour, edges, masks, factors, packed, flops=work,
        )
        near, far, edges = new_near, new_far, new_edges
        neighbour = with_neighbour(for_neighbour)
        sibling, edges = to_sibling(for_sibling), to_mirror(edges)
        (low_near,) = call(
            lower_near_kernel, [(rows, BF16)], flags, near, far, sibling, edges, masks, factors, flops=work
        )
        (lowered,) = call(
            lower_far_kernel, [((2 * PAD, LANES), BF16)],
            flags, near, far, neighbour, edges, masks, factors, low_near, flops=work,
        )
        other = to_side(lowered)
        early = call(
            early_kernel, [(rows, F32)] * 2, flags, *matrix, partner_matrix, lowered, flops=multiply
        )
        near, far, for_sibling, for_neighbour, edges = call(
            late_kernel, sends, flags, *matrix, partner_matrix, other, *early, factors,
            flops=multiply, scratch=[(rows, F32)] * 2,
        )

    neighbour = with_neighbour(for_neighbour)
    sibling, edges = to_sibling(for_sibling), to_mirror(edges)
    (new_near,) = call(
        last_near_kernel, [(rows, F32)], flags, near, far, sibling, edges, masks, factors, flops=work
    )
    kept, message = call(
        last_far_kernel, [(rows, F32), (rows, BF16)],
        flags, near, far, neighbour, edges, masks, factors, new_near, flops=work,
    )
    received = to_mirror(message)
    (kept,) = call(reorder_kernel, [(rows, F32)], flags, kept, flops=2 * 3 * PAD * PAD * LANES)
    (evolved,) = call(
        finish_kernel, [((ROWS, 2 * LANES), F32)], flags, kept, received, flops=2 * PAD * PAD * LANES
    )
    return evolved[:, None, :]


def solution(mesh):
    in_specs = (P("vel", "cells", None), P("cells", None), P("vel", None))
    out_specs = P("vel", "cells", None)
    return jax.shard_map(
        per_device, mesh=mesh, in_specs=in_specs, out_specs=out_specs, check_vma=False
    )
```

```python
import math

import jax
import jax.numpy as jnp
from jax import lax
from jax.experimental import pallas as pl
from jax.experimental.pallas import tpu as pltpu
from jax.sharding import PartitionSpec as P


K = 14
STEPS = 2
NZ = 16
BOTH = ("cells", "vel")
ROWS = 686
PAD = 704
CHUNK = 88
PART = 2 * CHUNK
EDGE = 96
LANES = 128
RING = 16
F32 = jnp.float32
BF16 = jnp.bfloat16
PARAMS = pltpu.CompilerParams(vmem_limit_bytes=20 * 1024 * 1024)


def pairs_of(target):
    pairs = []
    for cell in range(128):
        for part in range(4):
            to_cell, to_part = target(cell, part)
            pairs.append((cell * 4 + part, to_cell * 4 + to_part))
    return pairs


def with_sibling(array):
    groups = [[cell, cell + 1] for cell in range(0, 128, 2)]
    return lax.all_gather(array, "cells", axis=0, tiled=True, axis_index_groups=groups)


def to_layer(array, turned):
    def target(cell, part):
        return (cell - 1 if part < 2 else cell + 1) % 128, 3 - part if turned else part

    return lax.ppermute(array, BOTH, pairs_of(target))


def neighbour_of(cell, part):
    other = (cell - 1 if cell % 2 == 0 else cell + 1) % 128
    return other, part if (other // RING) % 2 == (cell // RING) % 2 else 3 - part


def to_neighbour(array):
    return lax.ppermute(array, BOTH, pairs_of(neighbour_of))


def to_mirror(array):
    return lax.ppermute(array, "vel", [(i, 3 - i) for i in range(4)])


def to_side(array):
    return lax.ppermute(array, "vel", [(i, i ^ 1) for i in range(4)])


def call(kernel, outs, flags, *arrays, flops=0, scratch=()):
    moved = sum(x.size * x.dtype.itemsize for x in arrays)
    moved += sum(math.prod(shape) * jnp.dtype(dtype).itemsize for shape, dtype in outs)
    vmem = pl.BlockSpec(memory_space=pltpu.VMEM)
    result = pl.pallas_call(
        kernel,
        out_shape=[jax.ShapeDtypeStruct(shape, dtype) for shape, dtype in outs],
        in_specs=[pl.BlockSpec(memory_space=pltpu.SMEM)] + [vmem] * len(arrays),
        out_specs=[vmem] * len(outs),
        scratch_shapes=[pltpu.VMEM(shape, dtype) for shape, dtype in scratch],
        compiler_params=PARAMS,
        cost_estimate=pl.CostEstimate(flops=flops, bytes_accessed=moved, transcendentals=0),
    )(flags, *arrays)
    return result


def roll(values, shift):
    return pltpu.roll(values, shift % values.shape[1], 1)


def order_matrix(low):
    row = lax.broadcasted_iota(jnp.int32, (PAD, PAD), 0)
    column = lax.broadcasted_iota(jnp.int32, (PAD, PAD), 1)
    wanted = jnp.where(low, row, ROWS - 1 - row)
    return jnp.where((column == wanted) & (row < ROWS), 1.0, 0.0).astype(BF16)


def reordered(order, values):
    total = jnp.zeros(values.shape, F32)
    for _ in range(3):
        part = values.astype(BF16)
        total += jnp.dot(order, part, preferred_element_type=F32)
        values = values - part.astype(F32)
    return total


def signed_factors(block, chunk):
    row = CHUNK * chunk + lax.broadcasted_iota(jnp.int32, (CHUNK, LANES), 0)
    ids = ROWS * block + row
    upper = (ids * 4682) >> 16
    k_z = ids - K * upper
    k_x = (upper * 4682) >> 16
    k_y = upper - K * k_x
    centre = (K - 1) / 2.0
    x, y, z = ((k.astype(F32) - centre) * (0.3 / centre) for k in (k_x, k_y, k_z))
    return jnp.abs(x), y, z


def lanes_of(rows):
    return lax.broadcasted_iota(jnp.int32, (rows, LANES), 1)


def lower_z(values):
    z_place = lax.broadcasted_iota(jnp.int32, values.shape, 1) % NZ
    return jnp.where(z_place == 0, roll(values, 1 - NZ), roll(values, 1))


def upper_z(values):
    z_place = lax.broadcasted_iota(jnp.int32, values.shape, 1) % NZ
    return jnp.where(z_place == NZ - 1, roll(values, NZ - 1), roll(values, -1))


def picked(values, lanes):
    return jnp.take_along_axis(values, lanes, axis=1, mode="promise_in_bounds")


def pack_edge(packed, values, positive, chunk, lane):
    place = lane & (NZ - 1)
    edge = picked(values, jnp.where(positive, place + LANES - NZ, place))
    return jnp.where((lane >> 4) == chunk, edge, packed)


def edge_block(packed):
    return jnp.concatenate([packed, jnp.zeros((EDGE - CHUNK, LANES), F32)], axis=0).astype(BF16)


def prepare_kernel(
    flags, populations, solid, own, own_edge, message, straight, turned, masks, factors
):
    low, block, half = flags[0] == 1, flags[2], flags[3]
    ordered = reordered(order_matrix(low), populations[...])
    left, right = ordered[:, :LANES], ordered[:, LANES:]
    mine = jnp.where(half == 0, left, right)
    rest = jnp.where(half == 0, right, left)
    own[...] = mine
    edges = jnp.zeros((CHUNK, LANES), F32)
    sent = jnp.zeros((CHUNK, LANES), F32)
    lane = lanes_of(CHUNK)
    for chunk in range(PAD // CHUNK):
        rows = slice(CHUNK * chunk, CHUNK * (chunk + 1))
        x, y, z = signed_factors(block, chunk)
        factors[0, rows], factors[1, rows], factors[2, rows] = x, y, z
        positive = jnp.where(low, y, -y) > 0
        edges = pack_edge(edges, rest[rows], positive, chunk, lane)
        sent = pack_edge(sent, mine[rows], positive, chunk, lane)
    own_edge[...] = edges
    message[:PAD] = rest.astype(BF16)
    message[PAD:] = edge_block(sent)
    fluid = jnp.where(jnp.broadcast_to(solid[...], (8, 2 * LANES)) == 0, 1.0, 0.0)
    place = lax.broadcasted_iota(jnp.int32, (8, 2 * LANES), 0)
    found = jnp.zeros((8, 2 * LANES), F32)
    near = (fluid, roll(fluid, NZ), roll(fluid, -NZ), lower_z(fluid), upper_z(fluid))
    for index, value in enumerate(near):
        found = jnp.where(place == index, value, found)
    masks[...] = jnp.where(half == 0, found[:, :LANES], found[:, LANES:])
    row = lax.broadcasted_iota(jnp.int32, (16, LANES), 0)
    halves = []
    for side in range(2):
        cells = slice(LANES * side, LANES * (side + 1))
        open_cells = jnp.where(row == 0, jnp.broadcast_to(fluid[:1, cells], (16, LANES)), 0.0)
        halves.append((ordered[:, cells].astype(BF16), open_cells.astype(BF16)))
    for place, target in ((flags[5], straight), (1 - flags[5], turned)):
        for rows, low_value, high_value in zip((slice(0, PAD), slice(PAD, PAD + 16)), *halves):
            target[rows] = jnp.where(place == 0, low_value, high_value)


def rows_of(index, size):
    return slice(size * index, size * (index + 1))


def stream_part(part, sign, values, mirror, layer, edge, masks, open_x, factors):
    fluid, below_open_y, above_open_y, below_open_z, above_open_z = (
        jnp.broadcast_to(masks[i : i + 1], (CHUNK, LANES)) for i in range(5)
    )
    open_x = jnp.broadcast_to(open_x, (CHUNK, LANES))
    lane = lanes_of(CHUNK)
    z_place = lane & (NZ - 1)
    below_z = jnp.where(z_place == 0, lane + NZ - 1, lane - 1)
    above_z = jnp.where(z_place == NZ - 1, lane + 1 - NZ, lane + 1)
    below_y, above_y = (lane + LANES - NZ) & (LANES - 1), (lane + NZ) & (LANES - 1)
    results = []
    for index in range(2):
        chunk = 2 * part + index
        x, y, z = (factors[i, rows_of(chunk, CHUNK)] for i in range(3))
        up_y, up_z = y * sign > 0, z * sign > 0
        here, back = values[rows_of(index, CHUNK)], mirror[rows_of(index, CHUNK)]
        at_edge = jnp.where(up_y, lane, lane + NZ)
        put = picked(edge, (at_edge + NZ * chunk) & (LANES - 1))
        outside = (up_y & (lane < NZ)) | (~up_y & (lane >= LANES - NZ))
        near_y = jnp.where(outside, put, picked(here, jnp.where(up_y, below_y, above_y)))
        near_z = picked(here, jnp.where(up_z, below_z, above_z))
        upwind_x = jnp.where(open_x > 0, layer[rows_of(index, CHUNK)], back)
        upwind_y = jnp.where(jnp.where(up_y, below_open_y, above_open_y) > 0, near_y, back)
        upwind_z = jnp.where(jnp.where(up_z, below_open_z, above_open_z) > 0, near_z, back)
        outflow = x * (here - upwind_x)
        outflow += jnp.abs(y) * (here - upwind_y)
        outflow += jnp.abs(z) * (here - upwind_z)
        results.append((here - outflow) * fluid)
    return jnp.concatenate(results, axis=0)


def pack_part(packed, part, sign, values, factors):
    lane = lanes_of(CHUNK)
    for index in range(2):
        chunk = 2 * part + index
        positive = factors[1, rows_of(chunk, CHUNK)] * sign > 0
        packed = pack_edge(packed, values[rows_of(index, CHUNK)], positive, chunk, lane)
    return packed


def signs(flags):
    near = jnp.where(flags[1] == 1, 1.0, -1.0)
    return near, -near


def place_of_near(flags):
    return pl.multiple_of(PAD * (1 - flags[1]), 16), pl.multiple_of(PAD * flags[1], 16)


def first_kernel(
    flags, own, own_edge, received, straight, turned, masks_in, factors, lowered, masks_out
):
    same = flags[4] == 1
    place = lax.broadcasted_iota(jnp.int32, (8, LANES), 0)
    open_own = straight[PAD:].astype(F32)[:1]
    open_other = turned[PAD:].astype(F32)[:1]
    masks = masks_in[...]
    masks = jnp.where(place == 5, jnp.where(same, open_own, open_other), masks)
    masks = jnp.where(place == 6, jnp.where(same, open_other, open_own), masks)
    masks_out[...] = masks
    edge_own, edge_other = own_edge[...], received[PAD:].astype(F32)[:CHUNK]
    sign = jnp.where(flags[0] == 1, 1.0, -1.0)
    at_own = pl.multiple_of(PAD * (1 - flags[0]), 16)
    at_other = pl.multiple_of(PAD * flags[0], 16)
    for part in range(PAD // PART):
        span = rows_of(part, PART)
        mine, theirs = own[span], received[span].astype(F32)
        new_own = stream_part(
            part, sign, mine, theirs, straight[span].astype(F32), edge_own, masks, open_own, factors
        )
        new_other = stream_part(
            part, -sign, theirs, mine, turned[span].astype(F32), edge_other, masks, open_other, factors
        )
        lowered[pl.ds(at_own + PART * part, PART)] = new_own.astype(BF16)
        lowered[pl.ds(at_other + PART * part, PART)] = new_other.astype(BF16)


def streamed(flags, near, far, sibling, neighbour, edges, masks, factors):
    values = masks[...]
    edge_near, edge_far = (edges[rows_of(i, EDGE)].astype(F32)[:CHUNK] for i in range(2))
    sign_near, sign_far = signs(flags)
    start = pl.multiple_of(PAD * flags[1], 16)
    for part in range(PAD // PART):
        span = rows_of(part, PART)
        rows_near, rows_far = near[span], far[span]
        layer = sibling[pl.ds(start + PART * part, PART)].astype(F32)
        new_near = stream_part(
            part, sign_near, rows_near, rows_far, layer, edge_near, values, values[5:6], factors
        )
        layer = neighbour[span].astype(F32)
        new_far = stream_part(
            part, sign_far, rows_far, rows_near, layer, edge_far, values, values[6:7], factors
        )
        yield part, span, new_near, new_far


def between_kernel(flags, near, far, sibling, neighbour, edges, masks, factors, *outs):
    packed = (jnp.zeros((CHUNK, LANES), F32),) * 2
    for part, span, new_near, new_far in streamed(
        flags, near, far, sibling, neighbour, edges, masks, factors
    ):
        packed = give_rows(flags, part, new_near, new_far, factors, packed, outs[:4])
    outs[4][:EDGE], outs[4][EDGE:] = edge_block(packed[0]), edge_block(packed[1])


def lower_kernel(flags, near, far, sibling, neighbour, edges, masks, factors, lowered):
    at_near, at_far = place_of_near(flags)
    for part, span, new_near, new_far in streamed(
        flags, near, far, sibling, neighbour, edges, masks, factors
    ):
        lowered[pl.ds(at_near + PART * part, PART)] = new_near.astype(BF16)
        lowered[pl.ds(at_far + PART * part, PART)] = new_far.astype(BF16)


def last_kernel(flags, near, far, sibling, neighbour, edges, masks, factors, kept, message):
    same = flags[4] == 1
    for part, span, new_near, new_far in streamed(
        flags, near, far, sibling, neighbour, edges, masks, factors
    ):
        kept[span] = jnp.where(same, new_near, new_far)
        message[span] = jnp.where(same, new_far, new_near).astype(BF16)


def dot(left, right):
    return jnp.dot(left, right, preferred_element_type=F32)


def own_product(parts, half, values, span):
    return dot(parts[2 * half][span], values[:PAD]) + dot(parts[2 * half + 1][span], values[PAD:])


def collide_kernel(flags, m0, m1, m2, m3, lowered, other, rows_out):
    swapped = flags[2] == 1
    first = jnp.where(swapped, other[...], lowered[...])
    second = jnp.where(swapped, lowered[...], other[...])
    for part in range(PAD // PART):
        span = rows_of(part, PART)
        parts = m0, m1, m2, m3
        rows_out[span] = own_product(parts, 0, first, span) + own_product(parts, 1, second, span)


def give_rows(flags, part, rows_near, rows_far, factors, packed, outs):
    near, far, to_other_core, to_neighbour_chip = outs
    span = rows_of(part, PART)
    near[span], far[span] = rows_near, rows_far
    to_neighbour_chip[span] = rows_near.astype(BF16)
    to_other_core[span] = rows_far.astype(BF16)
    sign_near, sign_far = signs(flags)
    return (
        pack_part(packed[0], part, sign_near, rows_near, factors),
        pack_part(packed[1], part, sign_far, rows_far, factors),
    )


def give_product(flags, part, own, partner, factors, packed, outs):
    same = flags[4] == 1
    near, far = jnp.where(same, own, partner), jnp.where(same, partner, own)
    return give_rows(flags, part, near, far, factors, packed, outs)


def collide_partner_kernel(flags, own, matrix, lowered, other, factors, *outs):
    swapped = flags[2] == 1
    first = jnp.where(swapped, other[...], lowered[...])
    second = jnp.where(swapped, lowered[...], other[...])
    packed = (jnp.zeros((CHUNK, LANES), F32),) * 2
    for part in range(PAD // PART):
        span = rows_of(part, PART)
        partner = dot(matrix[span], first) + dot(matrix[PAD + PART * part : PAD + PART * (part + 1)], second)
        packed = give_product(flags, part, own[span], partner, factors, packed, outs[:4])
    outs[4][:EDGE], outs[4][EDGE:] = edge_block(packed[0]), edge_block(packed[1])


def early_kernel(flags, m0, m1, m2, m3, matrix, lowered, own_out, partner_out):
    values = lowered[...]
    for half in range(2):

        @pl.when(flags[2] == half)
        def _():
            for part in range(PAD // PART):
                span = rows_of(part, PART)
                start = PAD * half + PART * part
                own_out[span] = own_product((m0, m1, m2, m3), half, values, span)
                partner_out[span] = dot(matrix[start : start + PART], values)


def late_kernel(flags, m0, m1, m2, m3, matrix, other, own, partner, factors, *outs):
    *outs, total_own, total_partner = outs
    values = other[...]
    for half in range(2):

        @pl.when(flags[2] != half)
        def _():
            for part in range(PAD // PART):
                span = rows_of(part, PART)
                start = PAD * half + PART * part
                total_own[span] = own[span] + own_product((m0, m1, m2, m3), half, values, span)
                total_partner[span] = partner[span] + dot(matrix[start : start + PART], values)

    packed = (jnp.zeros((CHUNK, LANES), F32),) * 2
    for part in range(PAD // PART):
        span = rows_of(part, PART)
        packed = give_product(
            flags, part, total_own[span], total_partner[span], factors, packed, outs[:4]
        )
    outs[4][:EDGE], outs[4][EDGE:] = edge_block(packed[0]), edge_block(packed[1])


def reorder_kernel(flags, kept, ordered):
    ordered[...] = reordered(order_matrix(flags[0] == 1), kept[...])


def finish_kernel(flags, kept, received, evolved):
    order = order_matrix(flags[0] == 1)
    rest = jnp.dot(order, received[...], preferred_element_type=F32)
    mine = kept[...]
    half = flags[3]
    evolved[:, :LANES] = jnp.where(half == 0, mine, rest)[:ROWS]
    evolved[:, LANES:] = jnp.where(half == 0, rest, mine)[:ROWS]


def place(rows, columns, wanted):
    return (lax.broadcasted_iota(jnp.int32, (rows, columns), 0) == wanted[None, :]).astype(BF16)


def chosen(left, right):
    return jnp.dot(left, right, preferred_element_type=BF16)


def column_half(wide, block):
    column = lax.iota(jnp.int32, PAD)
    inside = column < ROWS
    start_a, start_b = 640 * block, jnp.where(block == 1, 1280, 2048)
    part_a = lax.dynamic_slice(wide, (0, start_a), (wide.shape[0], 768))
    part_b = lax.dynamic_slice(wide, (0, start_b), (wide.shape[0], 896))
    wanted_a = jnp.where(inside, ROWS * block + column - start_a, -1)
    wanted_b = jnp.where(inside, 4 * ROWS - 1 - ROWS * block - column - start_b, -1)
    halves = chosen(part_a, place(768, PAD, wanted_a)), chosen(part_b, place(896, PAD, wanted_b))
    return halves


def padded_columns(matrix):
    return jnp.pad(matrix, ((0, 0), (0, 2944 - matrix.shape[1])))


def per_device(populations, solid_mask, collision):
    cell, vel = lax.axis_index("cells"), lax.axis_index("vel")
    low = (vel < 2).astype(jnp.int32)
    core, z = cell % 2, cell // 2 % 8
    block = jnp.minimum(vel, 3 - vel)
    half = (1 - low) ^ (cell // RING % 2)
    needing = (cell + 1 - 2 * low) % 128
    straight_half = (1 - low) ^ (needing // RING % 2)
    same = (low != core).astype(jnp.int32)
    flags = jnp.stack([low, 1 - core, block, half, same, straight_half])
    flags = flags.astype(jnp.int32)

    row = CHUNK * z + lax.iota(jnp.int32, CHUNK)
    start = jnp.clip(jnp.where(low == 1, CHUNK * z, ROWS - CHUNK - CHUNK * z), 0, ROWS - CHUNK)
    wanted = jnp.where(row < ROWS, jnp.where(low == 1, row, ROWS - 1 - row) - start, -1)
    window = lax.dynamic_slice(collision, (start, 0), (CHUNK, collision.shape[1]))
    window = padded_columns(chosen(place(CHUNK, CHUNK, wanted).T, window))
    piece = jnp.concatenate(column_half(window, core), axis=1)
    populations, piece = lax.optimization_barrier((populations, piece))
    piece = to_mirror(piece)

    padded = jnp.pad(populations[:, 0, :], ((0, PAD - ROWS), (0, 0)))
    rows = (PAD, LANES)
    own, own_edge, message, straight, turned, masks, factors = call(
        prepare_kernel,
        [(rows, F32), ((CHUNK, LANES), F32), ((PAD + EDGE, LANES), BF16),
         ((PAD + 16, LANES), BF16), ((PAD + 16, LANES), BF16), ((8, LANES), F32), ((3, *rows), F32)],
        flags, padded, solid_mask, flops=2 * 3 * PAD * PAD * 256,
    )
    piece, _ = lax.optimization_barrier((piece, message))
    groups = [
        [(line * 8 + step) * 2 + side for side in range(2) for step in range(8)] for line in range(8)
    ]
    partner_matrix = lax.all_gather(piece, "cells", axis=0, tiled=True, axis_index_groups=groups)
    straight, turned = to_layer(straight, False), to_layer(turned, True)
    received = to_mirror(message)

    row = lax.iota(jnp.int32, PAD)
    wanted = jnp.where(row < ROWS, jnp.where(low == 1, row, ROWS - 1 - row), -1)
    received, collision = lax.optimization_barrier((received, collision))
    ordered = padded_columns(chosen(place(ROWS, PAD, wanted).T, collision))

    lowered, masks = call(
        first_kernel,
        [((2 * PAD, LANES), BF16), ((8, LANES), F32)],
        flags, own, own_edge, received, straight, turned, masks, factors, flops=100 * PAD * 256,
    )
    lowered, ordered = lax.optimization_barrier((lowered, ordered))
    matrix = *column_half(ordered, 0), *column_half(ordered, 1)
    edges_shape = ((2 * EDGE, LANES), BF16)
    sends = [(rows, F32)] * 2 + [(rows, BF16)] * 2 + [edges_shape]
    multiply = 2 * PAD * 4 * PAD * LANES
    work = 100 * PAD * LANES

    other = to_side(lowered)
    (own,) = call(collide_kernel, [(rows, F32)], flags, *matrix, lowered, other, flops=multiply)
    partner_matrix, own = lax.optimization_barrier((partner_matrix, own))
    near, far, for_sibling, for_neighbour, edges = call(
        collide_partner_kernel, sends, flags, own, partner_matrix, lowered, other, factors, flops=multiply
    )

    for step in range(1, STEPS):
        neighbour, edges = to_neighbour(for_neighbour), to_mirror(edges)
        sibling = with_sibling(for_sibling)
        near, far, for_sibling, for_neighbour, edges = call(
            between_kernel, sends, flags, near, far, sibling, neighbour, edges, masks, factors, flops=work
        )
        neighbour, edges = to_neighbour(for_neighbour), to_mirror(edges)
        sibling = with_sibling(for_sibling)
        (lowered,) = call(
            lower_kernel, [((2 * PAD, LANES), BF16)],
            flags, near, far, sibling, neighbour, edges, masks, factors, flops=work,
        )
        other = to_side(lowered)
        early = call(
            early_kernel, [(rows, F32)] * 2, flags, *matrix, partner_matrix, lowered, flops=multiply
        )
        near, far, for_sibling, for_neighbour, edges = call(
            late_kernel, sends, flags, *matrix, partner_matrix, other, *early, factors,
            flops=multiply, scratch=[(rows, F32)] * 2,
        )

    neighbour, edges = to_neighbour(for_neighbour), to_mirror(edges)
    sibling = with_sibling(for_sibling)
    kept, message = call(
        last_kernel, [(rows, F32), (rows, BF16)],
        flags, near, far, sibling, neighbour, edges, masks, factors, flops=work,
    )
    received = to_mirror(message)
    (kept,) = call(reorder_kernel, [(rows, F32)], flags, kept, flops=2 * 3 * PAD * PAD * LANES)
    (evolved,) = call(
        finish_kernel, [((ROWS, 2 * LANES), F32)], flags, kept, received, flops=2 * PAD * PAD * LANES
    )
    return evolved[:, None, :]


def solution(mesh):
    in_specs = (P("vel", "cells", None), P("cells", None), P("vel", None))
    out_specs = P("vel", "cells", None)
    return jax.shard_map(
        per_device, mesh=mesh, in_specs=in_specs, out_specs=out_specs, check_vma=False
    )
```

```python
import functools
import math

import jax
import jax.numpy as jnp
from jax import lax
from jax.experimental import pallas as pl
from jax.experimental.pallas import tpu as pltpu
from jax.sharding import PartitionSpec as P


K = 14
STEPS = 2
NZ = 16
BOTH = ("cells", "vel")
ROWS = 686
PAD = 704
CHUNK = 88
PART = 2 * CHUNK
EDGE = 96
LANES = 128
RING = 16
F32 = jnp.float32
BF16 = jnp.bfloat16
PARAMS = pltpu.CompilerParams(vmem_limit_bytes=20 * 1024 * 1024)


def pairs_of(target):
    pairs = []
    for cell in range(128):
        for part in range(4):
            to_cell, to_part = target(cell, part)
            pairs.append((cell * 4 + part, to_cell * 4 + to_part))
    return pairs


def with_sibling(array):
    groups = [[cell, cell + 1] for cell in range(0, 128, 2)]
    return lax.all_gather(array, "cells", axis=0, tiled=True, axis_index_groups=groups)


def to_layer(array, turned):
    def target(cell, part):
        return (cell - 1 if part < 2 else cell + 1) % 128, 3 - part if turned else part

    return lax.ppermute(array, BOTH, pairs_of(target))


def neighbour_of(cell, part):
    other = (cell - 1 if cell % 2 == 0 else cell + 1) % 128
    return other, part if (other // RING) % 2 == (cell // RING) % 2 else 3 - part


def to_neighbour(array):
    return lax.ppermute(array, BOTH, pairs_of(neighbour_of))


def to_mirror(array):
    return lax.ppermute(array, "vel", [(i, 3 - i) for i in range(4)])


def to_side(array):
    return lax.ppermute(array, "vel", [(i, i ^ 1) for i in range(4)])


def call(kernel, outs, flags, *arrays, flops=0, stay=0, scratch=()):
    moved = sum(x.size * x.dtype.itemsize for x in arrays)
    moved += sum(math.prod(shape) * jnp.dtype(dtype).itemsize for shape, dtype in outs)
    vmem, hbm = (pl.BlockSpec(memory_space=space) for space in (pltpu.VMEM, pltpu.HBM))
    count = len(arrays) - stay
    specs = [vmem] * count + [hbm] * stay
    arrays = *arrays[:count], *(pltpu.with_memory_space_constraint(x, pltpu.HBM) for x in arrays[count:])
    return pl.pallas_call(
        kernel,
        out_shape=[jax.ShapeDtypeStruct(shape, dtype) for shape, dtype in outs],
        in_specs=[pl.BlockSpec(memory_space=pltpu.SMEM)] + specs,
        out_specs=[vmem] * len(outs),
        scratch_shapes=scratch,
        compiler_params=PARAMS,
        cost_estimate=pl.CostEstimate(flops=flops, bytes_accessed=moved, transcendentals=0),
    )(flags, *arrays)


def roll(values, shift):
    return pltpu.roll(values, shift % values.shape[1], 1)


def order_matrix(low):
    row = lax.broadcasted_iota(jnp.int32, (PAD, PAD), 0)
    column = lax.broadcasted_iota(jnp.int32, (PAD, PAD), 1)
    wanted = jnp.where(low, row, ROWS - 1 - row)
    return jnp.where((column == wanted) & (row < ROWS), 1.0, 0.0).astype(BF16)


def reordered(order, values):
    total = jnp.zeros(values.shape, F32)
    for _ in range(3):
        part = values.astype(BF16)
        total += jnp.dot(order, part, preferred_element_type=F32)
        values = values - part.astype(F32)
    return total


def signed_factors(block, chunk):
    row = CHUNK * chunk + lax.broadcasted_iota(jnp.int32, (CHUNK, LANES), 0)
    ids = ROWS * block + row
    upper = (ids * 4682) >> 16
    k_z = ids - K * upper
    k_x = (upper * 4682) >> 16
    k_y = upper - K * k_x
    centre = (K - 1) / 2.0
    x, y, z = ((k.astype(F32) - centre) * (0.3 / centre) for k in (k_x, k_y, k_z))
    return jnp.abs(x), y, z


def lanes_of(rows):
    return lax.broadcasted_iota(jnp.int32, (rows, LANES), 1)


def lower_z(values):
    z_place = lax.broadcasted_iota(jnp.int32, values.shape, 1) % NZ
    return jnp.where(z_place == 0, roll(values, 1 - NZ), roll(values, 1))


def upper_z(values):
    z_place = lax.broadcasted_iota(jnp.int32, values.shape, 1) % NZ
    return jnp.where(z_place == NZ - 1, roll(values, NZ - 1), roll(values, -1))


def picked(values, lanes):
    return jnp.take_along_axis(values, lanes, axis=1, mode="promise_in_bounds")


def pack_edge(packed, values, positive, chunk, lane):
    place = lane & (NZ - 1)
    edge = picked(values, jnp.where(positive, place + LANES - NZ, place))
    return jnp.where((lane >> 4) == chunk, edge, packed)


def edge_block(packed):
    return jnp.concatenate([packed, jnp.zeros((EDGE - CHUNK, LANES), F32)], axis=0).astype(BF16)


def prepare_kernel(
    flags, populations, solid, own, own_edge, message, straight, turned, masks, factors
):
    low, block, half = flags[0] == 1, flags[2], flags[3]
    ordered = reordered(order_matrix(low), populations[...])
    left, right = ordered[:, :LANES], ordered[:, LANES:]
    mine = jnp.where(half == 0, left, right)
    rest = jnp.where(half == 0, right, left)
    own[...] = mine
    edges = jnp.zeros((CHUNK, LANES), F32)
    sent = jnp.zeros((CHUNK, LANES), F32)
    lane = lanes_of(CHUNK)
    for chunk in range(PAD // CHUNK):
        rows = slice(CHUNK * chunk, CHUNK * (chunk + 1))
        x, y, z = signed_factors(block, chunk)
        factors[0, rows], factors[1, rows], factors[2, rows] = x, y, z
        positive = jnp.where(low, y, -y) > 0
        edges = pack_edge(edges, rest[rows], positive, chunk, lane)
        sent = pack_edge(sent, mine[rows], positive, chunk, lane)
    own_edge[...] = edges
    message[:PAD] = rest.astype(BF16)
    message[PAD:] = edge_block(sent)
    fluid = jnp.where(jnp.broadcast_to(solid[...], (8, 2 * LANES)) == 0, 1.0, 0.0)
    place = lax.broadcasted_iota(jnp.int32, (8, 2 * LANES), 0)
    found = jnp.zeros((8, 2 * LANES), F32)
    near = (fluid, roll(fluid, NZ), roll(fluid, -NZ), lower_z(fluid), upper_z(fluid))
    for index, value in enumerate(near):
        found = jnp.where(place == index, value, found)
    masks[...] = jnp.where(half == 0, found[:, :LANES], found[:, LANES:])
    row = lax.broadcasted_iota(jnp.int32, (16, LANES), 0)
    halves = []
    for side in range(2):
        cells = slice(LANES * side, LANES * (side + 1))
        open_cells = jnp.where(row == 0, jnp.broadcast_to(fluid[:1, cells], (16, LANES)), 0.0)
        halves.append((ordered[:, cells].astype(BF16), open_cells.astype(BF16)))
    for place, target in ((flags[5], straight), (1 - flags[5], turned)):
        for rows, low_value, high_value in zip((slice(0, PAD), slice(PAD, PAD + 16)), *halves):
            target[rows] = jnp.where(place == 0, low_value, high_value)


def rows_of(index, size):
    return slice(size * index, size * (index + 1))


def stream_part(part, sign, values, mirror, layer, edge, masks, open_x, factors):
    fluid, below_open_y, above_open_y, below_open_z, above_open_z = (
        jnp.broadcast_to(masks[i : i + 1], (CHUNK, LANES)) for i in range(5)
    )
    open_x = jnp.broadcast_to(open_x, (CHUNK, LANES))
    lane = lanes_of(CHUNK)
    z_place = lane & (NZ - 1)
    below_z = jnp.where(z_place == 0, lane + NZ - 1, lane - 1)
    above_z = jnp.where(z_place == NZ - 1, lane + 1 - NZ, lane + 1)
    below_y, above_y = (lane + LANES - NZ) & (LANES - 1), (lane + NZ) & (LANES - 1)
    results = []
    for index in range(2):
        chunk = 2 * part + index
        x, y, z = (factors[i, rows_of(chunk, CHUNK)] for i in range(3))
        up_y, up_z = y * sign > 0, z * sign > 0
        here, back = values[rows_of(index, CHUNK)], mirror[rows_of(index, CHUNK)]
        at_edge = jnp.where(up_y, lane, lane + NZ)
        put = picked(edge, (at_edge + NZ * chunk) & (LANES - 1))
        outside = (up_y & (lane < NZ)) | (~up_y & (lane >= LANES - NZ))
        near_y = jnp.where(outside, put, picked(here, jnp.where(up_y, below_y, above_y)))
        near_z = picked(here, jnp.where(up_z, below_z, above_z))
        upwind_x = jnp.where(open_x > 0, layer[rows_of(index, CHUNK)], back)
        upwind_y = jnp.where(jnp.where(up_y, below_open_y, above_open_y) > 0, near_y, back)
        upwind_z = jnp.where(jnp.where(up_z, below_open_z, above_open_z) > 0, near_z, back)
        outflow = x * (here - upwind_x)
        outflow += jnp.abs(y) * (here - upwind_y)
        outflow += jnp.abs(z) * (here - upwind_z)
        results.append((here - outflow) * fluid)
    return jnp.concatenate(results, axis=0)


def pack_part(packed, part, sign, values, factors):
    lane = lanes_of(CHUNK)
    for index in range(2):
        chunk = 2 * part + index
        positive = factors[1, rows_of(chunk, CHUNK)] * sign > 0
        packed = pack_edge(packed, values[rows_of(index, CHUNK)], positive, chunk, lane)
    return packed


def signs(flags):
    near = jnp.where(flags[1] == 1, 1.0, -1.0)
    return near, -near


def place_of_near(flags):
    return pl.multiple_of(PAD * (1 - flags[1]), 16), pl.multiple_of(PAD * flags[1], 16)


def first_kernel(
    flags, own, own_edge, received, straight, turned, masks_in, factors, lowered, masks_out
):
    same = flags[4] == 1
    place = lax.broadcasted_iota(jnp.int32, (8, LANES), 0)
    open_own = straight[PAD:].astype(F32)[:1]
    open_other = turned[PAD:].astype(F32)[:1]
    masks = masks_in[...]
    masks = jnp.where(place == 5, jnp.where(same, open_own, open_other), masks)
    masks = jnp.where(place == 6, jnp.where(same, open_other, open_own), masks)
    masks_out[...] = masks
    edge_own, edge_other = own_edge[...], received[PAD:].astype(F32)[:CHUNK]
    sign = jnp.where(flags[0] == 1, 1.0, -1.0)
    at_own = pl.multiple_of(PAD * (1 - flags[0]), 16)
    at_other = pl.multiple_of(PAD * flags[0], 16)
    for part in range(PAD // PART):
        span = rows_of(part, PART)
        mine, theirs = own[span], received[span].astype(F32)
        new_own = stream_part(
            part, sign, mine, theirs, straight[span].astype(F32), edge_own, masks, open_own, factors
        )
        new_other = stream_part(
            part, -sign, theirs, mine, turned[span].astype(F32), edge_other, masks, open_other, factors
        )
        lowered[pl.ds(at_own + PART * part, PART)] = new_own.astype(BF16)
        lowered[pl.ds(at_other + PART * part, PART)] = new_other.astype(BF16)


def streamed(flags, near, far, sibling, neighbour, edges, masks, factors):
    values = masks[...]
    edge_near, edge_far = (edges[rows_of(i, EDGE)].astype(F32)[:CHUNK] for i in range(2))
    sign_near, sign_far = signs(flags)
    start = pl.multiple_of(PAD * flags[1], 16)
    for part in range(PAD // PART):
        span = rows_of(part, PART)
        rows_near, rows_far = near[span], far[span]
        layer = sibling[pl.ds(start + PART * part, PART)].astype(F32)
        new_near = stream_part(
            part, sign_near, rows_near, rows_far, layer, edge_near, values, values[5:6], factors
        )
        layer = neighbour[span].astype(F32)
        new_far = stream_part(
            part, sign_far, rows_far, rows_near, layer, edge_far, values, values[6:7], factors
        )
        yield part, span, new_near, new_far


def between_kernel(flags, near, far, sibling, neighbour, edges, masks, factors, *outs):
    packed = (jnp.zeros((CHUNK, LANES), F32),) * 2
    for part, span, new_near, new_far in streamed(
        flags, near, far, sibling, neighbour, edges, masks, factors
    ):
        packed = give_rows(flags, part, new_near, new_far, factors, packed, outs[:4])
    outs[4][:EDGE], outs[4][EDGE:] = edge_block(packed[0]), edge_block(packed[1])


def lower_kernel(flags, near, far, sibling, neighbour, edges, masks, factors, lowered):
    at_near, at_far = place_of_near(flags)
    for part, span, new_near, new_far in streamed(
        flags, near, far, sibling, neighbour, edges, masks, factors
    ):
        lowered[pl.ds(at_near + PART * part, PART)] = new_near.astype(BF16)
        lowered[pl.ds(at_far + PART * part, PART)] = new_far.astype(BF16)


def last_kernel(given, flags, near, far, sibling, neighbour, edges, masks, factors, out):
    same = (flags[4] == 1) != given
    values = masks[...]
    edge_near, edge_far = (edges[rows_of(i, EDGE)].astype(F32)[:CHUNK] for i in range(2))
    edge, open_x = jnp.where(same, edge_near, edge_far), jnp.where(same, values[5:6], values[6:7])
    sign = jnp.where((flags[0] == 1) != given, 1.0, -1.0)
    start = pl.multiple_of(PAD * flags[1], 16)
    results = []
    for part in range(PAD // PART):
        span = rows_of(part, PART)
        rows_near, rows_far = near[span], far[span]
        layer_near = sibling[pl.ds(start + PART * part, PART)].astype(F32)
        layer = jnp.where(same, layer_near, neighbour[span].astype(F32))
        rows, mirror = jnp.where(same, rows_near, rows_far), jnp.where(same, rows_far, rows_near)
        results.append(stream_part(part, sign, rows, mirror, layer, edge, values, open_x, factors))
    results = jnp.concatenate(results, axis=0)
    if given:
        out[...] = results.astype(BF16)
    else:
        out[...] = reordered(order_matrix(flags[0] == 1), results)


def dot(left, right):
    return jnp.dot(left, right, preferred_element_type=F32)


def collide_kernel(flags, lowered, other, m0, m1, m2, m3, rows_out, held, done):
    copies = [
        pltpu.make_async_copy(source, held.at[index], done.at[index])
        for index, source in enumerate((m0, m1, m2, m3))
    ]
    for copy in copies:
        copy.start()
    swapped = flags[2] == 1
    first = jnp.where(swapped, other[...], lowered[...])
    second = jnp.where(swapped, lowered[...], other[...])
    values = first[:PAD], first[PAD:], second[:PAD], second[PAD:]
    for index, copy in enumerate(copies):
        copy.wait()
        for part in range(PAD // PART):
            span = rows_of(part, PART)
            total = dot(held[index, span], values[index])
            rows_out[span] = total if index == 0 else rows_out[span] + total


def give_rows(flags, part, rows_near, rows_far, factors, packed, outs):
    near, far, to_other_core, to_neighbour_chip = outs
    span = rows_of(part, PART)
    near[span], far[span] = rows_near, rows_far
    to_neighbour_chip[span] = rows_near.astype(BF16)
    to_other_core[span] = rows_far.astype(BF16)
    sign_near, sign_far = signs(flags)
    return (
        pack_part(packed[0], part, sign_near, rows_near, factors),
        pack_part(packed[1], part, sign_far, rows_far, factors),
    )


def give_product(flags, part, own, partner, factors, packed, outs):
    same = flags[4] == 1
    near, far = jnp.where(same, own, partner), jnp.where(same, partner, own)
    return give_rows(flags, part, near, far, factors, packed, outs)


def collide_partner_kernel(flags, own, lowered, other, factors, matrix, *refs):
    *outs, held, done = refs
    parts = PAD // PART
    copies = []
    for part in range(parts):
        for half in range(2):
            index = parts * half + part
            copy = pltpu.make_async_copy(
                matrix.at[rows_of(index, PART)], held.at[rows_of(index, PART)], done.at[index]
            )
            copy.start()
            copies.append(copy)
    swapped = flags[2] == 1
    first = jnp.where(swapped, other[...], lowered[...])
    second = jnp.where(swapped, lowered[...], other[...])
    packed = (jnp.zeros((CHUNK, LANES), F32),) * 2
    for part in range(parts):
        span = rows_of(part, PART)
        copies[2 * part].wait()
        partner = dot(held[span], first)
        copies[2 * part + 1].wait()
        partner += dot(held[rows_of(parts + part, PART)], second)
        packed = give_product(flags, part, own[span], partner, factors, packed, outs[:4])
    outs[4][:EDGE], outs[4][EDGE:] = edge_block(packed[0]), edge_block(packed[1])


def half_products(half, values, parts, matrix, held_own, held_partner, done, give):
    count = PAD // PART
    own = [
        pltpu.make_async_copy(parts[2 * half + i], held_own.at[i], done.at[i]) for i in range(2)
    ]
    partner = [
        pltpu.make_async_copy(
            matrix.at[rows_of(count * half + i, PART)], held_partner.at[rows_of(i, PART)], done.at[2 + i]
        )
        for i in range(count)
    ]
    for copy in partner + own:
        copy.start()
    totals = []
    for part in range(count):
        partner[part].wait()
        totals.append(dot(held_partner[rows_of(part, PART)], values))
    for copy in own:
        copy.wait()
    for part in range(count):
        span = rows_of(part, PART)
        total = dot(held_own[0, span], values[:PAD]) + dot(held_own[1, span], values[PAD:])
        give(span, total, totals[part])


def early_kernel(flags, lowered, m0, m1, m2, m3, matrix, own_out, partner_out, *scratch):
    values = lowered[...]

    def give(span, own, partner):
        own_out[span] = own
        partner_out[span] = partner

    for half in range(2):

        @pl.when(flags[2] == half)
        def _():
            half_products(half, values, (m0, m1, m2, m3), matrix, *scratch, give)


def late_kernel(flags, other, own, partner, factors, m0, m1, m2, m3, matrix, *refs):
    outs, (total_own, total_partner, *scratch) = refs[:5], refs[5:]
    values = other[...]

    def give(span, more_own, more_partner):
        total_own[span] = own[span] + more_own
        total_partner[span] = partner[span] + more_partner

    for half in range(2):

        @pl.when(flags[2] != half)
        def _():
            half_products(half, values, (m0, m1, m2, m3), matrix, *scratch, give)

    packed = (jnp.zeros((CHUNK, LANES), F32),) * 2
    for part in range(PAD // PART):
        span = rows_of(part, PART)
        packed = give_product(
            flags, part, total_own[span], total_partner[span], factors, packed, outs[:4]
        )
    outs[4][:EDGE], outs[4][EDGE:] = edge_block(packed[0]), edge_block(packed[1])


def finish_kernel(flags, kept, received, evolved):
    order = order_matrix(flags[0] == 1)
    rest = jnp.dot(order, received[...], preferred_element_type=F32)
    mine = kept[...]
    half = flags[3]
    evolved[:, 0, :LANES] = jnp.where(half == 0, mine, rest)[:ROWS]
    evolved[:, 0, LANES:] = jnp.where(half == 0, rest, mine)[:ROWS]


def place(rows, columns, wanted):
    return (lax.broadcasted_iota(jnp.int32, (rows, columns), 0) == wanted[None, :]).astype(BF16)


def chosen(left, right):
    return jnp.dot(left, right, preferred_element_type=BF16)


def column_half(wide, block):
    column = lax.iota(jnp.int32, PAD)
    inside = column < ROWS
    start_a, start_b = 640 * block, jnp.where(block == 1, 1280, 2048)
    part_a = lax.dynamic_slice(wide, (0, start_a), (wide.shape[0], 768))
    part_b = lax.dynamic_slice(wide, (0, start_b), (wide.shape[0], 896))
    wanted_a = jnp.where(inside, ROWS * block + column - start_a, -1)
    wanted_b = jnp.where(inside, 4 * ROWS - 1 - ROWS * block - column - start_b, -1)
    halves = chosen(part_a, place(768, PAD, wanted_a)), chosen(part_b, place(896, PAD, wanted_b))
    return halves


def padded_columns(matrix):
    return jnp.pad(matrix, ((0, 0), (0, 2944 - matrix.shape[1])))


def per_device(populations, solid_mask, collision):
    cell, vel = lax.axis_index("cells"), lax.axis_index("vel")
    low = (vel < 2).astype(jnp.int32)
    core, z = cell % 2, cell // 2 % 8
    block = jnp.minimum(vel, 3 - vel)
    half = (1 - low) ^ (cell // RING % 2)
    needing = (cell + 1 - 2 * low) % 128
    straight_half = (1 - low) ^ (needing // RING % 2)
    same = (low != core).astype(jnp.int32)
    flags = jnp.stack([low, 1 - core, block, half, same, straight_half])
    flags = flags.astype(jnp.int32)

    row = CHUNK * z + lax.iota(jnp.int32, CHUNK)
    start = jnp.clip(jnp.where(low == 1, CHUNK * z, ROWS - CHUNK - CHUNK * z), 0, ROWS - CHUNK)
    wanted = jnp.where(row < ROWS, jnp.where(low == 1, row, ROWS - 1 - row) - start, -1)
    window = lax.dynamic_slice(collision, (start, 0), (CHUNK, collision.shape[1]))
    window = padded_columns(chosen(place(CHUNK, CHUNK, wanted).T, window))
    piece = jnp.concatenate(column_half(window, core), axis=1)
    populations, piece = lax.optimization_barrier((populations, piece))
    piece = to_mirror(piece)

    padded = jnp.pad(populations[:, 0, :], ((0, PAD - ROWS), (0, 0)))
    rows = (PAD, LANES)
    own, own_edge, message, straight, turned, masks, factors = call(
        prepare_kernel,
        [(rows, F32), ((CHUNK, LANES), F32), ((PAD + EDGE, LANES), BF16),
         ((PAD + 16, LANES), BF16), ((PAD + 16, LANES), BF16), ((8, LANES), F32), ((3, *rows), F32)],
        flags, padded, solid_mask, flops=2 * 3 * PAD * PAD * 256,
    )
    piece, _ = lax.optimization_barrier((piece, message))
    groups = [
        [(line * 8 + step) * 2 + side for side in range(2) for step in range(8)] for line in range(8)
    ]
    partner_matrix = lax.all_gather(piece, "cells", axis=0, tiled=True, axis_index_groups=groups)
    straight, turned = to_layer(straight, False), to_layer(turned, True)
    received = to_mirror(message)

    row = lax.iota(jnp.int32, PAD)
    wanted = jnp.where(row < ROWS, jnp.where(low == 1, row, ROWS - 1 - row), -1)
    received, collision = lax.optimization_barrier((received, collision))
    ordered = padded_columns(chosen(place(ROWS, PAD, wanted).T, collision))

    lowered, masks = call(
        first_kernel,
        [((2 * PAD, LANES), BF16), ((8, LANES), F32)],
        flags, own, own_edge, received, straight, turned, masks, factors, flops=100 * PAD * 256,
    )
    lowered, ordered = lax.optimization_barrier((lowered, ordered))
    matrix = *column_half(ordered, 0), *column_half(ordered, 1)
    edges_shape = ((2 * EDGE, LANES), BF16)
    sends = [(rows, F32)] * 2 + [(rows, BF16)] * 2 + [edges_shape]
    multiply = 2 * PAD * 4 * PAD * LANES
    work = 100 * PAD * LANES

    other = to_side(lowered)
    dma = pltpu.SemaphoreType.DMA
    (own,) = call(
        collide_kernel, [(rows, F32)], flags, lowered, other, *matrix, flops=multiply, stay=4,
        scratch=[pltpu.VMEM((4, PAD, PAD), BF16), dma((4,))],
    )
    partner_matrix, own = lax.optimization_barrier((partner_matrix, own))
    near, far, for_sibling, for_neighbour, edges = call(
        collide_partner_kernel, sends, flags, own, lowered, other, factors, partner_matrix,
        flops=multiply, stay=1, scratch=[pltpu.VMEM((2 * PAD, 2 * PAD), BF16), dma((8,))],
    )
    held = [pltpu.VMEM((2, PAD, PAD), BF16), pltpu.VMEM((PAD, 2 * PAD), BF16), dma((6,))]

    for step in range(1, STEPS):
        neighbour, edges = to_neighbour(for_neighbour), to_mirror(edges)
        sibling = with_sibling(for_sibling)
        near, far, for_sibling, for_neighbour, edges = call(
            between_kernel, sends, flags, near, far, sibling, neighbour, edges, masks, factors, flops=work
        )
        neighbour, edges = to_neighbour(for_neighbour), to_mirror(edges)
        sibling = with_sibling(for_sibling)
        (lowered,) = call(
            lower_kernel, [((2 * PAD, LANES), BF16)],
            flags, near, far, sibling, neighbour, edges, masks, factors, flops=work,
        )
        other = to_side(lowered)
        early = call(
            early_kernel, [(rows, F32)] * 2, flags, lowered, *matrix, partner_matrix,
            flops=multiply, stay=5, scratch=held,
        )
        near, far, for_sibling, for_neighbour, edges = call(
            late_kernel, sends, flags, other, *early, factors, *matrix, partner_matrix,
            flops=multiply, stay=5, scratch=[pltpu.VMEM(rows, F32)] * 2 + held,
        )

    neighbour, edges = to_neighbour(for_neighbour), to_mirror(edges)
    sibling = with_sibling(for_sibling)
    last = flags, near, far, sibling, neighbour, edges, masks, factors
    (message,) = call(functools.partial(last_kernel, True), [(rows, BF16)], *last, flops=work)
    received = to_mirror(message)
    (kept,) = call(functools.partial(last_kernel, False), [(rows, F32)], *last, flops=multiply)
    (evolved,) = call(
        finish_kernel, [((ROWS, 1, 2 * LANES), F32)], flags, kept, received, flops=2 * PAD * PAD * LANES
    )
    return evolved


def solution(mesh):
    in_specs = (P("vel", "cells", None), P("cells", None), P("vel", None))
    out_specs = P("vel", "cells", None)
    return jax.shard_map(
        per_device, mesh=mesh, in_specs=in_specs, out_specs=out_specs, check_vma=False
    )
```

```python
import functools
import math

import jax
import jax.numpy as jnp
from jax import lax
from jax.experimental import pallas as pl
from jax.experimental.pallas import tpu as pltpu
from jax.sharding import PartitionSpec as P


K = 14
STEPS = 2
NZ = 16
BOTH = ("cells", "vel")
ROWS = 686
PAD = 704
CHUNK = 88
PART = 2 * CHUNK
EDGE = 96
LANES = 128
RING = 16
F32 = jnp.float32
BF16 = jnp.bfloat16
PARAMS = pltpu.CompilerParams(vmem_limit_bytes=20 * 1024 * 1024)


def pairs_of(target):
    pairs = []
    for cell in range(128):
        for part in range(4):
            to_cell, to_part = target(cell, part)
            pairs.append((cell * 4 + part, to_cell * 4 + to_part))
    return pairs


def with_sibling(array):
    groups = [[cell, cell + 1] for cell in range(0, 128, 2)]
    return lax.all_gather(array, "cells", axis=0, tiled=True, axis_index_groups=groups)


def to_layer(array, turned):
    def target(cell, part):
        return (cell - 1 if part < 2 else cell + 1) % 128, 3 - part if turned else part

    return lax.ppermute(array, BOTH, pairs_of(target))


def neighbour_of(cell, part):
    other = (cell - 1 if cell % 2 == 0 else cell + 1) % 128
    return other, part if (other // RING) % 2 == (cell // RING) % 2 else 3 - part


def to_neighbour(array):
    return lax.ppermute(array, BOTH, pairs_of(neighbour_of))


def to_mirror(array):
    return lax.ppermute(array, "vel", [(i, 3 - i) for i in range(4)])


def to_side(array):
    return lax.ppermute(array, "vel", [(i, i ^ 1) for i in range(4)])


def call(kernel, outs, flags, *arrays, flops=0, stay=0, scratch=()):
    moved = sum(x.size * x.dtype.itemsize for x in arrays)
    moved += sum(math.prod(shape) * jnp.dtype(dtype).itemsize for shape, dtype in outs)
    vmem, hbm = (pl.BlockSpec(memory_space=space) for space in (pltpu.VMEM, pltpu.HBM))
    count = len(arrays) - stay
    specs = [vmem] * count + [hbm] * stay
    arrays = *arrays[:count], *(pltpu.with_memory_space_constraint(x, pltpu.HBM) for x in arrays[count:])
    return pl.pallas_call(
        kernel,
        out_shape=[jax.ShapeDtypeStruct(shape, dtype) for shape, dtype in outs],
        in_specs=[pl.BlockSpec(memory_space=pltpu.SMEM)] + specs,
        out_specs=[vmem] * len(outs),
        scratch_shapes=scratch,
        compiler_params=PARAMS,
        cost_estimate=pl.CostEstimate(flops=flops, bytes_accessed=moved, transcendentals=0),
    )(flags, *arrays)


def roll(values, shift):
    return pltpu.roll(values, shift % values.shape[1], 1)


def order_matrix(low):
    row = lax.broadcasted_iota(jnp.int32, (PAD, PAD), 0)
    column = lax.broadcasted_iota(jnp.int32, (PAD, PAD), 1)
    wanted = jnp.where(low, row, ROWS - 1 - row)
    return jnp.where((column == wanted) & (row < ROWS), 1.0, 0.0).astype(BF16)


def reordered(order, values):
    total = jnp.zeros(values.shape, F32)
    for _ in range(3):
        part = values.astype(BF16)
        total += jnp.dot(order, part, preferred_element_type=F32)
        values = values - part.astype(F32)
    return total


def signed_factors(block, chunk):
    row = CHUNK * chunk + lax.broadcasted_iota(jnp.int32, (CHUNK, LANES), 0)
    ids = ROWS * block + row
    upper = (ids * 4682) >> 16
    k_z = ids - K * upper
    k_x = (upper * 4682) >> 16
    k_y = upper - K * k_x
    centre = (K - 1) / 2.0
    x, y, z = ((k.astype(F32) - centre) * (0.3 / centre) for k in (k_x, k_y, k_z))
    return jnp.abs(x), y, z


def lanes_of(rows):
    return lax.broadcasted_iota(jnp.int32, (rows, LANES), 1)


def lower_z(values):
    z_place = lax.broadcasted_iota(jnp.int32, values.shape, 1) % NZ
    return jnp.where(z_place == 0, roll(values, 1 - NZ), roll(values, 1))


def upper_z(values):
    z_place = lax.broadcasted_iota(jnp.int32, values.shape, 1) % NZ
    return jnp.where(z_place == NZ - 1, roll(values, NZ - 1), roll(values, -1))


def picked(values, lanes):
    return jnp.take_along_axis(values, lanes, axis=1, mode="promise_in_bounds")


def pack_edge(packed, values, positive, chunk, lane):
    place = lane & (NZ - 1)
    edge = picked(values, jnp.where(positive, place + LANES - NZ, place))
    return jnp.where((lane >> 4) == chunk, edge, packed)


def edge_block(packed):
    return jnp.concatenate([packed, jnp.zeros((EDGE - CHUNK, LANES), F32)], axis=0).astype(BF16)


def prepare_kernel(
    flags, populations, solid, own, own_edge, message, straight, turned, masks, factors
):
    low, block, half = flags[0] == 1, flags[2], flags[3]
    ordered = reordered(order_matrix(low), populations[...])
    left, right = ordered[:, :LANES], ordered[:, LANES:]
    mine = jnp.where(half == 0, left, right)
    rest = jnp.where(half == 0, right, left)
    own[...] = mine
    edges = jnp.zeros((CHUNK, LANES), F32)
    sent = jnp.zeros((CHUNK, LANES), F32)
    lane = lanes_of(CHUNK)
    for chunk in range(PAD // CHUNK):
        rows = slice(CHUNK * chunk, CHUNK * (chunk + 1))
        x, y, z = signed_factors(block, chunk)
        factors[0, rows], factors[1, rows], factors[2, rows] = x, y, z
        positive = jnp.where(low, y, -y) > 0
        edges = pack_edge(edges, rest[rows], positive, chunk, lane)
        sent = pack_edge(sent, mine[rows], positive, chunk, lane)
    own_edge[...] = edges
    message[:PAD] = rest.astype(BF16)
    message[PAD:] = edge_block(sent)
    fluid = jnp.where(jnp.broadcast_to(solid[...], (8, 2 * LANES)) == 0, 1.0, 0.0)
    place = lax.broadcasted_iota(jnp.int32, (8, 2 * LANES), 0)
    found = jnp.zeros((8, 2 * LANES), F32)
    near = (fluid, roll(fluid, NZ), roll(fluid, -NZ), lower_z(fluid), upper_z(fluid))
    for index, value in enumerate(near):
        found = jnp.where(place == index, value, found)
    masks[...] = jnp.where(half == 0, found[:, :LANES], found[:, LANES:])
    row = lax.broadcasted_iota(jnp.int32, (16, LANES), 0)
    halves = []
    for side in range(2):
        cells = slice(LANES * side, LANES * (side + 1))
        open_cells = jnp.where(row == 0, jnp.broadcast_to(fluid[:1, cells], (16, LANES)), 0.0)
        halves.append((ordered[:, cells].astype(BF16), open_cells.astype(BF16)))
    for place, target in ((flags[5], straight), (1 - flags[5], turned)):
        for rows, low_value, high_value in zip((slice(0, PAD), slice(PAD, PAD + 16)), *halves):
            target[rows] = jnp.where(place == 0, low_value, high_value)


def rows_of(index, size):
    return slice(size * index, size * (index + 1))


def stream_part(part, sign, values, mirror, layer, edge, masks, open_x, factors):
    fluid, below_open_y, above_open_y, below_open_z, above_open_z = (
        jnp.broadcast_to(masks[i : i + 1], (CHUNK, LANES)) for i in range(5)
    )
    open_x = jnp.broadcast_to(open_x, (CHUNK, LANES))
    lane = lanes_of(CHUNK)
    z_place = lane & (NZ - 1)
    below_z = jnp.where(z_place == 0, lane + NZ - 1, lane - 1)
    above_z = jnp.where(z_place == NZ - 1, lane + 1 - NZ, lane + 1)
    below_y, above_y = (lane + LANES - NZ) & (LANES - 1), (lane + NZ) & (LANES - 1)
    results = []
    for index in range(2):
        chunk = 2 * part + index
        x, y, z = (factors[i, rows_of(chunk, CHUNK)] for i in range(3))
        up_y, up_z = y * sign > 0, z * sign > 0
        here, back = values[rows_of(index, CHUNK)], mirror[rows_of(index, CHUNK)]
        at_edge = jnp.where(up_y, lane, lane + NZ)
        put = picked(edge, (at_edge + NZ * chunk) & (LANES - 1))
        outside = (up_y & (lane < NZ)) | (~up_y & (lane >= LANES - NZ))
        near_y = jnp.where(outside, put, picked(here, jnp.where(up_y, below_y, above_y)))
        near_z = picked(here, jnp.where(up_z, below_z, above_z))
        upwind_x = jnp.where(open_x > 0, layer[rows_of(index, CHUNK)], back)
        upwind_y = jnp.where(jnp.where(up_y, below_open_y, above_open_y) > 0, near_y, back)
        upwind_z = jnp.where(jnp.where(up_z, below_open_z, above_open_z) > 0, near_z, back)
        outflow = x * (here - upwind_x)
        outflow += jnp.abs(y) * (here - upwind_y)
        outflow += jnp.abs(z) * (here - upwind_z)
        results.append((here - outflow) * fluid)
    return jnp.concatenate(results, axis=0)


def pack_part(packed, part, sign, values, factors):
    lane = lanes_of(CHUNK)
    for index in range(2):
        chunk = 2 * part + index
        positive = factors[1, rows_of(chunk, CHUNK)] * sign > 0
        packed = pack_edge(packed, values[rows_of(index, CHUNK)], positive, chunk, lane)
    return packed


def signs(flags):
    near = jnp.where(flags[1] == 1, 1.0, -1.0)
    return near, -near


def place_of_near(flags):
    return pl.multiple_of(PAD * (1 - flags[1]), 16), pl.multiple_of(PAD * flags[1], 16)


def first_kernel(
    flags, own, own_edge, received, straight, turned, masks_in, factors, lowered, masks_out
):
    same = flags[4] == 1
    place = lax.broadcasted_iota(jnp.int32, (8, LANES), 0)
    open_own = straight[PAD:].astype(F32)[:1]
    open_other = turned[PAD:].astype(F32)[:1]
    masks = masks_in[...]
    masks = jnp.where(place == 5, jnp.where(same, open_own, open_other), masks)
    masks = jnp.where(place == 6, jnp.where(same, open_other, open_own), masks)
    masks_out[...] = masks
    edge_own, edge_other = own_edge[...], received[PAD:].astype(F32)[:CHUNK]
    sign = jnp.where(flags[0] == 1, 1.0, -1.0)
    at_own = pl.multiple_of(PAD * (1 - flags[0]), 16)
    at_other = pl.multiple_of(PAD * flags[0], 16)
    for part in range(PAD // PART):
        span = rows_of(part, PART)
        mine, theirs = own[span], received[span].astype(F32)
        new_own = stream_part(
            part, sign, mine, theirs, straight[span].astype(F32), edge_own, masks, open_own, factors
        )
        new_other = stream_part(
            part, -sign, theirs, mine, turned[span].astype(F32), edge_other, masks, open_other, factors
        )
        lowered[pl.ds(at_own + PART * part, PART)] = new_own.astype(BF16)
        lowered[pl.ds(at_other + PART * part, PART)] = new_other.astype(BF16)


def streamed(flags, near, far, sibling, neighbour, edges, masks, factors):
    values = masks[...]
    edge_near, edge_far = (edges[rows_of(i, EDGE)].astype(F32)[:CHUNK] for i in range(2))
    sign_near, sign_far = signs(flags)
    start = pl.multiple_of(PAD * flags[1], 16)
    for part in range(PAD // PART):
        span = rows_of(part, PART)
        rows_near, rows_far = near[span], far[span]
        layer = sibling[pl.ds(start + PART * part, PART)].astype(F32)
        new_near = stream_part(
            part, sign_near, rows_near, rows_far, layer, edge_near, values, values[5:6], factors
        )
        layer = neighbour[span].astype(F32)
        new_far = stream_part(
            part, sign_far, rows_far, rows_near, layer, edge_far, values, values[6:7], factors
        )
        yield part, span, new_near, new_far


def between_kernel(flags, near, far, sibling, neighbour, edges, masks, factors, *outs):
    packed = (jnp.zeros((CHUNK, LANES), F32),) * 2
    for part, span, new_near, new_far in streamed(
        flags, near, far, sibling, neighbour, edges, masks, factors
    ):
        packed = give_rows(flags, part, new_near, new_far, factors, packed, outs[:4])
    outs[4][:EDGE], outs[4][EDGE:] = edge_block(packed[0]), edge_block(packed[1])


def lower_kernel(flags, near, far, sibling, neighbour, edges, masks, factors, lowered):
    at_near, at_far = place_of_near(flags)
    for part, span, new_near, new_far in streamed(
        flags, near, far, sibling, neighbour, edges, masks, factors
    ):
        lowered[pl.ds(at_near + PART * part, PART)] = new_near.astype(BF16)
        lowered[pl.ds(at_far + PART * part, PART)] = new_far.astype(BF16)


def last_kernel(given, flags, near, far, sibling, neighbour, edges, masks, factors, out):
    same = (flags[4] == 1) != given
    values = masks[...]
    edge_near, edge_far = (edges[rows_of(i, EDGE)].astype(F32)[:CHUNK] for i in range(2))
    edge, open_x = jnp.where(same, edge_near, edge_far), jnp.where(same, values[5:6], values[6:7])
    sign = jnp.where((flags[0] == 1) != given, 1.0, -1.0)
    start = pl.multiple_of(PAD * flags[1], 16)
    results = []
    for part in range(PAD // PART):
        span = rows_of(part, PART)
        rows_near, rows_far = near[span], far[span]
        layer_near = sibling[pl.ds(start + PART * part, PART)].astype(F32)
        layer = jnp.where(same, layer_near, neighbour[span].astype(F32))
        rows, mirror = jnp.where(same, rows_near, rows_far), jnp.where(same, rows_far, rows_near)
        results.append(stream_part(part, sign, rows, mirror, layer, edge, values, open_x, factors))
    results = jnp.concatenate(results, axis=0)
    if given:
        out[...] = results.astype(BF16)
    else:
        out[...] = reordered(order_matrix(flags[0] == 1), results)


def dot(left, right):
    return jnp.dot(left, right, preferred_element_type=F32)


AHEAD = 8


def in_turn(copies):
    for copy in copies[:AHEAD]:
        copy.start()
    waited = iter(range(len(copies)))

    def wait():
        index = next(waited)
        copies[index].wait()
        if index + AHEAD < len(copies):
            copies[index + AHEAD].start()

    return wait


def collide_kernel(flags, lowered, other, m0, m1, m2, m3, rows_out):
    swapped = flags[2] == 1
    first = jnp.where(swapped, other[...], lowered[...])
    second = jnp.where(swapped, lowered[...], other[...])
    values = first[:PAD], first[PAD:], second[:PAD], second[PAD:]
    for part in range(PAD // PART):
        span = rows_of(part, PART)
        rows_out[span] = sum(dot(m[span], v) for m, v in zip((m0, m1, m2, m3), values))


def give_rows(flags, part, rows_near, rows_far, factors, packed, outs):
    near, far, to_other_core, to_neighbour_chip = outs
    span = rows_of(part, PART)
    near[span], far[span] = rows_near, rows_far
    to_neighbour_chip[span] = rows_near.astype(BF16)
    to_other_core[span] = rows_far.astype(BF16)
    sign_near, sign_far = signs(flags)
    return (
        pack_part(packed[0], part, sign_near, rows_near, factors),
        pack_part(packed[1], part, sign_far, rows_far, factors),
    )


def give_product(flags, part, own, partner, factors, packed, outs):
    same = flags[4] == 1
    near, far = jnp.where(same, own, partner), jnp.where(same, partner, own)
    return give_rows(flags, part, near, far, factors, packed, outs)


def collide_partner_kernel(flags, own, lowered, other, factors, matrix, *refs):
    *outs, held, done = refs
    parts = PAD // PART
    order = [parts * half + part for part in range(parts) for half in range(2)]
    wait = in_turn(
        [
            pltpu.make_async_copy(matrix.at[rows_of(i, PART)], held.at[rows_of(i, PART)], done.at[i])
            for i in order
        ]
    )
    swapped = flags[2] == 1
    first = jnp.where(swapped, other[...], lowered[...])
    second = jnp.where(swapped, lowered[...], other[...])
    packed = (jnp.zeros((CHUNK, LANES), F32),) * 2
    for part in range(parts):
        span = rows_of(part, PART)
        wait()
        partner = dot(held[span], first)
        wait()
        partner += dot(held[rows_of(parts + part, PART)], second)
        packed = give_product(flags, part, own[span], partner, factors, packed, outs[:4])
    outs[4][:EDGE], outs[4][EDGE:] = edge_block(packed[0]), edge_block(packed[1])


def early_kernel(
    flags, lowered, m0, m1, m2, m3, matrix, own_out, partner_out, next_own, next_partner,
    held_own, held_partner, done,
):
    values = lowered[...]
    parts = m0, m1, m2, m3
    for half in range(2):

        @pl.when(flags[2] == half)
        def _():
            copies = [
                pltpu.make_async_copy(
                    matrix.at[rows_of(half, PAD)], held_partner, done.at[0]
                )
            ]
            for i in range(2):
                copies.append(pltpu.make_async_copy(parts[2 * half + i], held_own.at[i], done.at[1 + i]))
            copies.append(
                pltpu.make_async_copy(matrix.at[rows_of(1 - half, PAD)], next_partner, done.at[3])
            )
            for i in range(2):
                source = parts[2 * (1 - half) + i]
                copies.append(pltpu.make_async_copy(source, next_own.at[i], done.at[4 + i]))
            wait = in_turn(copies)
            wait()
            for part in range(PAD // PART):
                span = rows_of(part, PART)
                partner_out[span] = dot(held_partner[span], values)
            wait()
            wait()
            for part in range(PAD // PART):
                span = rows_of(part, PART)
                own_out[span] = dot(held_own[0, span], values[:PAD]) + dot(held_own[1, span], values[PAD:])
            for _ in range(3):
                wait()


def late_kernel(flags, other, own, partner, factors, matrix_own, matrix_partner, *outs):
    values = other[...]
    packed = (jnp.zeros((CHUNK, LANES), F32),) * 2
    for part in range(PAD // PART):
        span = rows_of(part, PART)
        more_own = dot(matrix_own[0, span], values[:PAD]) + dot(matrix_own[1, span], values[PAD:])
        more_partner = dot(matrix_partner[span], values)
        packed = give_product(
            flags, part, own[span] + more_own, partner[span] + more_partner, factors, packed, outs[:4]
        )
    outs[4][:EDGE], outs[4][EDGE:] = edge_block(packed[0]), edge_block(packed[1])


ROWS_F32 = ((PAD, LANES), F32)
PARTNER_SCRATCH = [pltpu.VMEM((2 * PAD, 2 * PAD), BF16), pltpu.SemaphoreType.DMA((8,))]
HELD = [pltpu.VMEM((2, PAD, PAD), BF16), pltpu.VMEM((PAD, 2 * PAD), BF16)]
EARLY = [ROWS_F32, ROWS_F32, ((2, PAD, PAD), BF16), ((PAD, 2 * PAD), BF16)]
EARLY_SCRATCH = HELD + [pltpu.SemaphoreType.DMA((6,))]


def finish_kernel(flags, kept, received, evolved):
    order = order_matrix(flags[0] == 1)
    rest = jnp.dot(order, received[...], preferred_element_type=F32)
    mine = kept[...]
    half = flags[3]
    evolved[:, 0, :LANES] = jnp.where(half == 0, mine, rest)[:ROWS]
    evolved[:, 0, LANES:] = jnp.where(half == 0, rest, mine)[:ROWS]


def place(rows, columns, wanted):
    return (lax.broadcasted_iota(jnp.int32, (rows, columns), 0) == wanted[None, :]).astype(BF16)


def chosen(left, right):
    return jnp.dot(left, right, preferred_element_type=BF16)


def column_half(wide, block):
    column = lax.iota(jnp.int32, PAD)
    inside = column < ROWS
    start_a, start_b = 640 * block, jnp.where(block == 1, 1280, 2048)
    part_a = lax.dynamic_slice(wide, (0, start_a), (wide.shape[0], 768))
    part_b = lax.dynamic_slice(wide, (0, start_b), (wide.shape[0], 896))
    wanted_a = jnp.where(inside, ROWS * block + column - start_a, -1)
    wanted_b = jnp.where(inside, 4 * ROWS - 1 - ROWS * block - column - start_b, -1)
    halves = chosen(part_a, place(768, PAD, wanted_a)), chosen(part_b, place(896, PAD, wanted_b))
    return halves


def padded_columns(matrix):
    return jnp.pad(matrix, ((0, 0), (0, 2944 - matrix.shape[1])))


def per_device(populations, solid_mask, collision):
    cell, vel = lax.axis_index("cells"), lax.axis_index("vel")
    low = (vel < 2).astype(jnp.int32)
    core, ring_place = cell % 2, cell // 32 + 4 * (cell // 2 % 2)
    block = jnp.minimum(vel, 3 - vel)
    half = (1 - low) ^ (cell // RING % 2)
    needing = (cell + 1 - 2 * low) % 128
    straight_half = (1 - low) ^ (needing // RING % 2)
    same = (low != core).astype(jnp.int32)
    flags = jnp.stack([low, 1 - core, block, half, same, straight_half])
    flags = flags.astype(jnp.int32)

    first_row = CHUNK * ring_place
    row = first_row + lax.iota(jnp.int32, CHUNK)
    start = jnp.clip(jnp.where(low == 1, first_row, ROWS - CHUNK - first_row), 0, ROWS - CHUNK)
    wanted = jnp.where(row < ROWS, jnp.where(low == 1, row, ROWS - 1 - row) - start, -1)
    window = lax.dynamic_slice(collision, (start, 0), (CHUNK, collision.shape[1]))
    window = padded_columns(chosen(place(CHUNK, CHUNK, wanted).T, window))
    piece = jnp.concatenate(column_half(window, core), axis=1)
    populations, piece = lax.optimization_barrier((populations, piece))
    piece = to_mirror(piece)

    padded = jnp.pad(populations[:, 0, :], ((0, PAD - ROWS), (0, 0)))
    rows = (PAD, LANES)
    own, own_edge, message, straight, turned, masks, factors = call(
        prepare_kernel,
        [(rows, F32), ((CHUNK, LANES), F32), ((PAD + EDGE, LANES), BF16),
         ((PAD + 16, LANES), BF16), ((PAD + 16, LANES), BF16), ((8, LANES), F32), ((3, *rows), F32)],
        flags, padded, solid_mask, flops=2 * 3 * PAD * PAD * 256,
    )
    piece, _ = lax.optimization_barrier((piece, message))
    groups = [
        [x * 32 + y * 16 + 4 * pair + 2 * odd + side for side in range(2) for odd in range(2) for x in range(4)]
        for y in range(2)
        for pair in range(4)
    ]
    partner_matrix = lax.all_gather(piece, "cells", axis=0, tiled=True, axis_index_groups=groups)
    straight, turned = to_layer(straight, False), to_layer(turned, True)
    received = to_mirror(message)

    row = lax.iota(jnp.int32, PAD)
    wanted = jnp.where(row < ROWS, jnp.where(low == 1, row, ROWS - 1 - row), -1)
    received, collision = lax.optimization_barrier((received, collision))
    ordered = padded_columns(chosen(place(ROWS, PAD, wanted).T, collision))

    lowered, masks = call(
        first_kernel,
        [((2 * PAD, LANES), BF16), ((8, LANES), F32)],
        flags, own, own_edge, received, straight, turned, masks, factors, flops=100 * PAD * 256,
    )
    lowered, ordered = lax.optimization_barrier((lowered, ordered))
    matrix = *column_half(ordered, 0), *column_half(ordered, 1)
    edges_shape = ((2 * EDGE, LANES), BF16)
    sends = [(rows, F32)] * 2 + [(rows, BF16)] * 2 + [edges_shape]
    multiply = 2 * PAD * 4 * PAD * LANES
    work = 100 * PAD * LANES

    other = to_side(lowered)
    (own,) = call(
        collide_kernel, [(rows, F32)], flags, lowered, other, *matrix, flops=multiply
    )
    partner_matrix, own = lax.optimization_barrier((partner_matrix, own))
    near, far, for_sibling, for_neighbour, edges = call(
        collide_partner_kernel, sends, flags, own, lowered, other, factors, partner_matrix,
        flops=multiply, stay=1, scratch=PARTNER_SCRATCH,
    )
    for step in range(1, STEPS):
        neighbour, edges = to_neighbour(for_neighbour), to_mirror(edges)
        sibling = with_sibling(for_sibling)
        near, far, for_sibling, for_neighbour, edges = call(
            between_kernel, sends, flags, near, far, sibling, neighbour, edges, masks, factors, flops=work
        )
        neighbour, edges = to_neighbour(for_neighbour), to_mirror(edges)
        sibling = with_sibling(for_sibling)
        (lowered,) = call(
            lower_kernel, [((2 * PAD, LANES), BF16)],
            flags, near, far, sibling, neighbour, edges, masks, factors, flops=work,
        )
        other = to_side(lowered)
        early = call(
            early_kernel, EARLY, flags, lowered, *matrix, partner_matrix,
            flops=multiply, stay=5, scratch=EARLY_SCRATCH,
        )
        near, far, for_sibling, for_neighbour, edges = call(
            late_kernel, sends, flags, other, *early[:2], factors, *early[2:], flops=multiply
        )

    neighbour, edges = to_neighbour(for_neighbour), to_mirror(edges)
    sibling = with_sibling(for_sibling)
    last = flags, near, far, sibling, neighbour, edges, masks, factors
    (message,) = call(functools.partial(last_kernel, True), [(rows, BF16)], *last, flops=work)
    received = to_mirror(message)
    (kept,) = call(functools.partial(last_kernel, False), [(rows, F32)], *last, flops=multiply)
    (evolved,) = call(
        finish_kernel, [((ROWS, 1, 2 * LANES), F32)], flags, kept, received, flops=2 * PAD * PAD * LANES
    )
    return evolved


def solution(mesh):
    in_specs = (P("vel", "cells", None), P("cells", None), P("vel", None))
    out_specs = P("vel", "cells", None)
    return jax.shard_map(
        per_device, mesh=mesh, in_specs=in_specs, out_specs=out_specs, check_vma=False
    )
```

```python
import functools
import math

import jax
import jax.numpy as jnp
from jax import lax
from jax.experimental import pallas as pl
from jax.experimental.pallas import tpu as pltpu
from jax.sharding import PartitionSpec as P


K = 14
STEPS = 2
NZ = 16
BOTH = ("cells", "vel")
ROWS = 686
PAD = 704
CHUNK = 88
PART = 2 * CHUNK
EDGE = 96
LANES = 128
BAND = 4 * CHUNK
RING = 16
F32 = jnp.float32
BF16 = jnp.bfloat16
PARAMS = pltpu.CompilerParams(vmem_limit_bytes=20 * 1024 * 1024)


def pairs_of(target):
    pairs = []
    for cell in range(128):
        for part in range(4):
            to_cell, to_part = target(cell, part)
            pairs.append((cell * 4 + part, to_cell * 4 + to_part))
    return pairs


def with_sibling(array):
    groups = [[cell, cell + 1] for cell in range(0, 128, 2)]
    return lax.all_gather(array, "cells", axis=0, tiled=True, axis_index_groups=groups)


def to_layer(array, turned):
    def target(cell, part):
        return (cell - 1 if part < 2 else cell + 1) % 128, 3 - part if turned else part

    return lax.ppermute(array, BOTH, pairs_of(target))


def neighbour_of(cell, part):
    other = (cell - 1 if cell % 2 == 0 else cell + 1) % 128
    return other, part if (other // RING) % 2 == (cell // RING) % 2 else 3 - part


def to_neighbour(array):
    return lax.ppermute(array, BOTH, pairs_of(neighbour_of))


def to_mirror(array):
    return lax.ppermute(array, "vel", [(i, 3 - i) for i in range(4)])


def to_opposite(array):
    return lax.ppermute(array, "vel", [(i, i ^ 2) for i in range(4)])


def to_side(array):
    return lax.ppermute(array, "vel", [(i, i ^ 1) for i in range(4)])


def call(kernel, outs, flags, *arrays, flops=0, stay=0, scratch=()):
    moved = sum(x.size * x.dtype.itemsize for x in arrays)
    moved += sum(math.prod(shape) * jnp.dtype(dtype).itemsize for shape, dtype in outs)
    vmem, hbm = (pl.BlockSpec(memory_space=space) for space in (pltpu.VMEM, pltpu.HBM))
    count = len(arrays) - stay
    specs = [vmem] * count + [hbm] * stay
    arrays = *arrays[:count], *(pltpu.with_memory_space_constraint(x, pltpu.HBM) for x in arrays[count:])
    return pl.pallas_call(
        kernel,
        out_shape=[jax.ShapeDtypeStruct(shape, dtype) for shape, dtype in outs],
        in_specs=[pl.BlockSpec(memory_space=pltpu.SMEM)] + specs,
        out_specs=[vmem] * len(outs),
        scratch_shapes=scratch,
        compiler_params=PARAMS,
        cost_estimate=pl.CostEstimate(flops=flops, bytes_accessed=moved, transcendentals=0),
    )(flags, *arrays)


def roll(values, shift):
    return pltpu.roll(values, shift % values.shape[1], 1)


def order_matrix(low):
    row = lax.broadcasted_iota(jnp.int32, (PAD, PAD), 0)
    column = lax.broadcasted_iota(jnp.int32, (PAD, PAD), 1)
    wanted = jnp.where(low, row, ROWS - 1 - row)
    return jnp.where((column == wanted) & (row < ROWS), 1.0, 0.0).astype(BF16)


def reordered(order, values):
    total = jnp.zeros(values.shape, F32)
    for _ in range(3):
        part = values.astype(BF16)
        total += jnp.dot(order, part, preferred_element_type=F32)
        values = values - part.astype(F32)
    return total


def signed_factors(block, chunk):
    row = CHUNK * chunk + lax.broadcasted_iota(jnp.int32, (CHUNK, LANES), 0)
    ids = ROWS * block + row
    upper = (ids * 4682) >> 16
    k_z = ids - K * upper
    k_x = (upper * 4682) >> 16
    k_y = upper - K * k_x
    centre = (K - 1) / 2.0
    x, y, z = ((k.astype(F32) - centre) * (0.3 / centre) for k in (k_x, k_y, k_z))
    return jnp.abs(x), y, z


def lanes_of(rows):
    return lax.broadcasted_iota(jnp.int32, (rows, LANES), 1)


def lower_z(values):
    z_place = lax.broadcasted_iota(jnp.int32, values.shape, 1) % NZ
    return jnp.where(z_place == 0, roll(values, 1 - NZ), roll(values, 1))


def upper_z(values):
    z_place = lax.broadcasted_iota(jnp.int32, values.shape, 1) % NZ
    return jnp.where(z_place == NZ - 1, roll(values, NZ - 1), roll(values, -1))


def picked(values, lanes):
    return jnp.take_along_axis(values, lanes, axis=1, mode="promise_in_bounds")


def pack_edge(packed, values, positive, chunk, lane):
    place = lane & (NZ - 1)
    edge = picked(values, jnp.where(positive, place + LANES - NZ, place))
    return jnp.where((lane >> 4) == chunk, edge, packed)


def edge_block(packed):
    return jnp.concatenate([packed, jnp.zeros((EDGE - CHUNK, LANES), F32)], axis=0).astype(BF16)


def prepare_kernel(
    flags, populations, solid, own, own_edge, message, straight, turned, masks, factors
):
    low, block, half = flags[0] == 1, flags[2], flags[3]
    ordered = reordered(order_matrix(low), populations[...])
    left, right = ordered[:, :LANES], ordered[:, LANES:]
    mine = jnp.where(half == 0, left, right)
    rest = jnp.where(half == 0, right, left)
    own[...] = mine
    edges = jnp.zeros((CHUNK, LANES), F32)
    sent = jnp.zeros((CHUNK, LANES), F32)
    lane = lanes_of(CHUNK)
    for chunk in range(PAD // CHUNK):
        rows = slice(CHUNK * chunk, CHUNK * (chunk + 1))
        x, y, z = signed_factors(block, chunk)
        factors[0, rows], factors[1, rows], factors[2, rows] = x, y, z
        positive = jnp.where(low, y, -y) > 0
        edges = pack_edge(edges, rest[rows], positive, chunk, lane)
        sent = pack_edge(sent, mine[rows], positive, chunk, lane)
    own_edge[...] = edges
    message[:PAD] = rest.astype(BF16)
    message[PAD:] = edge_block(sent)
    fluid = jnp.where(jnp.broadcast_to(solid[...], (8, 2 * LANES)) == 0, 1.0, 0.0)
    place = lax.broadcasted_iota(jnp.int32, (8, 2 * LANES), 0)
    found = jnp.zeros((8, 2 * LANES), F32)
    near = (fluid, roll(fluid, NZ), roll(fluid, -NZ), lower_z(fluid), upper_z(fluid))
    for index, value in enumerate(near):
        found = jnp.where(place == index, value, found)
    masks[...] = jnp.where(half == 0, found[:, :LANES], found[:, LANES:])
    row = lax.broadcasted_iota(jnp.int32, (16, LANES), 0)
    halves = []
    for side in range(2):
        cells = slice(LANES * side, LANES * (side + 1))
        open_cells = jnp.where(row == 0, jnp.broadcast_to(fluid[:1, cells], (16, LANES)), 0.0)
        halves.append((ordered[:, cells].astype(BF16), open_cells.astype(BF16)))
    for place, target in ((flags[5], straight), (1 - flags[5], turned)):
        for rows, low_value, high_value in zip((slice(0, PAD), slice(PAD, PAD + 16)), *halves):
            target[rows] = jnp.where(place == 0, low_value, high_value)


def rows_of(index, size):
    return slice(size * index, size * (index + 1))


def stream_part(part, sign, values, mirror, layer, edge, masks, open_x, factors):
    fluid, below_open_y, above_open_y, below_open_z, above_open_z = (
        jnp.broadcast_to(masks[i : i + 1], (CHUNK, LANES)) for i in range(5)
    )
    open_x = jnp.broadcast_to(open_x, (CHUNK, LANES))
    lane = lanes_of(CHUNK)
    z_place = lane & (NZ - 1)
    below_z = jnp.where(z_place == 0, lane + NZ - 1, lane - 1)
    above_z = jnp.where(z_place == NZ - 1, lane + 1 - NZ, lane + 1)
    below_y, above_y = (lane + LANES - NZ) & (LANES - 1), (lane + NZ) & (LANES - 1)
    results = []
    for index in range(2):
        chunk = 2 * part + index
        x, y, z = (factors[i, rows_of(chunk, CHUNK)] for i in range(3))
        up_y, up_z = y * sign > 0, z * sign > 0
        here, back = values[rows_of(index, CHUNK)], mirror[rows_of(index, CHUNK)]
        at_edge = jnp.where(up_y, lane, lane + NZ)
        put = picked(edge, (at_edge + NZ * chunk) & (LANES - 1))
        outside = (up_y & (lane < NZ)) | (~up_y & (lane >= LANES - NZ))
        near_y = jnp.where(outside, put, picked(here, jnp.where(up_y, below_y, above_y)))
        near_z = picked(here, jnp.where(up_z, below_z, above_z))
        upwind_x = jnp.where(open_x > 0, layer[rows_of(index, CHUNK)], back)
        upwind_y = jnp.where(jnp.where(up_y, below_open_y, above_open_y) > 0, near_y, back)
        upwind_z = jnp.where(jnp.where(up_z, below_open_z, above_open_z) > 0, near_z, back)
        outflow = x * (here - upwind_x)
        outflow += jnp.abs(y) * (here - upwind_y)
        outflow += jnp.abs(z) * (here - upwind_z)
        results.append((here - outflow) * fluid)
    return jnp.concatenate(results, axis=0)


def pack_part(packed, part, sign, values, factors):
    lane = lanes_of(CHUNK)
    for index in range(2):
        chunk = 2 * part + index
        positive = factors[1, rows_of(chunk, CHUNK)] * sign > 0
        packed = pack_edge(packed, values[rows_of(index, CHUNK)], positive, chunk, lane)
    return packed


def signs(flags):
    near = jnp.where(flags[1] == 1, 1.0, -1.0)
    return near, -near


def place_of_near(flags):
    return pl.multiple_of(PAD * (1 - flags[1]), 16), pl.multiple_of(PAD * flags[1], 16)


def first_kernel(
    flags, own, own_edge, received, straight, turned, masks_in, factors, lowered, masks_out, bands
):
    same = flags[4] == 1
    place = lax.broadcasted_iota(jnp.int32, (8, LANES), 0)
    open_own = straight[PAD:].astype(F32)[:1]
    open_other = turned[PAD:].astype(F32)[:1]
    masks = masks_in[...]
    masks = jnp.where(place == 5, jnp.where(same, open_own, open_other), masks)
    masks = jnp.where(place == 6, jnp.where(same, open_other, open_own), masks)
    masks_out[...] = masks
    edge_own, edge_other = own_edge[...], received[PAD:].astype(F32)[:CHUNK]
    sign = jnp.where(flags[0] == 1, 1.0, -1.0)
    low = flags[0] == 1
    group = lanes_of(PART) >> 5
    packed = [jnp.zeros((PART, LANES), F32)] * 2
    for part in range(PAD // PART):
        span = rows_of(part, PART)
        mine, theirs = own[span], received[span].astype(F32)
        new_own = stream_part(
            part, sign, mine, theirs, straight[span].astype(F32), edge_own, masks, open_own, factors
        )
        new_other = stream_part(
            part, -sign, theirs, mine, turned[span].astype(F32), edge_other, masks, open_other, factors
        )
        rows_a, rows_b = jnp.where(low, new_own, new_other), jnp.where(low, new_other, new_own)
        for index, rows in enumerate((rows_a, rows_b)):
            lowered[PAD * index + PART * part : PAD * index + PART * (part + 1)] = rows.astype(BF16)
            place = 2 * index + part // 2
            edge = roll(rows, NZ + 2 * NZ * place)
            packed[part % 2] = jnp.where(group == place, edge, packed[part % 2])
    for index in range(2):
        bands[rows_of(index, PART)] = packed[index].astype(BF16)


def streamed(flags, near, far, sibling, neighbour, edges, masks, factors):
    values = masks[...]
    edge_near, edge_far = (edges[rows_of(i, EDGE)].astype(F32)[:CHUNK] for i in range(2))
    sign_near, sign_far = signs(flags)
    start = pl.multiple_of(PAD * flags[1], 16)
    for part in range(PAD // PART):
        span = rows_of(part, PART)
        rows_near, rows_far = near[span], far[span]
        layer = sibling[pl.ds(start + PART * part, PART)].astype(F32)
        new_near = stream_part(
            part, sign_near, rows_near, rows_far, layer, edge_near, values, values[5:6], factors
        )
        layer = neighbour[span].astype(F32)
        new_far = stream_part(
            part, sign_far, rows_far, rows_near, layer, edge_far, values, values[6:7], factors
        )
        yield part, span, new_near, new_far


def between_near_kernel(flags, near, far, sibling, edges, masks, factors, rows_out, sent, packed_out):
    values = masks[...]
    sign = signs(flags)[0]
    start = pl.multiple_of(PAD * flags[1], 16)
    edge = edges[:EDGE].astype(F32)[:CHUNK]
    packed = jnp.zeros((CHUNK, LANES), F32)
    for part in range(PAD // PART):
        span = rows_of(part, PART)
        layer = sibling[pl.ds(start + PART * part, PART)].astype(F32)
        rows = stream_part(
            part, sign, near[span], far[span], layer, edge, values, values[5:6], factors
        )
        rows_out[span] = rows
        sent[span] = rows.astype(BF16)
        packed = pack_part(packed, part, sign, rows, factors)
    packed_out[...] = edge_block(packed)


def between_far_kernel(
    flags, near, far, neighbour, edges, masks, factors, packed_near, rows_out, sent, packed_out
):
    values = masks[...]
    sign = signs(flags)[1]
    edge = edges[EDGE:].astype(F32)[:CHUNK]
    packed = jnp.zeros((CHUNK, LANES), F32)
    for part in range(PAD // PART):
        span = rows_of(part, PART)
        layer = neighbour[span].astype(F32)
        rows = stream_part(
            part, sign, far[span], near[span], layer, edge, values, values[6:7], factors
        )
        rows_out[span] = rows
        sent[span] = rows.astype(BF16)
        packed = pack_part(packed, part, sign, rows, factors)
    packed_out[:EDGE] = packed_near[...]
    packed_out[EDGE:] = edge_block(packed)


def lower_kernel(flags, near, far, sibling, neighbour, edges, masks, factors, lowered):
    at_near, at_far = place_of_near(flags)
    for part, span, new_near, new_far in streamed(
        flags, near, far, sibling, neighbour, edges, masks, factors
    ):
        lowered[pl.ds(at_near + PART * part, PART)] = new_near.astype(BF16)
        lowered[pl.ds(at_far + PART * part, PART)] = new_far.astype(BF16)


def last_kernel(given, flags, near, far, sibling, neighbour, edges, masks, factors, out):
    same = (flags[4] == 1) != given
    values = masks[...]
    edge_near, edge_far = (edges[rows_of(i, EDGE)].astype(F32)[:CHUNK] for i in range(2))
    edge, open_x = jnp.where(same, edge_near, edge_far), jnp.where(same, values[5:6], values[6:7])
    sign = jnp.where((flags[0] == 1) != given, 1.0, -1.0)
    start = pl.multiple_of(PAD * flags[1], 16)
    results = []
    for part in range(PAD // PART):
        span = rows_of(part, PART)
        rows_near, rows_far = near[span], far[span]
        layer_near = sibling[pl.ds(start + PART * part, PART)].astype(F32)
        layer = jnp.where(same, layer_near, neighbour[span].astype(F32))
        rows, mirror = jnp.where(same, rows_near, rows_far), jnp.where(same, rows_far, rows_near)
        results.append(stream_part(part, sign, rows, mirror, layer, edge, values, open_x, factors))
    results = jnp.concatenate(results, axis=0)
    if given:
        out[...] = results.astype(BF16)
    else:
        out[...] = reordered(order_matrix(flags[0] == 1), results)


def dot(left, right):
    return jnp.dot(left, right, preferred_element_type=F32)


def pack_other(packed, part, sign, values, factors):
    lane = lanes_of(CHUNK)
    place = lane & (NZ - 1)
    for index in range(2):
        chunk = 2 * part + index
        positive = factors[1, rows_of(chunk, CHUNK)] * sign > 0
        edge = picked(values[rows_of(index, CHUNK)], jnp.where(positive, place, place + NZ))
        packed = jnp.where((lane >> 4) == chunk, edge, packed)
    return packed


def unpacked(bands):
    values = bands.astype(F32)
    return jnp.concatenate([roll(values, -2 * NZ * group) for group in range(4)], axis=0).astype(BF16)


def collide_kernel(
    flags, lowered, other, bands, other_bands, factors, m0, m1, m2, m3, rows_out, packed_out, all_rows, all_bands
):
    swapped = flags[2] == 1
    for index, right in enumerate((swapped, ~swapped)):
        all_rows[rows_of(index, 2 * PAD)] = jnp.where(right, other[...], lowered[...])
        all_bands[rows_of(index, BAND)] = jnp.where(right, other_bands[...], bands[...])
    values = []
    for index in range(2):
        rows, band = all_rows[rows_of(index, 2 * PAD)], unpacked(all_bands[rows_of(index, BAND)])
        for side in range(2):
            span = rows_of(side, PAD)
            values.append(jnp.concatenate([rows[span], band[span]], axis=1))
    sign = jnp.where(flags[0] == 1, 1.0, -1.0)
    packed = jnp.zeros((CHUNK, LANES), F32)
    for part in range(PAD // PART):
        span = rows_of(part, PART)
        total = sum(dot(m[span], v) for m, v in zip((m0, m1, m2, m3), values))
        rows_out[span] = total[:, :LANES]
        packed = pack_other(packed, part, sign, total[:, LANES:], factors)
    packed_out[...] = edge_block(packed)


def give_rows(flags, part, rows_near, rows_far, factors, packed, outs):
    near, far, to_other_core, to_neighbour_chip = outs
    span = rows_of(part, PART)
    near[span], far[span] = rows_near, rows_far
    to_neighbour_chip[span] = rows_near.astype(BF16)
    to_other_core[span] = rows_far.astype(BF16)
    sign_near, sign_far = signs(flags)
    return (
        pack_part(packed[0], part, sign_near, rows_near, factors),
        pack_part(packed[1], part, sign_far, rows_far, factors),
    )


def give_product(flags, part, own, partner, factors, packed, outs):
    same = flags[4] == 1
    near, far = jnp.where(same, own, partner), jnp.where(same, partner, own)
    return give_rows(flags, part, near, far, factors, packed, outs)


def collide_partner_kernel(
    flags, own_packed, factors, all_rows, all_bands, own, matrix,
    near, far, for_sibling, for_neighbour, edges,
    held, held_rows, held_bands, held_own, done,
):
    small = [
        pltpu.make_async_copy(source, target, done.at[index])
        for index, (source, target) in enumerate(
            ((all_rows, held_rows), (all_bands, held_bands), (own, held_own))
        )
    ]
    parts = PAD // PART
    pieces = [
        [
            pltpu.make_async_copy(
                matrix.at[rows_of(parts * half + part, PART)],
                held.at[rows_of(parts * half + part, PART)],
                done.at[3 + parts * half + part],
            )
            for half in range(2)
        ]
        for part in range(parts)
    ]
    for copy in small + sum(pieces, []):
        copy.start()
    for copy in small:
        copy.wait()
    low, same = flags[0] == 1, flags[4] == 1
    values = []
    for index in range(2):
        band = unpacked(held_bands[rows_of(index, BAND)])
        values.append(jnp.concatenate([held_rows[rows_of(index, 2 * PAD)], band], axis=1))
    sign = jnp.where(low, -1.0, 1.0)
    packed = jnp.zeros((CHUNK, LANES), F32)
    for part in range(parts):
        span = rows_of(part, PART)
        total = 0.0
        for half in range(2):
            pieces[part][half].wait()
            total += dot(held[rows_of(parts * half + part, PART)], values[half])
        mine, theirs = held_own[span], total[:, :LANES]
        rows_near, rows_far = jnp.where(same, mine, theirs), jnp.where(same, theirs, mine)
        near[span], far[span] = rows_near, rows_far
        for_neighbour[span] = rows_near.astype(BF16)
        for_sibling[span] = rows_far.astype(BF16)
        packed = pack_other(packed, part, sign, total[:, LANES:], factors)
    mine, theirs = own_packed[...], edge_block(packed)
    edges[:EDGE] = jnp.where(same, mine, theirs)
    edges[EDGE:] = jnp.where(same, theirs, mine)


def early_kernel(
    flags, lowered, m0, m1, m2, m3, matrix, own_out, partner_out, next_own, next_partner,
    held_own, held_partner, done,
):
    values = lowered[...]
    parts = m0, m1, m2, m3
    for half in range(2):

        @pl.when(flags[2] == half)
        def _():
            copies = [
                pltpu.make_async_copy(
                    matrix.at[rows_of(half, PAD)], held_partner, done.at[0]
                )
            ]
            for i in range(2):
                copies.append(pltpu.make_async_copy(parts[2 * half + i], held_own.at[i], done.at[1 + i]))
            copies.append(
                pltpu.make_async_copy(matrix.at[rows_of(1 - half, PAD)], next_partner, done.at[3])
            )
            for i in range(2):
                source = parts[2 * (1 - half) + i]
                copies.append(pltpu.make_async_copy(source, next_own.at[i], done.at[4 + i]))
            for copy in copies:
                copy.start()
            copies[0].wait()
            for part in range(PAD // PART):
                span = rows_of(part, PART)
                partner_out[span] = dot(held_partner[span], values)
            copies[1].wait()
            copies[2].wait()
            for part in range(PAD // PART):
                span = rows_of(part, PART)
                own_out[span] = dot(held_own[0, span], values[:PAD]) + dot(held_own[1, span], values[PAD:])
            for copy in copies[3:]:
                copy.wait()


def late_kernel(flags, other, own, partner, factors, matrix_own, matrix_partner, *outs):
    values = other[...]
    packed = (jnp.zeros((CHUNK, LANES), F32),) * 2
    for part in range(PAD // PART):
        span = rows_of(part, PART)
        more_own = dot(matrix_own[0, span], values[:PAD]) + dot(matrix_own[1, span], values[PAD:])
        more_partner = dot(matrix_partner[span], values)
        packed = give_product(
            flags, part, own[span] + more_own, partner[span] + more_partner, factors, packed, outs[:4]
        )
    outs[4][:EDGE], outs[4][EDGE:] = edge_block(packed[0]), edge_block(packed[1])


ROWS_F32 = ((PAD, LANES), F32)
PARTNER_SCRATCH = [
    pltpu.VMEM((2 * PAD, 2 * PAD), BF16),
    pltpu.VMEM((4 * PAD, LANES), BF16),
    pltpu.VMEM((2 * BAND, LANES), BF16),
    pltpu.VMEM((PAD, LANES), F32),
    pltpu.SemaphoreType.DMA((11,)),
]
HELD = [pltpu.VMEM((2, PAD, PAD), BF16), pltpu.VMEM((PAD, 2 * PAD), BF16)]
EARLY = [ROWS_F32, ROWS_F32, ((2, PAD, PAD), BF16), ((PAD, 2 * PAD), BF16)]
EARLY_SCRATCH = HELD + [pltpu.SemaphoreType.DMA((6,))]


def finish_kernel(flags, kept, received, evolved):
    order = order_matrix(flags[0] == 1)
    rest = jnp.dot(order, received[...], preferred_element_type=F32)
    mine = kept[...]
    half = flags[3]
    evolved[:, 0, :LANES] = jnp.where(half == 0, mine, rest)[:ROWS]
    evolved[:, 0, LANES:] = jnp.where(half == 0, rest, mine)[:ROWS]


def place(rows, columns, wanted):
    return (lax.broadcasted_iota(jnp.int32, (rows, columns), 0) == wanted[None, :]).astype(BF16)


def chosen(left, right):
    return jnp.dot(left, right, preferred_element_type=BF16)


def column_half(wide, block):
    column = lax.iota(jnp.int32, PAD)
    inside = column < ROWS
    start_a, start_b = 640 * block, jnp.where(block == 1, 1280, 2048)
    part_a = lax.dynamic_slice(wide, (0, start_a), (wide.shape[0], 768))
    part_b = lax.dynamic_slice(wide, (0, start_b), (wide.shape[0], 896))
    wanted_a = jnp.where(inside, ROWS * block + column - start_a, -1)
    wanted_b = jnp.where(inside, 4 * ROWS - 1 - ROWS * block - column - start_b, -1)
    halves = chosen(part_a, place(768, PAD, wanted_a)), chosen(part_b, place(896, PAD, wanted_b))
    return halves


def padded_columns(matrix):
    return jnp.pad(matrix, ((0, 0), (0, 2944 - matrix.shape[1])))


def per_device(populations, solid_mask, collision):
    cell, vel = lax.axis_index("cells"), lax.axis_index("vel")
    low = (vel < 2).astype(jnp.int32)
    core, ring_place = cell % 2, cell // 32 + 4 * (cell // 2 % 2)
    block = jnp.minimum(vel, 3 - vel)
    half = (1 - low) ^ (cell // RING % 2)
    needing = (cell + 1 - 2 * low) % 128
    straight_half = (1 - low) ^ (needing // RING % 2)
    same = (low != core).astype(jnp.int32)
    flags = jnp.stack([low, 1 - core, block, half, same, straight_half])
    flags = flags.astype(jnp.int32)

    first_row = CHUNK * ring_place
    row = first_row + lax.iota(jnp.int32, CHUNK)
    start = jnp.clip(jnp.where(low == 1, first_row, ROWS - CHUNK - first_row), 0, ROWS - CHUNK)
    wanted = jnp.where(row < ROWS, jnp.where(low == 1, row, ROWS - 1 - row) - start, -1)
    window = lax.dynamic_slice(collision, (start, 0), (CHUNK, collision.shape[1]))
    window = padded_columns(chosen(place(CHUNK, CHUNK, wanted).T, window))
    piece = jnp.concatenate(column_half(window, core), axis=1)
    populations, piece = lax.optimization_barrier((populations, piece))
    piece = to_mirror(piece)

    padded = jnp.pad(populations[:, 0, :], ((0, PAD - ROWS), (0, 0)))
    rows = (PAD, LANES)
    own, own_edge, message, straight, turned, masks, factors = call(
        prepare_kernel,
        [(rows, F32), ((CHUNK, LANES), F32), ((PAD + EDGE, LANES), BF16),
         ((PAD + 16, LANES), BF16), ((PAD + 16, LANES), BF16), ((8, LANES), F32), ((3, *rows), F32)],
        flags, padded, solid_mask, flops=2 * 3 * PAD * PAD * 256,
    )
    piece, _ = lax.optimization_barrier((piece, message))
    groups = [
        [x * 32 + y * 16 + 4 * pair + 2 * odd + side for side in range(2) for odd in range(2) for x in range(4)]
        for y in range(2)
        for pair in range(4)
    ]
    partner_matrix = lax.all_gather(piece, "cells", axis=0, tiled=True, axis_index_groups=groups)
    straight, turned = to_layer(straight, False), to_layer(turned, True)
    received = to_mirror(message)

    row = lax.iota(jnp.int32, PAD)
    wanted = jnp.where(row < ROWS, jnp.where(low == 1, row, ROWS - 1 - row), -1)
    received, collision = lax.optimization_barrier((received, collision))
    ordered = padded_columns(chosen(place(ROWS, PAD, wanted).T, collision))

    lowered, masks, bands = call(
        first_kernel,
        [((2 * PAD, LANES), BF16), ((8, LANES), F32), ((BAND, LANES), BF16)],
        flags, own, own_edge, received, straight, turned, masks, factors, flops=100 * PAD * 256,
    )
    lowered, ordered = lax.optimization_barrier((lowered, ordered))
    matrix = *column_half(ordered, 0), *column_half(ordered, 1)
    edges_shape = ((2 * EDGE, LANES), BF16)
    sends = [(rows, F32)] * 2 + [(rows, BF16)] * 2 + [edges_shape]
    multiply = 2 * PAD * 4 * PAD * LANES
    work = 100 * PAD * LANES

    other = to_side(lowered)
    bands = to_mirror(bands), to_opposite(bands)
    own, own_packed, all_rows, all_bands = call(
        collide_kernel,
        [(rows, F32), ((EDGE, LANES), BF16), ((4 * PAD, LANES), BF16), ((2 * BAND, LANES), BF16)],
        flags, lowered, other, *bands, factors, *matrix, flops=2 * multiply,
    )
    partner_matrix, own = lax.optimization_barrier((partner_matrix, own))
    near, far, for_sibling, for_neighbour, edges = call(
        collide_partner_kernel, sends, flags, own_packed, factors, all_rows, all_bands, own, partner_matrix,
        flops=2 * multiply, stay=4, scratch=PARTNER_SCRATCH,
    )

    for step in range(1, STEPS):
        neighbour, sibling = to_neighbour(for_neighbour), with_sibling(for_sibling)
        new_near, for_neighbour, packed = call(
            between_near_kernel, [(rows, F32), (rows, BF16), ((EDGE, LANES), BF16)],
            flags, near, far, sibling, edges, masks, factors, flops=work,
        )
        new_far, for_sibling, edges = call(
            between_far_kernel, [(rows, F32), (rows, BF16), edges_shape],
            flags, near, far, neighbour, edges, masks, factors, packed, flops=work,
        )
        near, far = new_near, new_far
        neighbour, edges = to_neighbour(for_neighbour), to_mirror(edges)
        sibling = with_sibling(for_sibling)
        (lowered,) = call(
            lower_kernel, [((2 * PAD, LANES), BF16)],
            flags, near, far, sibling, neighbour, edges, masks, factors, flops=work,
        )
        other = to_side(lowered)
        early = call(
            early_kernel, EARLY, flags, lowered, *matrix, partner_matrix,
            flops=multiply, stay=5, scratch=EARLY_SCRATCH,
        )
        near, far, for_sibling, for_neighbour, edges = call(
            late_kernel, sends, flags, other, *early[:2], factors, *early[2:], flops=multiply
        )

    neighbour, edges = to_neighbour(for_neighbour), to_mirror(edges)
    sibling = with_sibling(for_sibling)
    last = flags, near, far, sibling, neighbour, edges, masks, factors
    (message,) = call(functools.partial(last_kernel, True), [(rows, BF16)], *last, flops=work)
    received = to_mirror(message)
    (kept,) = call(functools.partial(last_kernel, False), [(rows, F32)], *last, flops=multiply)
    (evolved,) = call(
        finish_kernel, [((ROWS, 1, 2 * LANES), F32)], flags, kept, received, flops=2 * PAD * PAD * LANES
    )
    return evolved


def solution(mesh):
    in_specs = (P("vel", "cells", None), P("cells", None), P("vel", None))
    out_specs = P("vel", "cells", None)
    return jax.shard_map(
        per_device, mesh=mesh, in_specs=in_specs, out_specs=out_specs, check_vma=False
    )
```

```python
import functools
import math

import jax
import jax.numpy as jnp
from jax import lax
from jax.experimental import pallas as pl
from jax.experimental.pallas import tpu as pltpu
from jax.sharding import PartitionSpec as P


K = 14
STEPS = 2
NZ = 16
BOTH = ("cells", "vel")
ROWS = 686
PAD = 704
CHUNK = 88
PART = 2 * CHUNK
EDGE = 96
LANES = 128
BAND = 4 * CHUNK
RING = 16
F32 = jnp.float32
BF16 = jnp.bfloat16
PARAMS = pltpu.CompilerParams(vmem_limit_bytes=20 * 1024 * 1024)


def pairs_of(target):
    pairs = []
    for cell in range(128):
        for part in range(4):
            to_cell, to_part = target(cell, part)
            pairs.append((cell * 4 + part, to_cell * 4 + to_part))
    return pairs


def with_sibling(array):
    groups = [[cell, cell + 1] for cell in range(0, 128, 2)]
    return lax.all_gather(array, "cells", axis=0, tiled=True, axis_index_groups=groups)


def to_layer(array, turned):
    def target(cell, part):
        return (cell - 1 if part < 2 else cell + 1) % 128, 3 - part if turned else part

    return lax.ppermute(array, BOTH, pairs_of(target))


def neighbour_of(cell, part):
    other = (cell - 1 if cell % 2 == 0 else cell + 1) % 128
    return other, part if (other // RING) % 2 == (cell // RING) % 2 else 3 - part


def to_neighbour(array):
    return lax.ppermute(array, BOTH, pairs_of(neighbour_of))


def to_mirror(array):
    return lax.ppermute(array, "vel", [(i, 3 - i) for i in range(4)])


def to_opposite(array):
    return lax.ppermute(array, "vel", [(i, i ^ 2) for i in range(4)])


def to_side(array):
    return lax.ppermute(array, "vel", [(i, i ^ 1) for i in range(4)])


def call(kernel, outs, flags, *arrays, flops=0, stay=0, scratch=(), leave=False):
    moved = sum(x.size * x.dtype.itemsize for x in arrays)
    moved += sum(math.prod(shape) * jnp.dtype(dtype).itemsize for shape, dtype in outs)
    vmem, hbm = (pl.BlockSpec(memory_space=space) for space in (pltpu.VMEM, pltpu.HBM))
    count = len(arrays) - stay
    specs = [vmem] * count + [hbm] * stay
    arrays = *arrays[:count], *(pltpu.with_memory_space_constraint(x, pltpu.HBM) for x in arrays[count:])
    return pl.pallas_call(
        kernel,
        out_shape=[(pltpu.HBM if leave else jax.ShapeDtypeStruct)(shape, dtype) for shape, dtype in outs],
        in_specs=[pl.BlockSpec(memory_space=pltpu.SMEM)] + specs,
        out_specs=[vmem] * len(outs),
        scratch_shapes=scratch,
        compiler_params=PARAMS,
        cost_estimate=pl.CostEstimate(flops=flops, bytes_accessed=moved, transcendentals=0),
    )(flags, *arrays)


def roll(values, shift):
    return pltpu.roll(values, shift % values.shape[1], 1)


def order_matrix(low):
    row = lax.broadcasted_iota(jnp.int32, (PAD, PAD), 0)
    column = lax.broadcasted_iota(jnp.int32, (PAD, PAD), 1)
    wanted = jnp.where(low, row, ROWS - 1 - row)
    return jnp.where((column == wanted) & (row < ROWS), 1.0, 0.0).astype(BF16)


def reordered(order, values):
    total = jnp.zeros(values.shape, F32)
    for _ in range(3):
        part = values.astype(BF16)
        total += jnp.dot(order, part, preferred_element_type=F32)
        values = values - part.astype(F32)
    return total


def signed_factors(block, chunk):
    row = CHUNK * chunk + lax.broadcasted_iota(jnp.int32, (CHUNK, LANES), 0)
    ids = ROWS * block + row
    upper = (ids * 4682) >> 16
    k_z = ids - K * upper
    k_x = (upper * 4682) >> 16
    k_y = upper - K * k_x
    centre = (K - 1) / 2.0
    x, y, z = ((k.astype(F32) - centre) * (0.3 / centre) for k in (k_x, k_y, k_z))
    return jnp.abs(x), y, z


def lanes_of(rows):
    return lax.broadcasted_iota(jnp.int32, (rows, LANES), 1)


def lower_z(values):
    z_place = lax.broadcasted_iota(jnp.int32, values.shape, 1) % NZ
    return jnp.where(z_place == 0, roll(values, 1 - NZ), roll(values, 1))


def upper_z(values):
    z_place = lax.broadcasted_iota(jnp.int32, values.shape, 1) % NZ
    return jnp.where(z_place == NZ - 1, roll(values, NZ - 1), roll(values, -1))


def picked(values, lanes):
    return jnp.take_along_axis(values, lanes, axis=1, mode="promise_in_bounds")


def pack_edge(packed, values, positive, chunk, lane):
    place = lane & (NZ - 1)
    edge = picked(values, jnp.where(positive, place + LANES - NZ, place))
    return jnp.where((lane >> 4) == chunk, edge, packed)


def edge_block(packed):
    return jnp.concatenate([packed, jnp.zeros((EDGE - CHUNK, LANES), F32)], axis=0).astype(BF16)


def prepare_kernel(
    flags, populations, solid, own, own_edge, message, straight, turned, masks, factors
):
    low, block, half = flags[0] == 1, flags[2], flags[3]
    ordered = reordered(order_matrix(low), populations[...])
    left, right = ordered[:, :LANES], ordered[:, LANES:]
    mine = jnp.where(half == 0, left, right)
    rest = jnp.where(half == 0, right, left)
    own[...] = mine
    edges = jnp.zeros((CHUNK, LANES), F32)
    sent = jnp.zeros((CHUNK, LANES), F32)
    lane = lanes_of(CHUNK)
    for chunk in range(PAD // CHUNK):
        rows = slice(CHUNK * chunk, CHUNK * (chunk + 1))
        x, y, z = signed_factors(block, chunk)
        factors[0, rows], factors[1, rows], factors[2, rows] = x, y, z
        positive = jnp.where(low, y, -y) > 0
        edges = pack_edge(edges, rest[rows], positive, chunk, lane)
        sent = pack_edge(sent, mine[rows], positive, chunk, lane)
    own_edge[...] = edges
    message[:PAD] = rest.astype(BF16)
    message[PAD:] = edge_block(sent)
    fluid = jnp.where(jnp.broadcast_to(solid[...], (8, 2 * LANES)) == 0, 1.0, 0.0)
    place = lax.broadcasted_iota(jnp.int32, (8, 2 * LANES), 0)
    found = jnp.zeros((8, 2 * LANES), F32)
    near = (fluid, roll(fluid, NZ), roll(fluid, -NZ), lower_z(fluid), upper_z(fluid))
    for index, value in enumerate(near):
        found = jnp.where(place == index, value, found)
    masks[...] = jnp.where(half == 0, found[:, :LANES], found[:, LANES:])
    row = lax.broadcasted_iota(jnp.int32, (16, LANES), 0)
    halves = []
    for side in range(2):
        cells = slice(LANES * side, LANES * (side + 1))
        open_cells = jnp.where(row == 0, jnp.broadcast_to(fluid[:1, cells], (16, LANES)), 0.0)
        halves.append((ordered[:, cells].astype(BF16), open_cells.astype(BF16)))
    for place, target in ((flags[5], straight), (1 - flags[5], turned)):
        for rows, low_value, high_value in zip((slice(0, PAD), slice(PAD, PAD + 16)), *halves):
            target[rows] = jnp.where(place == 0, low_value, high_value)


def rows_of(index, size):
    return slice(size * index, size * (index + 1))


def stream_part(part, sign, values, mirror, layer, edge, masks, open_x, factors):
    fluid, below_open_y, above_open_y, below_open_z, above_open_z = (
        jnp.broadcast_to(masks[i : i + 1], (CHUNK, LANES)) for i in range(5)
    )
    open_x = jnp.broadcast_to(open_x, (CHUNK, LANES))
    lane = lanes_of(CHUNK)
    z_place = lane & (NZ - 1)
    below_z = jnp.where(z_place == 0, lane + NZ - 1, lane - 1)
    above_z = jnp.where(z_place == NZ - 1, lane + 1 - NZ, lane + 1)
    below_y, above_y = (lane + LANES - NZ) & (LANES - 1), (lane + NZ) & (LANES - 1)
    results = []
    for index in range(2):
        chunk = 2 * part + index
        x, y, z = (factors[i, rows_of(chunk, CHUNK)] for i in range(3))
        up_y, up_z = y * sign > 0, z * sign > 0
        here, back = values[rows_of(index, CHUNK)], mirror[rows_of(index, CHUNK)]
        at_edge = jnp.where(up_y, lane, lane + NZ)
        put = picked(edge, (at_edge + NZ * chunk) & (LANES - 1))
        outside = (up_y & (lane < NZ)) | (~up_y & (lane >= LANES - NZ))
        near_y = jnp.where(outside, put, picked(here, jnp.where(up_y, below_y, above_y)))
        near_z = picked(here, jnp.where(up_z, below_z, above_z))
        upwind_x = jnp.where(open_x > 0, layer[rows_of(index, CHUNK)], back)
        upwind_y = jnp.where(jnp.where(up_y, below_open_y, above_open_y) > 0, near_y, back)
        upwind_z = jnp.where(jnp.where(up_z, below_open_z, above_open_z) > 0, near_z, back)
        outflow = x * (here - upwind_x)
        outflow += jnp.abs(y) * (here - upwind_y)
        outflow += jnp.abs(z) * (here - upwind_z)
        results.append((here - outflow) * fluid)
    return jnp.concatenate(results, axis=0)


def pack_part(packed, part, sign, values, factors):
    lane = lanes_of(CHUNK)
    for index in range(2):
        chunk = 2 * part + index
        positive = factors[1, rows_of(chunk, CHUNK)] * sign > 0
        packed = pack_edge(packed, values[rows_of(index, CHUNK)], positive, chunk, lane)
    return packed


def signs(flags):
    near = jnp.where(flags[1] == 1, 1.0, -1.0)
    return near, -near


def place_of_near(flags):
    return pl.multiple_of(PAD * (1 - flags[1]), 16), pl.multiple_of(PAD * flags[1], 16)


def first_kernel(
    flags, own, own_edge, received, straight, turned, masks_in, factors, lowered, masks_out, bands
):
    same = flags[4] == 1
    place = lax.broadcasted_iota(jnp.int32, (8, LANES), 0)
    open_own = straight[PAD:].astype(F32)[:1]
    open_other = turned[PAD:].astype(F32)[:1]
    masks = masks_in[...]
    masks = jnp.where(place == 5, jnp.where(same, open_own, open_other), masks)
    masks = jnp.where(place == 6, jnp.where(same, open_other, open_own), masks)
    masks_out[...] = masks
    edge_own, edge_other = own_edge[...], received[PAD:].astype(F32)[:CHUNK]
    sign = jnp.where(flags[0] == 1, 1.0, -1.0)
    low = flags[0] == 1
    group = lanes_of(PART) >> 5
    packed = [jnp.zeros((PART, LANES), F32)] * 2
    for part in range(PAD // PART):
        span = rows_of(part, PART)
        mine, theirs = own[span], received[span].astype(F32)
        new_own = stream_part(
            part, sign, mine, theirs, straight[span].astype(F32), edge_own, masks, open_own, factors
        )
        new_other = stream_part(
            part, -sign, theirs, mine, turned[span].astype(F32), edge_other, masks, open_other, factors
        )
        rows_a, rows_b = jnp.where(low, new_own, new_other), jnp.where(low, new_other, new_own)
        for index, rows in enumerate((rows_a, rows_b)):
            lowered[PAD * index + PART * part : PAD * index + PART * (part + 1)] = rows.astype(BF16)
            place = 2 * index + part // 2
            edge = roll(rows, NZ + 2 * NZ * place)
            packed[part % 2] = jnp.where(group == place, edge, packed[part % 2])
    for index in range(2):
        bands[rows_of(index, PART)] = packed[index].astype(BF16)


def streamed(flags, near, far, sibling, neighbour, edges, masks, factors):
    values = masks[...]
    edge_near, edge_far = (edges[rows_of(i, EDGE)].astype(F32)[:CHUNK] for i in range(2))
    sign_near, sign_far = signs(flags)
    start = pl.multiple_of(PAD * flags[1], 16)
    for part in range(PAD // PART):
        span = rows_of(part, PART)
        rows_near, rows_far = near[span], far[span]
        layer = sibling[pl.ds(start + PART * part, PART)].astype(F32)
        new_near = stream_part(
            part, sign_near, rows_near, rows_far, layer, edge_near, values, values[5:6], factors
        )
        layer = neighbour[span].astype(F32)
        new_far = stream_part(
            part, sign_far, rows_far, rows_near, layer, edge_far, values, values[6:7], factors
        )
        yield part, span, new_near, new_far


def between_near_kernel(flags, near, far, sibling, edges, masks, factors, rows_out, sent, packed_out):
    values = masks[...]
    sign = signs(flags)[0]
    start = pl.multiple_of(PAD * flags[1], 16)
    edge = edges[:EDGE].astype(F32)[:CHUNK]
    packed = jnp.zeros((CHUNK, LANES), F32)
    for part in range(PAD // PART):
        span = rows_of(part, PART)
        layer = sibling[pl.ds(start + PART * part, PART)].astype(F32)
        rows = stream_part(
            part, sign, near[span], far[span], layer, edge, values, values[5:6], factors
        )
        rows_out[span] = rows
        sent[span] = rows.astype(BF16)
        packed = pack_part(packed, part, sign, rows, factors)
    packed_out[...] = edge_block(packed)


def between_far_kernel(
    flags, near, far, neighbour, edges, masks, factors, packed_near, rows_out, sent, packed_out
):
    values = masks[...]
    sign = signs(flags)[1]
    edge = edges[EDGE:].astype(F32)[:CHUNK]
    packed = jnp.zeros((CHUNK, LANES), F32)
    for part in range(PAD // PART):
        span = rows_of(part, PART)
        layer = neighbour[span].astype(F32)
        rows = stream_part(
            part, sign, far[span], near[span], layer, edge, values, values[6:7], factors
        )
        rows_out[span] = rows
        sent[span] = rows.astype(BF16)
        packed = pack_part(packed, part, sign, rows, factors)
    packed_out[:EDGE] = packed_near[...]
    packed_out[EDGE:] = edge_block(packed)


def lower_kernel(flags, near, far, sibling, neighbour, edges, masks, factors, lowered):
    at_near, at_far = place_of_near(flags)
    for part, span, new_near, new_far in streamed(
        flags, near, far, sibling, neighbour, edges, masks, factors
    ):
        lowered[pl.ds(at_near + PART * part, PART)] = new_near.astype(BF16)
        lowered[pl.ds(at_far + PART * part, PART)] = new_far.astype(BF16)


def last_kernel(given, flags, near, far, sibling, neighbour, edges, masks, factors, out):
    same = (flags[4] == 1) != given
    values = masks[...]
    edge_near, edge_far = (edges[rows_of(i, EDGE)].astype(F32)[:CHUNK] for i in range(2))
    edge, open_x = jnp.where(same, edge_near, edge_far), jnp.where(same, values[5:6], values[6:7])
    sign = jnp.where((flags[0] == 1) != given, 1.0, -1.0)
    start = pl.multiple_of(PAD * flags[1], 16)
    results = []
    for part in range(PAD // PART):
        span = rows_of(part, PART)
        rows_near, rows_far = near[span], far[span]
        layer_near = sibling[pl.ds(start + PART * part, PART)].astype(F32)
        layer = jnp.where(same, layer_near, neighbour[span].astype(F32))
        rows, mirror = jnp.where(same, rows_near, rows_far), jnp.where(same, rows_far, rows_near)
        results.append(stream_part(part, sign, rows, mirror, layer, edge, values, open_x, factors))
    results = jnp.concatenate(results, axis=0)
    if given:
        out[...] = results.astype(BF16)
    else:
        out[...] = reordered(order_matrix(flags[0] == 1), results)


def dot(left, right):
    return jnp.dot(left, right, preferred_element_type=F32)


def pack_other(packed, part, sign, values, factors):
    lane = lanes_of(CHUNK)
    place = lane & (NZ - 1)
    for index in range(2):
        chunk = 2 * part + index
        positive = factors[1, rows_of(chunk, CHUNK)] * sign > 0
        edge = picked(values[rows_of(index, CHUNK)], jnp.where(positive, place, place + NZ))
        packed = jnp.where((lane >> 4) == chunk, edge, packed)
    return packed


def unpacked(bands):
    values = bands.astype(F32)
    return jnp.concatenate([roll(values, -2 * NZ * group) for group in range(4)], axis=0).astype(BF16)


def collide_kernel(
    flags, lowered, other, bands, other_bands, factors, m0, m1, m2, m3, rows_out, packed_out, all_rows, all_bands
):
    swapped = flags[2] == 1
    for index, right in enumerate((swapped, ~swapped)):
        all_rows[rows_of(index, 2 * PAD)] = jnp.where(right, other[...], lowered[...])
        all_bands[rows_of(index, BAND)] = jnp.where(right, other_bands[...], bands[...])
    values = []
    for index in range(2):
        rows, band = all_rows[rows_of(index, 2 * PAD)], unpacked(all_bands[rows_of(index, BAND)])
        for side in range(2):
            span = rows_of(side, PAD)
            values.append(jnp.concatenate([rows[span], band[span]], axis=1))
    sign = jnp.where(flags[0] == 1, 1.0, -1.0)
    packed = jnp.zeros((CHUNK, LANES), F32)
    for part in range(PAD // PART):
        span = rows_of(part, PART)
        total = sum(dot(m[span], v) for m, v in zip((m0, m1, m2, m3), values))
        rows_out[span] = total[:, :LANES]
        packed = pack_other(packed, part, sign, total[:, LANES:], factors)
    packed_out[...] = edge_block(packed)


def give_rows(flags, part, rows_near, rows_far, factors, packed, outs):
    near, far, to_other_core, to_neighbour_chip = outs
    span = rows_of(part, PART)
    near[span], far[span] = rows_near, rows_far
    to_neighbour_chip[span] = rows_near.astype(BF16)
    to_other_core[span] = rows_far.astype(BF16)
    sign_near, sign_far = signs(flags)
    return (
        pack_part(packed[0], part, sign_near, rows_near, factors),
        pack_part(packed[1], part, sign_far, rows_far, factors),
    )


def give_product(flags, part, own, partner, factors, packed, outs):
    same = flags[4] == 1
    near, far = jnp.where(same, own, partner), jnp.where(same, partner, own)
    return give_rows(flags, part, near, far, factors, packed, outs)


def collide_partner_kernel(
    flags, factors, own_packed, all_rows, all_bands, own, matrix,
    near, far, for_sibling, for_neighbour, edges,
    held, held_rows, held_bands, held_own, held_packed, done,
):
    small = [
        pltpu.make_async_copy(source, target, done.at[index])
        for index, (source, target) in enumerate(
            ((all_rows, held_rows), (all_bands, held_bands), (own, held_own), (own_packed, held_packed))
        )
    ]
    parts = PAD // PART
    pieces = [
        [
            pltpu.make_async_copy(
                matrix.at[rows_of(parts * half + part, PART)],
                held.at[rows_of(parts * half + part, PART)],
                done.at[4 + parts * half + part],
            )
            for half in range(2)
        ]
        for part in range(parts)
    ]
    for copy in small + sum(pieces, []):
        copy.start()
    for copy in small:
        copy.wait()
    low, same = flags[0] == 1, flags[4] == 1
    values = []
    for index in range(2):
        band = unpacked(held_bands[rows_of(index, BAND)])
        values.append(jnp.concatenate([held_rows[rows_of(index, 2 * PAD)], band], axis=1))
    sign = jnp.where(low, -1.0, 1.0)
    packed = jnp.zeros((CHUNK, LANES), F32)
    for part in range(parts):
        span = rows_of(part, PART)
        total = 0.0
        for half in range(2):
            pieces[part][half].wait()
            total += dot(held[rows_of(parts * half + part, PART)], values[half])
        mine, theirs = held_own[span], total[:, :LANES]
        rows_near, rows_far = jnp.where(same, mine, theirs), jnp.where(same, theirs, mine)
        near[span], far[span] = rows_near, rows_far
        for_neighbour[span] = rows_near.astype(BF16)
        for_sibling[span] = rows_far.astype(BF16)
        packed = pack_other(packed, part, sign, total[:, LANES:], factors)
    mine, theirs = held_packed[...], edge_block(packed)
    edges[:EDGE] = jnp.where(same, mine, theirs)
    edges[EDGE:] = jnp.where(same, theirs, mine)


def early_kernel(
    flags, lowered, m0, m1, m2, m3, matrix, own_out, partner_out, next_own, next_partner,
    held_own, held_partner, done,
):
    values = lowered[...]
    parts = m0, m1, m2, m3
    for half in range(2):

        @pl.when(flags[2] == half)
        def _():
            copies = [
                pltpu.make_async_copy(
                    matrix.at[rows_of(half, PAD)], held_partner, done.at[0]
                )
            ]
            for i in range(2):
                copies.append(pltpu.make_async_copy(parts[2 * half + i], held_own.at[i], done.at[1 + i]))
            copies.append(
                pltpu.make_async_copy(matrix.at[rows_of(1 - half, PAD)], next_partner, done.at[3])
            )
            for i in range(2):
                source = parts[2 * (1 - half) + i]
                copies.append(pltpu.make_async_copy(source, next_own.at[i], done.at[4 + i]))
            for copy in copies:
                copy.start()
            copies[0].wait()
            for part in range(PAD // PART):
                span = rows_of(part, PART)
                partner_out[span] = dot(held_partner[span], values)
            copies[1].wait()
            copies[2].wait()
            for part in range(PAD // PART):
                span = rows_of(part, PART)
                own_out[span] = dot(held_own[0, span], values[:PAD]) + dot(held_own[1, span], values[PAD:])
            for copy in copies[3:]:
                copy.wait()


def late_kernel(flags, other, own, partner, factors, matrix_own, matrix_partner, *outs):
    values = other[...]
    packed = (jnp.zeros((CHUNK, LANES), F32),) * 2
    for part in range(PAD // PART):
        span = rows_of(part, PART)
        more_own = dot(matrix_own[0, span], values[:PAD]) + dot(matrix_own[1, span], values[PAD:])
        more_partner = dot(matrix_partner[span], values)
        packed = give_product(
            flags, part, own[span] + more_own, partner[span] + more_partner, factors, packed, outs[:4]
        )
    outs[4][:EDGE], outs[4][EDGE:] = edge_block(packed[0]), edge_block(packed[1])


ROWS_F32 = ((PAD, LANES), F32)
PARTNER_SCRATCH = [
    pltpu.VMEM((2 * PAD, 2 * PAD), BF16),
    pltpu.VMEM((4 * PAD, LANES), BF16),
    pltpu.VMEM((2 * BAND, LANES), BF16),
    pltpu.VMEM((PAD, LANES), F32),
    pltpu.VMEM((EDGE, LANES), BF16),
    pltpu.SemaphoreType.DMA((12,)),
]
HELD = [pltpu.VMEM((2, PAD, PAD), BF16), pltpu.VMEM((PAD, 2 * PAD), BF16)]
EARLY = [ROWS_F32, ROWS_F32, ((2, PAD, PAD), BF16), ((PAD, 2 * PAD), BF16)]
EARLY_SCRATCH = HELD + [pltpu.SemaphoreType.DMA((6,))]


def finish_kernel(flags, kept, received, evolved):
    order = order_matrix(flags[0] == 1)
    rest = jnp.dot(order, received[...], preferred_element_type=F32)
    mine = kept[...]
    half = flags[3]
    evolved[:, 0, :LANES] = jnp.where(half == 0, mine, rest)[:ROWS]
    evolved[:, 0, LANES:] = jnp.where(half == 0, rest, mine)[:ROWS]


def place(rows, columns, wanted):
    return (lax.broadcasted_iota(jnp.int32, (rows, columns), 0) == wanted[None, :]).astype(BF16)


def chosen(left, right):
    return jnp.dot(left, right, preferred_element_type=BF16)


def column_half(wide, block):
    column = lax.iota(jnp.int32, PAD)
    inside = column < ROWS
    start_a, start_b = 640 * block, jnp.where(block == 1, 1280, 2048)
    part_a = lax.dynamic_slice(wide, (0, start_a), (wide.shape[0], 768))
    part_b = lax.dynamic_slice(wide, (0, start_b), (wide.shape[0], 896))
    wanted_a = jnp.where(inside, ROWS * block + column - start_a, -1)
    wanted_b = jnp.where(inside, 4 * ROWS - 1 - ROWS * block - column - start_b, -1)
    halves = chosen(part_a, place(768, PAD, wanted_a)), chosen(part_b, place(896, PAD, wanted_b))
    return halves


def padded_columns(matrix):
    return jnp.pad(matrix, ((0, 0), (0, 2944 - matrix.shape[1])))


def per_device(populations, solid_mask, collision):
    cell, vel = lax.axis_index("cells"), lax.axis_index("vel")
    low = (vel < 2).astype(jnp.int32)
    core, ring_place = cell % 2, cell // 32 + 4 * (cell // 2 % 2)
    block = jnp.minimum(vel, 3 - vel)
    half = (1 - low) ^ (cell // RING % 2)
    needing = (cell + 1 - 2 * low) % 128
    straight_half = (1 - low) ^ (needing // RING % 2)
    same = (low != core).astype(jnp.int32)
    flags = jnp.stack([low, 1 - core, block, half, same, straight_half])
    flags = flags.astype(jnp.int32)

    first_row = CHUNK * ring_place
    row = first_row + lax.iota(jnp.int32, CHUNK)
    start = jnp.clip(jnp.where(low == 1, first_row, ROWS - CHUNK - first_row), 0, ROWS - CHUNK)
    wanted = jnp.where(row < ROWS, jnp.where(low == 1, row, ROWS - 1 - row) - start, -1)
    window = lax.dynamic_slice(collision, (start, 0), (CHUNK, collision.shape[1]))
    window = padded_columns(chosen(place(CHUNK, CHUNK, wanted).T, window))
    piece = jnp.concatenate(column_half(window, core), axis=1)
    populations, piece = lax.optimization_barrier((populations, piece))
    piece = to_mirror(piece)

    padded = jnp.pad(populations[:, 0, :], ((0, PAD - ROWS), (0, 0)))
    rows = (PAD, LANES)
    own, own_edge, message, straight, turned, masks, factors = call(
        prepare_kernel,
        [(rows, F32), ((CHUNK, LANES), F32), ((PAD + EDGE, LANES), BF16),
         ((PAD + 16, LANES), BF16), ((PAD + 16, LANES), BF16), ((8, LANES), F32), ((3, *rows), F32)],
        flags, padded, solid_mask, flops=2 * 3 * PAD * PAD * 256,
    )
    piece, _ = lax.optimization_barrier((piece, message))
    groups = [
        [x * 32 + y * 16 + 4 * pair + 2 * odd + side for side in range(2) for odd in range(2) for x in range(4)]
        for y in range(2)
        for pair in range(4)
    ]
    partner_matrix = lax.all_gather(piece, "cells", axis=0, tiled=True, axis_index_groups=groups)
    straight, turned = to_layer(straight, False), to_layer(turned, True)
    received = to_mirror(message)

    row = lax.iota(jnp.int32, PAD)
    wanted = jnp.where(row < ROWS, jnp.where(low == 1, row, ROWS - 1 - row), -1)
    received, collision = lax.optimization_barrier((received, collision))
    ordered = padded_columns(chosen(place(ROWS, PAD, wanted).T, collision))

    matrix = *column_half(ordered, 0), *column_half(ordered, 1)
    turned, *matrix = lax.optimization_barrier((turned, *matrix))
    lowered, masks, bands = call(
        first_kernel,
        [((2 * PAD, LANES), BF16), ((8, LANES), F32), ((BAND, LANES), BF16)],
        flags, own, own_edge, received, straight, turned, masks, factors, flops=100 * PAD * 256,
    )
    edges_shape = ((2 * EDGE, LANES), BF16)
    sends = [(rows, F32)] * 2 + [(rows, BF16)] * 2 + [edges_shape]
    multiply = 2 * PAD * 4 * PAD * LANES
    work = 100 * PAD * LANES

    other = to_side(lowered)
    bands = to_mirror(bands), to_opposite(bands)
    own, own_packed, all_rows, all_bands = call(
        collide_kernel,
        [(rows, F32), ((EDGE, LANES), BF16), ((4 * PAD, LANES), BF16), ((2 * BAND, LANES), BF16)],
        flags, lowered, other, *bands, factors, *matrix, flops=2 * multiply, leave=True,
    )
    partner_matrix, own = lax.optimization_barrier((partner_matrix, own))
    near, far, for_sibling, for_neighbour, edges = call(
        collide_partner_kernel, sends, flags, factors, own_packed, all_rows, all_bands, own, partner_matrix,
        flops=2 * multiply, stay=5, scratch=PARTNER_SCRATCH,
    )

    for step in range(1, STEPS):
        neighbour, sibling = to_neighbour(for_neighbour), with_sibling(for_sibling)
        new_near, for_neighbour, packed = call(
            between_near_kernel, [(rows, F32), (rows, BF16), ((EDGE, LANES), BF16)],
            flags, near, far, sibling, edges, masks, factors, flops=work,
        )
        new_far, for_sibling, edges = call(
            between_far_kernel, [(rows, F32), (rows, BF16), edges_shape],
            flags, near, far, neighbour, edges, masks, factors, packed, flops=work,
        )
        near, far = new_near, new_far
        neighbour, edges = to_neighbour(for_neighbour), to_mirror(edges)
        sibling = with_sibling(for_sibling)
        (lowered,) = call(
            lower_kernel, [((2 * PAD, LANES), BF16)],
            flags, near, far, sibling, neighbour, edges, masks, factors, flops=work,
        )
        other = to_side(lowered)
        early = call(
            early_kernel, EARLY, flags, lowered, *matrix, partner_matrix,
            flops=multiply, stay=5, scratch=EARLY_SCRATCH,
        )
        near, far, for_sibling, for_neighbour, edges = call(
            late_kernel, sends, flags, other, *early[:2], factors, *early[2:], flops=multiply
        )

    neighbour, edges = to_neighbour(for_neighbour), to_mirror(edges)
    sibling = with_sibling(for_sibling)
    last = flags, near, far, sibling, neighbour, edges, masks, factors
    (message,) = call(functools.partial(last_kernel, True), [(rows, BF16)], *last, flops=work)
    received = to_mirror(message)
    (kept,) = call(functools.partial(last_kernel, False), [(rows, F32)], *last, flops=multiply)
    (evolved,) = call(
        finish_kernel, [((ROWS, 1, 2 * LANES), F32)], flags, kept, received, flops=2 * PAD * PAD * LANES
    )
    return evolved


def solution(mesh):
    in_specs = (P("vel", "cells", None), P("cells", None), P("vel", None))
    out_specs = P("vel", "cells", None)
    return jax.shard_map(
        per_device, mesh=mesh, in_specs=in_specs, out_specs=out_specs, check_vma=False
    )
```

```python
import functools
import math

import jax
import jax.numpy as jnp
from jax import lax
from jax.experimental import pallas as pl
from jax.experimental.pallas import tpu as pltpu
from jax.sharding import PartitionSpec as P


K = 14
STEPS = 2
NZ = 16
BOTH = ("cells", "vel")
ROWS = 686
PAD = 704
CHUNK = 88
PART = 2 * CHUNK
EDGE = 96
LANES = 128
BAND = 4 * CHUNK
PIECE = 96
PIECES = 8
RING = 16
F32 = jnp.float32
BF16 = jnp.bfloat16
PARAMS = pltpu.CompilerParams(vmem_limit_bytes=20 * 1024 * 1024)


def pairs_of(target):
    pairs = []
    for cell in range(128):
        for part in range(4):
            to_cell, to_part = target(cell, part)
            pairs.append((cell * 4 + part, to_cell * 4 + to_part))
    return pairs


def to_sibling(array):
    return lax.ppermute(array, "cells", [(cell, cell ^ 1) for cell in range(128)])


def with_sibling(array):
    groups = [[cell, cell + 1] for cell in range(0, 128, 2)]
    return lax.all_gather(array, "cells", axis=0, tiled=True, axis_index_groups=groups)


def to_layer(array, turned):
    def target(cell, part):
        return (cell - 1 if part < 2 else cell + 1) % 128, 3 - part if turned else part

    return lax.ppermute(array, BOTH, pairs_of(target))


def neighbour_of(cell, part):
    other = (cell - 1 if cell % 2 == 0 else cell + 1) % 128
    return other, part if (other // RING) % 2 == (cell // RING) % 2 else 3 - part


def to_neighbour(array):
    return lax.ppermute(array, BOTH, pairs_of(neighbour_of))


def to_next_z(array):
    return lax.ppermute(array, "cells", [(cell, cell ^ 2) for cell in range(128)])


def along_x(array, step):
    return lax.ppermute(array, "cells", [(cell, (cell + 32 * step) % 128) for cell in range(128)])


def to_mirror(array):
    return lax.ppermute(array, "vel", [(i, 3 - i) for i in range(4)])


def to_opposite(array):
    return lax.ppermute(array, "vel", [(i, i ^ 2) for i in range(4)])


def to_side(array):
    return lax.ppermute(array, "vel", [(i, i ^ 1) for i in range(4)])


def call(kernel, outs, flags, *arrays, flops=0, scratch=()):
    moved = sum(x.size * x.dtype.itemsize for x in arrays)
    moved += sum(math.prod(shape) * jnp.dtype(dtype).itemsize for shape, dtype in outs)
    vmem = pl.BlockSpec(memory_space=pltpu.VMEM)
    return pl.pallas_call(
        kernel,
        out_shape=[jax.ShapeDtypeStruct(shape, dtype) for shape, dtype in outs],
        in_specs=[pl.BlockSpec(memory_space=pltpu.SMEM)] + [vmem] * len(arrays),
        out_specs=[vmem] * len(outs),
        scratch_shapes=[pltpu.VMEM(shape, dtype) for shape, dtype in scratch],
        compiler_params=PARAMS,
        cost_estimate=pl.CostEstimate(flops=flops, bytes_accessed=moved, transcendentals=0),
    )(flags, *arrays)


def roll(values, shift):
    return pltpu.roll(values, shift % values.shape[1], 1)


def order_matrix(low):
    row = lax.broadcasted_iota(jnp.int32, (PAD, PAD), 0)
    column = lax.broadcasted_iota(jnp.int32, (PAD, PAD), 1)
    wanted = jnp.where(low, row, ROWS - 1 - row)
    return jnp.where((column == wanted) & (row < ROWS), 1.0, 0.0).astype(BF16)


def reordered(order, values):
    total = jnp.zeros(values.shape, F32)
    for _ in range(3):
        part = values.astype(BF16)
        total += jnp.dot(order, part, preferred_element_type=F32)
        values = values - part.astype(F32)
    return total


def signed_factors(block, chunk):
    row = CHUNK * chunk + lax.broadcasted_iota(jnp.int32, (CHUNK, LANES), 0)
    ids = ROWS * block + row
    upper = (ids * 4682) >> 16
    k_z = ids - K * upper
    k_x = (upper * 4682) >> 16
    k_y = upper - K * k_x
    centre = (K - 1) / 2.0
    x, y, z = ((k.astype(F32) - centre) * (0.3 / centre) for k in (k_x, k_y, k_z))
    return jnp.abs(x), y, z


def lanes_of(rows):
    return lax.broadcasted_iota(jnp.int32, (rows, LANES), 1)


def lower_z(values):
    z_place = lax.broadcasted_iota(jnp.int32, values.shape, 1) % NZ
    return jnp.where(z_place == 0, roll(values, 1 - NZ), roll(values, 1))


def upper_z(values):
    z_place = lax.broadcasted_iota(jnp.int32, values.shape, 1) % NZ
    return jnp.where(z_place == NZ - 1, roll(values, NZ - 1), roll(values, -1))


def picked(values, lanes):
    return jnp.take_along_axis(values, lanes, axis=1, mode="promise_in_bounds")


def pack_edge(packed, values, positive, chunk, lane):
    place = lane & (NZ - 1)
    edge = picked(values, jnp.where(positive, place + LANES - NZ, place))
    return jnp.where((lane >> 4) == chunk, edge, packed)


def edge_block(packed):
    return jnp.concatenate([packed, jnp.zeros((EDGE - CHUNK, LANES), F32)], axis=0).astype(BF16)


def prepare_kernel(
    flags, populations, solid, own, own_edge, message, straight, turned, masks, factors
):
    low, block, half = flags[0] == 1, flags[2], flags[3]
    ordered = reordered(order_matrix(low), populations[...])
    left, right = ordered[:, :LANES], ordered[:, LANES:]
    mine = jnp.where(half == 0, left, right)
    rest = jnp.where(half == 0, right, left)
    own[...] = mine
    edges = jnp.zeros((CHUNK, LANES), F32)
    sent = jnp.zeros((CHUNK, LANES), F32)
    lane = lanes_of(CHUNK)
    for chunk in range(PAD // CHUNK):
        rows = slice(CHUNK * chunk, CHUNK * (chunk + 1))
        x, y, z = signed_factors(block, chunk)
        factors[0, rows], factors[1, rows], factors[2, rows] = x, y, z
        positive = jnp.where(low, y, -y) > 0
        edges = pack_edge(edges, rest[rows], positive, chunk, lane)
        sent = pack_edge(sent, mine[rows], positive, chunk, lane)
    own_edge[...] = edges
    message[:PAD] = rest.astype(BF16)
    message[PAD:] = edge_block(sent)
    fluid = jnp.where(jnp.broadcast_to(solid[...], (8, 2 * LANES)) == 0, 1.0, 0.0)
    place = lax.broadcasted_iota(jnp.int32, (8, 2 * LANES), 0)
    found = jnp.zeros((8, 2 * LANES), F32)
    near = (fluid, roll(fluid, NZ), roll(fluid, -NZ), lower_z(fluid), upper_z(fluid))
    for index, value in enumerate(near):
        found = jnp.where(place == index, value, found)
    masks[...] = jnp.where(half == 0, found[:, :LANES], found[:, LANES:])
    row = lax.broadcasted_iota(jnp.int32, (16, LANES), 0)
    halves = []
    for side in range(2):
        cells = slice(LANES * side, LANES * (side + 1))
        open_cells = jnp.where(row == 0, jnp.broadcast_to(fluid[:1, cells], (16, LANES)), 0.0)
        halves.append((ordered[:, cells].astype(BF16), open_cells.astype(BF16)))
    for place, target in ((flags[5], straight), (1 - flags[5], turned)):
        for rows, low_value, high_value in zip((slice(0, PAD), slice(PAD, PAD + 16)), *halves):
            target[rows] = jnp.where(place == 0, low_value, high_value)


def rows_of(index, size):
    return slice(size * index, size * (index + 1))


def stream_part(part, sign, values, mirror, layer, edge, masks, open_x, factors):
    fluid, below_open_y, above_open_y, below_open_z, above_open_z = (
        jnp.broadcast_to(masks[i : i + 1], (CHUNK, LANES)) for i in range(5)
    )
    open_x = jnp.broadcast_to(open_x, (CHUNK, LANES))
    lane = lanes_of(CHUNK)
    z_place = lane & (NZ - 1)
    below_z = jnp.where(z_place == 0, lane + NZ - 1, lane - 1)
    above_z = jnp.where(z_place == NZ - 1, lane + 1 - NZ, lane + 1)
    below_y, above_y = (lane + LANES - NZ) & (LANES - 1), (lane + NZ) & (LANES - 1)
    results = []
    for index in range(2):
        chunk = 2 * part + index
        x, y, z = (factors[i, rows_of(chunk, CHUNK)] for i in range(3))
        up_y, up_z = y * sign > 0, z * sign > 0
        here, back = values[rows_of(index, CHUNK)], mirror[rows_of(index, CHUNK)]
        at_edge = jnp.where(up_y, lane, lane + NZ)
        put = picked(edge, (at_edge + NZ * chunk) & (LANES - 1))
        outside = (up_y & (lane < NZ)) | (~up_y & (lane >= LANES - NZ))
        near_y = jnp.where(outside, put, picked(here, jnp.where(up_y, below_y, above_y)))
        near_z = picked(here, jnp.where(up_z, below_z, above_z))
        upwind_x = jnp.where(open_x > 0, layer[rows_of(index, CHUNK)], back)
        upwind_y = jnp.where(jnp.where(up_y, below_open_y, above_open_y) > 0, near_y, back)
        upwind_z = jnp.where(jnp.where(up_z, below_open_z, above_open_z) > 0, near_z, back)
        outflow = x * (here - upwind_x)
        outflow += jnp.abs(y) * (here - upwind_y)
        outflow += jnp.abs(z) * (here - upwind_z)
        results.append((here - outflow) * fluid)
    return jnp.concatenate(results, axis=0)


def pack_part(packed, part, sign, values, factors):
    lane = lanes_of(CHUNK)
    for index in range(2):
        chunk = 2 * part + index
        positive = factors[1, rows_of(chunk, CHUNK)] * sign > 0
        packed = pack_edge(packed, values[rows_of(index, CHUNK)], positive, chunk, lane)
    return packed


def signs(flags):
    near = jnp.where(flags[1] == 1, 1.0, -1.0)
    return near, -near


def place_of_near(flags):
    return pl.multiple_of(PAD * (1 - flags[1]), 16), pl.multiple_of(PAD * flags[1], 16)


def first_kernel(
    flags, own, own_edge, received, straight, turned, masks_in, factors, lowered, masks_out, bands
):
    same = flags[4] == 1
    place = lax.broadcasted_iota(jnp.int32, (8, LANES), 0)
    open_own = straight[PAD:].astype(F32)[:1]
    open_other = turned[PAD:].astype(F32)[:1]
    masks = masks_in[...]
    masks = jnp.where(place == 5, jnp.where(same, open_own, open_other), masks)
    masks = jnp.where(place == 6, jnp.where(same, open_other, open_own), masks)
    masks_out[...] = masks
    edge_own, edge_other = own_edge[...], received[PAD:].astype(F32)[:CHUNK]
    sign = jnp.where(flags[0] == 1, 1.0, -1.0)
    low = flags[0] == 1
    group = lanes_of(PART) >> 5
    packed = [jnp.zeros((PART, LANES), F32)] * 2
    for part in range(PAD // PART):
        span = rows_of(part, PART)
        mine, theirs = own[span], received[span].astype(F32)
        new_own = stream_part(
            part, sign, mine, theirs, straight[span].astype(F32), edge_own, masks, open_own, factors
        )
        new_other = stream_part(
            part, -sign, theirs, mine, turned[span].astype(F32), edge_other, masks, open_other, factors
        )
        rows_a, rows_b = jnp.where(low, new_own, new_other), jnp.where(low, new_other, new_own)
        for index, rows in enumerate((rows_a, rows_b)):
            lowered[PAD * index + PART * part : PAD * index + PART * (part + 1)] = rows.astype(BF16)
            place = 2 * index + part // 2
            edge = roll(rows, NZ + 2 * NZ * place)
            packed[part % 2] = jnp.where(group == place, edge, packed[part % 2])
    for index in range(2):
        bands[rows_of(index, PART)] = packed[index].astype(BF16)


def streamed(flags, near, far, sibling, neighbour, edges, masks, factors):
    values = masks[...]
    edge_near, edge_far = (edges[rows_of(i, EDGE)].astype(F32)[:CHUNK] for i in range(2))
    sign_near, sign_far = signs(flags)
    start = pl.multiple_of(PAD * flags[1], 16)
    for part in range(PAD // PART):
        span = rows_of(part, PART)
        rows_near, rows_far = near[span], far[span]
        layer = sibling[pl.ds(start + PART * part, PART)].astype(F32)
        new_near = stream_part(
            part, sign_near, rows_near, rows_far, layer, edge_near, values, values[5:6], factors
        )
        layer = neighbour[span].astype(F32)
        new_far = stream_part(
            part, sign_far, rows_far, rows_near, layer, edge_far, values, values[6:7], factors
        )
        yield part, span, new_near, new_far


def between_near_kernel(flags, near, far, sibling, edges, masks, factors, rows_out, sent, packed_out):
    values = masks[...]
    sign = signs(flags)[0]
    start = pl.multiple_of(PAD * flags[1], 16)
    edge = edges[:EDGE].astype(F32)[:CHUNK]
    packed = jnp.zeros((CHUNK, LANES), F32)
    for part in range(PAD // PART):
        span = rows_of(part, PART)
        layer = sibling[pl.ds(start + PART * part, PART)].astype(F32)
        rows = stream_part(
            part, sign, near[span], far[span], layer, edge, values, values[5:6], factors
        )
        rows_out[span] = rows
        sent[span] = rows.astype(BF16)
        packed = pack_part(packed, part, sign, rows, factors)
    packed_out[...] = edge_block(packed)


def between_far_kernel(
    flags, near, far, neighbour, edges, masks, factors, packed_near, rows_out, sent, packed_out
):
    values = masks[...]
    sign = signs(flags)[1]
    edge = edges[EDGE:].astype(F32)[:CHUNK]
    packed = jnp.zeros((CHUNK, LANES), F32)
    for part in range(PAD // PART):
        span = rows_of(part, PART)
        layer = neighbour[span].astype(F32)
        rows = stream_part(
            part, sign, far[span], near[span], layer, edge, values, values[6:7], factors
        )
        rows_out[span] = rows
        sent[span] = rows.astype(BF16)
        packed = pack_part(packed, part, sign, rows, factors)
    packed_out[:EDGE] = packed_near[...]
    packed_out[EDGE:] = edge_block(packed)


def lower_kernel(flags, near, far, sibling, neighbour, edges, masks, factors, lowered):
    at_near, at_far = place_of_near(flags)
    for part, span, new_near, new_far in streamed(
        flags, near, far, sibling, neighbour, edges, masks, factors
    ):
        lowered[pl.ds(at_near + PART * part, PART)] = new_near.astype(BF16)
        lowered[pl.ds(at_far + PART * part, PART)] = new_far.astype(BF16)


def last_kernel(given, flags, near, far, sibling, neighbour, edges, masks, factors, out):
    same = (flags[4] == 1) != given
    values = masks[...]
    edge_near, edge_far = (edges[rows_of(i, EDGE)].astype(F32)[:CHUNK] for i in range(2))
    edge, open_x = jnp.where(same, edge_near, edge_far), jnp.where(same, values[5:6], values[6:7])
    sign = jnp.where((flags[0] == 1) != given, 1.0, -1.0)
    start = pl.multiple_of(PAD * flags[1], 16)
    results = []
    for part in range(PAD // PART):
        span = rows_of(part, PART)
        rows_near, rows_far = near[span], far[span]
        layer_near = sibling[pl.ds(start + PART * part, PART)].astype(F32)
        layer = jnp.where(same, layer_near, neighbour[span].astype(F32))
        rows, mirror = jnp.where(same, rows_near, rows_far), jnp.where(same, rows_far, rows_near)
        results.append(stream_part(part, sign, rows, mirror, layer, edge, values, open_x, factors))
    results = jnp.concatenate(results, axis=0)
    if given:
        out[...] = results.astype(BF16)
    else:
        out[...] = reordered(order_matrix(flags[0] == 1), results)


def dot(left, right):
    return jnp.dot(left, right, preferred_element_type=F32)


def pack_other(packed, part, sign, values, factors):
    lane = lanes_of(CHUNK)
    place = lane & (NZ - 1)
    for index in range(2):
        chunk = 2 * part + index
        positive = factors[1, rows_of(chunk, CHUNK)] * sign > 0
        edge = picked(values[rows_of(index, CHUNK)], jnp.where(positive, place, place + NZ))
        packed = jnp.where((lane >> 4) == chunk, edge, packed)
    return packed


def unpacked(bands):
    values = bands.astype(F32)
    return jnp.concatenate([roll(values, -2 * NZ * group) for group in range(4)], axis=0).astype(BF16)


def collide_kernel(
    flags, lowered, other, bands, other_bands, factors, m0, m1, m2, m3, rows_out, packed_out, all_rows, all_bands
):
    swapped = flags[2] == 1
    values = []
    for index, right in enumerate((swapped, ~swapped)):
        slot = jnp.where(flags[1] == 1, index, 1 - index)
        rows = jnp.where(right, other[...], lowered[...])
        all_rows[pl.ds(pl.multiple_of(2 * PAD * slot, 16), 2 * PAD)] = rows
        band = unpacked(jnp.where(right, other_bands[...], bands[...]))
        all_bands[pl.ds(pl.multiple_of(2 * PAD * slot, 16), 2 * PAD)] = band
        for side in range(2):
            span = rows_of(side, PAD)
            values.append(jnp.concatenate([rows[span], band[span]], axis=1))
    sign = jnp.where(flags[0] == 1, 1.0, -1.0)
    packed = jnp.zeros((CHUNK, LANES), F32)
    for part in range(PAD // PART):
        span = rows_of(part, PART)
        total = sum(dot(m[span], v) for m, v in zip((m0, m1, m2, m3), values))
        rows_out[span] = total[:, :LANES]
        packed = pack_other(packed, part, sign, total[:, LANES:], factors)
    packed_out[...] = edge_block(packed)


def give_rows(flags, part, rows_near, rows_far, factors, packed, outs):
    near, far, to_other_core, to_neighbour_chip = outs
    span = rows_of(part, PART)
    near[span], far[span] = rows_near, rows_far
    to_neighbour_chip[span] = rows_near.astype(BF16)
    to_other_core[span] = rows_far.astype(BF16)
    sign_near, sign_far = signs(flags)
    return (
        pack_part(packed[0], part, sign_near, rows_near, factors),
        pack_part(packed[1], part, sign_far, rows_far, factors),
    )


def give_product(flags, part, own, partner, factors, packed, outs):
    same = flags[4] == 1
    near, far = jnp.where(same, own, partner), jnp.where(same, partner, own)
    return give_rows(flags, part, near, far, factors, packed, outs)


def partner_product(flags, matrix, values, give):
    for index in range(PIECES):
        start = pl.multiple_of(PIECE * flags[6 + index], 8)
        give(pl.ds(start, PIECE), dot(matrix[rows_of(index, PIECE)], values))


def collide_partner_kernel(
    flags, own, own_packed, all_rows, all_bands, factors, mine, theirs,
    near, far, for_sibling, for_neighbour, edges, total,
):
    values = [
        jnp.concatenate([all_rows[rows_of(i, 2 * PAD)], all_bands[rows_of(i, 2 * PAD)]], axis=1)
        for i in range(2)
    ]
    for index in range(PIECES):
        start = pl.multiple_of(PIECE * flags[6 + index], 8)
        span = rows_of(index, PIECE)
        total[pl.ds(start, PIECE)] = dot(mine[span], values[0]) + dot(theirs[span], values[1])
    low, same = flags[0] == 1, flags[4] == 1
    sign = jnp.where(low, -1.0, 1.0)
    packed = jnp.zeros((CHUNK, LANES), F32)
    for part in range(PAD // PART):
        span = rows_of(part, PART)
        rows_own, rows_partner = own[span], total[span, :LANES]
        rows_near = jnp.where(same, rows_own, rows_partner)
        rows_far = jnp.where(same, rows_partner, rows_own)
        near[span], far[span] = rows_near, rows_far
        for_neighbour[span] = rows_near.astype(BF16)
        for_sibling[span] = rows_far.astype(BF16)
        packed = pack_other(packed, part, sign, total[span, LANES:], factors)
    packed_own, packed_partner = own_packed[...], edge_block(packed)
    edges[:EDGE] = jnp.where(same, packed_own, packed_partner)
    edges[EDGE:] = jnp.where(same, packed_partner, packed_own)


def half_products(flags, half_wanted, lowered, parts, mine, theirs, give_own, give_partner):
    values = lowered[...]
    for half in range(2):

        @pl.when(half_wanted == half)
        def _():
            for part in range(PAD // PART):
                span = rows_of(part, PART)
                total = dot(parts[2 * half][span], values[:PAD])
                give_own(span, total + dot(parts[2 * half + 1][span], values[PAD:]))

    core = 1 - flags[1]
    for held, here in ((mine, half_wanted == core), (theirs, half_wanted != core)):

        @pl.when(here)
        def _():
            partner_product(flags, held, values, give_partner)


def early_kernel(flags, lowered, m0, m1, m2, m3, mine, theirs, own_out, partner_out):
    def give_own(span, rows):
        own_out[span] = rows

    def give_partner(span, rows):
        partner_out[span] = rows

    half_products(flags, flags[2], lowered, (m0, m1, m2, m3), mine, theirs, give_own, give_partner)


def late_kernel(flags, other, own, partner, factors, m0, m1, m2, m3, mine, theirs, *refs):
    outs, (total_own, total_partner) = refs[:5], refs[5:]

    def give_own(span, rows):
        total_own[span] = own[span] + rows

    def give_partner(span, rows):
        total_partner[span] = partner[span] + rows

    half_products(flags, 1 - flags[2], other, (m0, m1, m2, m3), mine, theirs, give_own, give_partner)
    packed = (jnp.zeros((CHUNK, LANES), F32),) * 2
    for part in range(PAD // PART):
        span = rows_of(part, PART)
        packed = give_product(
            flags, part, total_own[span], total_partner[span], factors, packed, outs[:4]
        )
    outs[4][:EDGE], outs[4][EDGE:] = edge_block(packed[0]), edge_block(packed[1])


ROWS_F32 = ((PAD, LANES), F32)
PIECES_F32 = ((PIECES * PIECE, LANES), F32)


def finish_kernel(flags, kept, received, evolved):
    order = order_matrix(flags[0] == 1)
    rest = jnp.dot(order, received[...], preferred_element_type=F32)
    mine = kept[...]
    half = flags[3]
    evolved[:, 0, :LANES] = jnp.where(half == 0, mine, rest)[:ROWS]
    evolved[:, 0, LANES:] = jnp.where(half == 0, rest, mine)[:ROWS]


def place(rows, columns, wanted):
    return (lax.broadcasted_iota(jnp.int32, (rows, columns), 0) == wanted[None, :]).astype(BF16)


def chosen(left, right):
    return jnp.dot(left, right, preferred_element_type=BF16)


def column_half(wide, block):
    column = lax.iota(jnp.int32, PAD)
    inside = column < ROWS
    start_a, start_b = 640 * block, jnp.where(block == 1, 1280, 2048)
    part_a = lax.dynamic_slice(wide, (0, start_a), (wide.shape[0], 768))
    part_b = lax.dynamic_slice(wide, (0, start_b), (wide.shape[0], 896))
    wanted_a = jnp.where(inside, ROWS * block + column - start_a, -1)
    wanted_b = jnp.where(inside, 4 * ROWS - 1 - ROWS * block - column - start_b, -1)
    halves = chosen(part_a, place(768, PAD, wanted_a)), chosen(part_b, place(896, PAD, wanted_b))
    return halves


def padded_columns(matrix):
    return jnp.pad(matrix, ((0, 0), (0, 2944 - matrix.shape[1])))


def per_device(populations, solid_mask, collision):
    cell, vel = lax.axis_index("cells"), lax.axis_index("vel")
    low = (vel < 2).astype(jnp.int32)
    core, line, odd = cell % 2, cell // 32, cell // 2 % 2
    pieces = [2 * ((line + step) % 4) + (odd ^ other) for step in (0, 3, 1, 2) for other in range(2)]
    block = jnp.minimum(vel, 3 - vel)
    half = (1 - low) ^ (cell // RING % 2)
    needing = (cell + 1 - 2 * low) % 128
    straight_half = (1 - low) ^ (needing // RING % 2)
    same = (low != core).astype(jnp.int32)
    flags = jnp.stack([low, 1 - core, block, half, same, straight_half, *pieces])
    flags = flags.astype(jnp.int32)

    first_row = PIECE * pieces[0]
    row = first_row + lax.iota(jnp.int32, PIECE)
    start = jnp.clip(jnp.where(low == 1, first_row, ROWS - PIECE - first_row), 0, ROWS - PIECE)
    wanted = jnp.where(row < ROWS, jnp.where(low == 1, row, ROWS - 1 - row) - start, -1)
    window = lax.dynamic_slice(collision, (start, 0), (PIECE, collision.shape[1]))
    window = padded_columns(chosen(place(PIECE, PIECE, wanted).T, window))
    piece = jnp.concatenate(column_half(window, core), axis=1)
    populations, piece = lax.optimization_barrier((populations, piece))
    piece = to_mirror(piece)
    pair = jnp.concatenate([piece, to_next_z(piece)], axis=0)
    below, above = along_x(pair, 1), along_x(pair, -1)
    beyond = along_x(below[:PIECE], 1), along_x(above[PIECE:], -1)
    mine = jnp.concatenate([pair, below, above, *beyond], axis=0)
    theirs = to_sibling(mine)

    padded = jnp.pad(populations[:, 0, :], ((0, PAD - ROWS), (0, 0)))
    rows = (PAD, LANES)
    own, own_edge, message, straight, turned, masks, factors = call(
        prepare_kernel,
        [(rows, F32), ((CHUNK, LANES), F32), ((PAD + EDGE, LANES), BF16),
         ((PAD + 16, LANES), BF16), ((PAD + 16, LANES), BF16), ((8, LANES), F32), ((3, *rows), F32)],
        flags, padded, solid_mask, flops=2 * 3 * PAD * PAD * 256,
    )
    straight, turned = to_layer(straight, False), to_layer(turned, True)
    received = to_mirror(message)

    row = lax.iota(jnp.int32, PAD)
    wanted = jnp.where(row < ROWS, jnp.where(low == 1, row, ROWS - 1 - row), -1)
    received, collision = lax.optimization_barrier((received, collision))
    ordered = padded_columns(chosen(place(ROWS, PAD, wanted).T, collision))

    matrix = *column_half(ordered, 0), *column_half(ordered, 1)
    turned, *matrix = lax.optimization_barrier((turned, *matrix))
    lowered, masks, bands = call(
        first_kernel,
        [((2 * PAD, LANES), BF16), ((8, LANES), F32), ((BAND, LANES), BF16)],
        flags, own, own_edge, received, straight, turned, masks, factors, flops=100 * PAD * 256,
    )
    edges_shape = ((2 * EDGE, LANES), BF16)
    sends = [(rows, F32)] * 2 + [(rows, BF16)] * 2 + [edges_shape]
    multiply = 2 * PAD * 4 * PAD * LANES
    work = 100 * PAD * LANES

    other = to_side(lowered)
    bands = to_mirror(bands), to_opposite(bands)
    wide = ((4 * PAD, LANES), BF16)
    own, own_packed, all_rows, all_bands = call(
        collide_kernel, [(rows, F32), ((EDGE, LANES), BF16), wide, wide],
        flags, lowered, other, *bands, factors, *matrix, flops=2 * multiply,
    )
    near, far, for_sibling, for_neighbour, edges = call(
        collide_partner_kernel, sends,
        flags, own, own_packed, all_rows, all_bands, factors, mine, theirs,
        flops=2 * multiply, scratch=[((PIECES * PIECE, 2 * LANES), F32)],
    )

    for step in range(1, STEPS):
        neighbour, sibling = to_neighbour(for_neighbour), with_sibling(for_sibling)
        new_near, for_neighbour, packed = call(
            between_near_kernel, [(rows, F32), (rows, BF16), ((EDGE, LANES), BF16)],
            flags, near, far, sibling, edges, masks, factors, flops=work,
        )
        new_far, for_sibling, edges = call(
            between_far_kernel, [(rows, F32), (rows, BF16), edges_shape],
            flags, near, far, neighbour, edges, masks, factors, packed, flops=work,
        )
        near, far = new_near, new_far
        neighbour, edges = to_neighbour(for_neighbour), to_mirror(edges)
        sibling = with_sibling(for_sibling)
        (lowered,) = call(
            lower_kernel, [((2 * PAD, LANES), BF16)],
            flags, near, far, sibling, neighbour, edges, masks, factors, flops=work,
        )
        other = to_side(lowered)
        early = call(
            early_kernel, [ROWS_F32, PIECES_F32], flags, lowered, *matrix, mine, theirs, flops=multiply
        )
        near, far, for_sibling, for_neighbour, edges = call(
            late_kernel, sends, flags, other, *early, factors, *matrix, mine, theirs,
            flops=multiply, scratch=[ROWS_F32, PIECES_F32],
        )

    neighbour, edges = to_neighbour(for_neighbour), to_mirror(edges)
    sibling = with_sibling(for_sibling)
    last = flags, near, far, sibling, neighbour, edges, masks, factors
    (message,) = call(functools.partial(last_kernel, True), [(rows, BF16)], *last, flops=work)
    received = to_mirror(message)
    (kept,) = call(functools.partial(last_kernel, False), [(rows, F32)], *last, flops=multiply)
    (evolved,) = call(
        finish_kernel, [((ROWS, 1, 2 * LANES), F32)], flags, kept, received, flops=2 * PAD * PAD * LANES
    )
    return evolved


def solution(mesh):
    in_specs = (P("vel", "cells", None), P("cells", None), P("vel", None))
    out_specs = P("vel", "cells", None)
    return jax.shard_map(
        per_device, mesh=mesh, in_specs=in_specs, out_specs=out_specs, check_vma=False
    )
```

```python
import functools
import math

import jax
import jax.numpy as jnp
from jax import lax
from jax.experimental import pallas as pl
from jax.experimental.pallas import tpu as pltpu
from jax.sharding import PartitionSpec as P


K = 14
STEPS = 2
NZ = 16
BOTH = ("cells", "vel")
ROWS = 686
PAD = 704
CHUNK = 88
PART = 2 * CHUNK
EDGE = 96
LANES = 128
BAND = 4 * CHUNK
PIECE = 96
PIECES = 8
RING = 16
F32 = jnp.float32
BF16 = jnp.bfloat16
PARAMS = pltpu.CompilerParams(vmem_limit_bytes=20 * 1024 * 1024)


def pairs_of(target):
    pairs = []
    for cell in range(128):
        for part in range(4):
            to_cell, to_part = target(cell, part)
            pairs.append((cell * 4 + part, to_cell * 4 + to_part))
    return pairs


def to_sibling(array):
    return lax.ppermute(array, "cells", [(cell, cell ^ 1) for cell in range(128)])


def with_sibling(array):
    groups = [[cell, cell + 1] for cell in range(0, 128, 2)]
    return lax.all_gather(array, "cells", axis=0, tiled=True, axis_index_groups=groups)


def to_layer(array, turned):
    def target(cell, part):
        return (cell - 1 if part < 2 else cell + 1) % 128, 3 - part if turned else part

    return lax.ppermute(array, BOTH, pairs_of(target))


def neighbour_of(cell, part):
    other = (cell - 1 if cell % 2 == 0 else cell + 1) % 128
    return other, part if (other // RING) % 2 == (cell // RING) % 2 else 3 - part


def to_neighbour(array):
    return lax.ppermute(array, BOTH, pairs_of(neighbour_of))


def to_next_z(array):
    return lax.ppermute(array, "cells", [(cell, cell ^ 2) for cell in range(128)])


def along_x(array, step):
    return lax.ppermute(array, "cells", [(cell, (cell + 32 * step) % 128) for cell in range(128)])


def to_mirror(array):
    return lax.ppermute(array, "vel", [(i, 3 - i) for i in range(4)])


def to_opposite(array):
    return lax.ppermute(array, "vel", [(i, i ^ 2) for i in range(4)])


def to_side(array):
    return lax.ppermute(array, "vel", [(i, i ^ 1) for i in range(4)])


def call(kernel, outs, flags, *arrays, flops=0, scratch=()):
    moved = sum(x.size * x.dtype.itemsize for x in arrays)
    moved += sum(math.prod(shape) * jnp.dtype(dtype).itemsize for shape, dtype in outs)
    vmem = pl.BlockSpec(memory_space=pltpu.VMEM)
    return pl.pallas_call(
        kernel,
        out_shape=[jax.ShapeDtypeStruct(shape, dtype) for shape, dtype in outs],
        in_specs=[pl.BlockSpec(memory_space=pltpu.SMEM)] + [vmem] * len(arrays),
        out_specs=[vmem] * len(outs),
        scratch_shapes=[pltpu.VMEM(shape, dtype) for shape, dtype in scratch],
        compiler_params=PARAMS,
        cost_estimate=pl.CostEstimate(flops=flops, bytes_accessed=moved, transcendentals=0),
    )(flags, *arrays)


def roll(values, shift):
    return pltpu.roll(values, shift % values.shape[1], 1)


def order_matrix(low):
    row = lax.broadcasted_iota(jnp.int32, (PAD, PAD), 0)
    column = lax.broadcasted_iota(jnp.int32, (PAD, PAD), 1)
    wanted = jnp.where(low, row, ROWS - 1 - row)
    return jnp.where((column == wanted) & (row < ROWS), 1.0, 0.0).astype(BF16)


def reordered(order, values):
    total = jnp.zeros(values.shape, F32)
    for _ in range(3):
        part = values.astype(BF16)
        total += jnp.dot(order, part, preferred_element_type=F32)
        values = values - part.astype(F32)
    return total


def signed_factors(block, chunk):
    row = CHUNK * chunk + lax.broadcasted_iota(jnp.int32, (CHUNK, LANES), 0)
    ids = ROWS * block + row
    upper = (ids * 4682) >> 16
    k_z = ids - K * upper
    k_x = (upper * 4682) >> 16
    k_y = upper - K * k_x
    centre = (K - 1) / 2.0
    x, y, z = ((k.astype(F32) - centre) * (0.3 / centre) for k in (k_x, k_y, k_z))
    return jnp.abs(x), y, z


def lanes_of(rows):
    return lax.broadcasted_iota(jnp.int32, (rows, LANES), 1)


def lower_z(values):
    z_place = lax.broadcasted_iota(jnp.int32, values.shape, 1) % NZ
    return jnp.where(z_place == 0, roll(values, 1 - NZ), roll(values, 1))


def upper_z(values):
    z_place = lax.broadcasted_iota(jnp.int32, values.shape, 1) % NZ
    return jnp.where(z_place == NZ - 1, roll(values, NZ - 1), roll(values, -1))


def picked(values, lanes):
    return jnp.take_along_axis(values, lanes, axis=1, mode="promise_in_bounds")


def pack_edge(packed, values, positive, chunk, lane):
    place = lane & (NZ - 1)
    edge = picked(values, jnp.where(positive, place + LANES - NZ, place))
    return jnp.where((lane >> 4) == chunk, edge, packed)


def edge_block(packed):
    return jnp.concatenate([packed, jnp.zeros((EDGE - CHUNK, LANES), F32)], axis=0).astype(BF16)


def prepare_kernel(
    flags, populations, solid, own, own_edge, message, straight, turned, masks, factors
):
    low, block, half = flags[0] == 1, flags[2], flags[3]
    ordered = reordered(order_matrix(low), populations[...])
    left, right = ordered[:, :LANES], ordered[:, LANES:]
    mine = jnp.where(half == 0, left, right)
    rest = jnp.where(half == 0, right, left)
    own[...] = mine
    edges = jnp.zeros((CHUNK, LANES), F32)
    sent = jnp.zeros((CHUNK, LANES), F32)
    lane = lanes_of(CHUNK)
    for chunk in range(PAD // CHUNK):
        rows = slice(CHUNK * chunk, CHUNK * (chunk + 1))
        x, y, z = signed_factors(block, chunk)
        factors[0, rows], factors[1, rows], factors[2, rows] = x, y, z
        positive = jnp.where(low, y, -y) > 0
        edges = pack_edge(edges, rest[rows], positive, chunk, lane)
        sent = pack_edge(sent, mine[rows], positive, chunk, lane)
    own_edge[...] = edges
    message[:PAD] = rest.astype(BF16)
    message[PAD:] = edge_block(sent)
    fluid = jnp.where(jnp.broadcast_to(solid[...], (8, 2 * LANES)) == 0, 1.0, 0.0)
    place = lax.broadcasted_iota(jnp.int32, (8, 2 * LANES), 0)
    found = jnp.zeros((8, 2 * LANES), F32)
    near = (fluid, roll(fluid, NZ), roll(fluid, -NZ), lower_z(fluid), upper_z(fluid))
    for index, value in enumerate(near):
        found = jnp.where(place == index, value, found)
    masks[...] = jnp.where(half == 0, found[:, :LANES], found[:, LANES:])
    row = lax.broadcasted_iota(jnp.int32, (16, LANES), 0)
    halves = []
    for side in range(2):
        cells = slice(LANES * side, LANES * (side + 1))
        open_cells = jnp.where(row == 0, jnp.broadcast_to(fluid[:1, cells], (16, LANES)), 0.0)
        halves.append((ordered[:, cells].astype(BF16), open_cells.astype(BF16)))
    for place, target in ((flags[5], straight), (1 - flags[5], turned)):
        for rows, low_value, high_value in zip((slice(0, PAD), slice(PAD, PAD + 16)), *halves):
            target[rows] = jnp.where(place == 0, low_value, high_value)


def rows_of(index, size):
    return slice(size * index, size * (index + 1))


def stream_part(part, sign, values, mirror, layer, edge, masks, open_x, factors):
    fluid, below_open_y, above_open_y, below_open_z, above_open_z = (
        jnp.broadcast_to(masks[i : i + 1], (CHUNK, LANES)) for i in range(5)
    )
    open_x = jnp.broadcast_to(open_x, (CHUNK, LANES))
    lane = lanes_of(CHUNK)
    z_place = lane & (NZ - 1)
    below_z = jnp.where(z_place == 0, lane + NZ - 1, lane - 1)
    above_z = jnp.where(z_place == NZ - 1, lane + 1 - NZ, lane + 1)
    below_y, above_y = (lane + LANES - NZ) & (LANES - 1), (lane + NZ) & (LANES - 1)
    results = []
    for index in range(2):
        chunk = 2 * part + index
        x, y, z = (factors[i, rows_of(chunk, CHUNK)] for i in range(3))
        up_y, up_z = y * sign > 0, z * sign > 0
        here, back = values[rows_of(index, CHUNK)], mirror[rows_of(index, CHUNK)]
        at_edge = jnp.where(up_y, lane, lane + NZ)
        put = picked(edge, (at_edge + NZ * chunk) & (LANES - 1))
        outside = (up_y & (lane < NZ)) | (~up_y & (lane >= LANES - NZ))
        near_y = jnp.where(outside, put, picked(here, jnp.where(up_y, below_y, above_y)))
        near_z = picked(here, jnp.where(up_z, below_z, above_z))
        upwind_x = jnp.where(open_x > 0, layer[rows_of(index, CHUNK)], back)
        upwind_y = jnp.where(jnp.where(up_y, below_open_y, above_open_y) > 0, near_y, back)
        upwind_z = jnp.where(jnp.where(up_z, below_open_z, above_open_z) > 0, near_z, back)
        outflow = x * (here - upwind_x)
        outflow += jnp.abs(y) * (here - upwind_y)
        outflow += jnp.abs(z) * (here - upwind_z)
        results.append((here - outflow) * fluid)
    return jnp.concatenate(results, axis=0)


def pack_part(packed, part, sign, values, factors):
    lane = lanes_of(CHUNK)
    for index in range(2):
        chunk = 2 * part + index
        positive = factors[1, rows_of(chunk, CHUNK)] * sign > 0
        packed = pack_edge(packed, values[rows_of(index, CHUNK)], positive, chunk, lane)
    return packed


def signs(flags):
    near = jnp.where(flags[1] == 1, 1.0, -1.0)
    return near, -near


def place_of_near(flags):
    return pl.multiple_of(PAD * (1 - flags[1]), 16), pl.multiple_of(PAD * flags[1], 16)


def first_kernel(
    flags, own, own_edge, received, straight, turned, masks_in, factors, lowered, masks_out, bands
):
    same = flags[4] == 1
    place = lax.broadcasted_iota(jnp.int32, (8, LANES), 0)
    open_own = straight[PAD:].astype(F32)[:1]
    open_other = turned[PAD:].astype(F32)[:1]
    masks = masks_in[...]
    masks = jnp.where(place == 5, jnp.where(same, open_own, open_other), masks)
    masks = jnp.where(place == 6, jnp.where(same, open_other, open_own), masks)
    masks_out[...] = masks
    edge_own, edge_other = own_edge[...], received[PAD:].astype(F32)[:CHUNK]
    sign = jnp.where(flags[0] == 1, 1.0, -1.0)
    low = flags[0] == 1
    group = lanes_of(PART) >> 5
    packed = [jnp.zeros((PART, LANES), F32)] * 2
    for part in range(PAD // PART):
        span = rows_of(part, PART)
        mine, theirs = own[span], received[span].astype(F32)
        new_own = stream_part(
            part, sign, mine, theirs, straight[span].astype(F32), edge_own, masks, open_own, factors
        )
        new_other = stream_part(
            part, -sign, theirs, mine, turned[span].astype(F32), edge_other, masks, open_other, factors
        )
        rows_a, rows_b = jnp.where(low, new_own, new_other), jnp.where(low, new_other, new_own)
        for index, rows in enumerate((rows_a, rows_b)):
            lowered[PAD * index + PART * part : PAD * index + PART * (part + 1)] = rows.astype(BF16)
            place = 2 * index + part // 2
            edge = roll(rows, NZ + 2 * NZ * place)
            packed[part % 2] = jnp.where(group == place, edge, packed[part % 2])
    for index in range(2):
        bands[rows_of(index, PART)] = packed[index].astype(BF16)


def streamed(flags, near, far, sibling, neighbour, edges, masks, factors):
    values = masks[...]
    edge_near, edge_far = (edges[rows_of(i, EDGE)].astype(F32)[:CHUNK] for i in range(2))
    sign_near, sign_far = signs(flags)
    start = pl.multiple_of(PAD * flags[1], 16)
    for part in range(PAD // PART):
        span = rows_of(part, PART)
        rows_near, rows_far = near[span], far[span]
        layer = sibling[pl.ds(start + PART * part, PART)].astype(F32)
        new_near = stream_part(
            part, sign_near, rows_near, rows_far, layer, edge_near, values, values[5:6], factors
        )
        layer = neighbour[span].astype(F32)
        new_far = stream_part(
            part, sign_far, rows_far, rows_near, layer, edge_far, values, values[6:7], factors
        )
        yield part, span, new_near, new_far


def between_near_kernel(flags, near, far, sibling, edges, masks, factors, rows_out, sent, packed_out):
    values = masks[...]
    sign = signs(flags)[0]
    start = pl.multiple_of(PAD * flags[1], 16)
    edge = edges[:EDGE].astype(F32)[:CHUNK]
    packed = jnp.zeros((CHUNK, LANES), F32)
    for part in range(PAD // PART):
        span = rows_of(part, PART)
        layer = sibling[pl.ds(start + PART * part, PART)].astype(F32)
        rows = stream_part(
            part, sign, near[span], far[span], layer, edge, values, values[5:6], factors
        )
        rows_out[span] = rows
        sent[span] = rows.astype(BF16)
        packed = pack_part(packed, part, sign, rows, factors)
    packed_out[...] = edge_block(packed)


def between_far_kernel(
    flags, near, far, neighbour, edges, masks, factors, packed_near, rows_out, sent, packed_out
):
    values = masks[...]
    sign = signs(flags)[1]
    edge = edges[EDGE:].astype(F32)[:CHUNK]
    packed = jnp.zeros((CHUNK, LANES), F32)
    for part in range(PAD // PART):
        span = rows_of(part, PART)
        layer = neighbour[span].astype(F32)
        rows = stream_part(
            part, sign, far[span], near[span], layer, edge, values, values[6:7], factors
        )
        rows_out[span] = rows
        sent[span] = rows.astype(BF16)
        packed = pack_part(packed, part, sign, rows, factors)
    packed_out[:EDGE] = packed_near[...]
    packed_out[EDGE:] = edge_block(packed)


def lower_kernel(flags, near, far, sibling, neighbour, edges, masks, factors, lowered):
    at_near, at_far = place_of_near(flags)
    for part, span, new_near, new_far in streamed(
        flags, near, far, sibling, neighbour, edges, masks, factors
    ):
        lowered[pl.ds(at_near + PART * part, PART)] = new_near.astype(BF16)
        lowered[pl.ds(at_far + PART * part, PART)] = new_far.astype(BF16)


def last_kernel(given, flags, near, far, sibling, neighbour, edges, masks, factors, out):
    same = (flags[4] == 1) != given
    values = masks[...]
    edge_near, edge_far = (edges[rows_of(i, EDGE)].astype(F32)[:CHUNK] for i in range(2))
    edge, open_x = jnp.where(same, edge_near, edge_far), jnp.where(same, values[5:6], values[6:7])
    sign = jnp.where((flags[0] == 1) != given, 1.0, -1.0)
    start = pl.multiple_of(PAD * flags[1], 16)
    results = []
    for part in range(PAD // PART):
        span = rows_of(part, PART)
        rows_near, rows_far = near[span], far[span]
        layer_near = sibling[pl.ds(start + PART * part, PART)].astype(F32)
        layer = jnp.where(same, layer_near, neighbour[span].astype(F32))
        rows, mirror = jnp.where(same, rows_near, rows_far), jnp.where(same, rows_far, rows_near)
        results.append(stream_part(part, sign, rows, mirror, layer, edge, values, open_x, factors))
    results = jnp.concatenate(results, axis=0)
    if given:
        out[...] = results.astype(BF16)
    else:
        out[...] = reordered(order_matrix(flags[0] == 1), results)


def dot(left, right):
    return jnp.dot(left, right, preferred_element_type=F32)


def pack_other(packed, part, sign, values, factors):
    lane = lanes_of(CHUNK)
    place = lane & (NZ - 1)
    for index in range(2):
        chunk = 2 * part + index
        positive = factors[1, rows_of(chunk, CHUNK)] * sign > 0
        edge = picked(values[rows_of(index, CHUNK)], jnp.where(positive, place, place + NZ))
        packed = jnp.where((lane >> 4) == chunk, edge, packed)
    return packed


def unpacked(bands):
    values = bands.astype(F32)
    return jnp.concatenate([roll(values, -2 * NZ * group) for group in range(4)], axis=0).astype(BF16)


def collide_kernel(
    flags, lowered, other, bands, other_bands, factors, m0, m1, m2, m3, rows_out, packed_out, all_rows, all_bands
):
    swapped = flags[2] == 1
    values = []
    for index, right in enumerate((swapped, ~swapped)):
        slot = jnp.where(flags[1] == 1, index, 1 - index)
        rows = jnp.where(right, other[...], lowered[...])
        all_rows[pl.ds(pl.multiple_of(2 * PAD * slot, 16), 2 * PAD)] = rows
        band = unpacked(jnp.where(right, other_bands[...], bands[...]))
        all_bands[pl.ds(pl.multiple_of(2 * PAD * slot, 16), 2 * PAD)] = band
        for side in range(2):
            span = rows_of(side, PAD)
            values.append(jnp.concatenate([rows[span], band[span]], axis=1))
    sign = jnp.where(flags[0] == 1, 1.0, -1.0)
    packed = jnp.zeros((CHUNK, LANES), F32)
    for part in range(PAD // PART):
        span = rows_of(part, PART)
        total = sum(dot(m[span], v) for m, v in zip((m0, m1, m2, m3), values))
        rows_out[span] = total[:, :LANES]
        packed = pack_other(packed, part, sign, total[:, LANES:], factors)
    packed_out[...] = edge_block(packed)


def give_rows(flags, part, rows_near, rows_far, factors, packed, outs):
    near, far, to_other_core, to_neighbour_chip = outs
    span = rows_of(part, PART)
    near[span], far[span] = rows_near, rows_far
    to_neighbour_chip[span] = rows_near.astype(BF16)
    to_other_core[span] = rows_far.astype(BF16)
    sign_near, sign_far = signs(flags)
    return (
        pack_part(packed[0], part, sign_near, rows_near, factors),
        pack_part(packed[1], part, sign_far, rows_far, factors),
    )


def give_product(flags, part, own, partner, factors, packed, outs):
    same = flags[4] == 1
    near, far = jnp.where(same, own, partner), jnp.where(same, partner, own)
    return give_rows(flags, part, near, far, factors, packed, outs)


def partner_product(flags, matrix, values, give):
    for index in range(PIECES):
        start = pl.multiple_of(PIECE * flags[6 + index], 8)
        give(pl.ds(start, PIECE), dot(matrix[rows_of(index, PIECE)], values))


def collide_partner_kernel(
    flags, own, own_packed, all_rows, all_bands, factors, mine, theirs,
    near, far, for_sibling, for_neighbour, edges, total,
):
    values = [
        jnp.concatenate([all_rows[rows_of(i, 2 * PAD)], all_bands[rows_of(i, 2 * PAD)]], axis=1)
        for i in range(2)
    ]
    for index in range(PIECES):
        start = pl.multiple_of(PIECE * flags[6 + index], 8)
        span = rows_of(index, PIECE)
        total[pl.ds(start, PIECE)] = dot(mine[span], values[0]) + dot(theirs[span], values[1])
    low, same = flags[0] == 1, flags[4] == 1
    sign = jnp.where(low, -1.0, 1.0)
    packed = jnp.zeros((CHUNK, LANES), F32)
    for part in range(PAD // PART):
        span = rows_of(part, PART)
        rows_own, rows_partner = own[span], total[span, :LANES]
        rows_near = jnp.where(same, rows_own, rows_partner)
        rows_far = jnp.where(same, rows_partner, rows_own)
        near[span], far[span] = rows_near, rows_far
        for_neighbour[span] = rows_near.astype(BF16)
        for_sibling[span] = rows_far.astype(BF16)
        packed = pack_other(packed, part, sign, total[span, LANES:], factors)
    packed_own, packed_partner = own_packed[...], edge_block(packed)
    edges[:EDGE] = jnp.where(same, packed_own, packed_partner)
    edges[EDGE:] = jnp.where(same, packed_partner, packed_own)


def half_products(flags, half_wanted, lowered, parts, mine, theirs, give_own, give_partner):
    values = lowered[...]
    for half in range(2):

        @pl.when(half_wanted == half)
        def _():
            for part in range(PAD // PART):
                span = rows_of(part, PART)
                total = dot(parts[2 * half][span], values[:PAD])
                give_own(span, total + dot(parts[2 * half + 1][span], values[PAD:]))

    core = 1 - flags[1]
    for held, here in ((mine, half_wanted == core), (theirs, half_wanted != core)):

        @pl.when(here)
        def _():
            partner_product(flags, held, values, give_partner)


def early_kernel(flags, lowered, m0, m1, m2, m3, mine, theirs, own_out, partner_out):
    def give_own(span, rows):
        own_out[span] = rows

    def give_partner(span, rows):
        partner_out[span] = rows

    half_products(flags, flags[2], lowered, (m0, m1, m2, m3), mine, theirs, give_own, give_partner)


def late_kernel(flags, other, own, partner, factors, m0, m1, m2, m3, mine, theirs, *refs):
    outs, (total_own, total_partner) = refs[:5], refs[5:]

    def give_own(span, rows):
        total_own[span] = own[span] + rows

    def give_partner(span, rows):
        total_partner[span] = partner[span] + rows

    half_products(flags, 1 - flags[2], other, (m0, m1, m2, m3), mine, theirs, give_own, give_partner)
    packed = (jnp.zeros((CHUNK, LANES), F32),) * 2
    for part in range(PAD // PART):
        span = rows_of(part, PART)
        packed = give_product(
            flags, part, total_own[span], total_partner[span], factors, packed, outs[:4]
        )
    outs[4][:EDGE], outs[4][EDGE:] = edge_block(packed[0]), edge_block(packed[1])


ROWS_F32 = ((PAD, LANES), F32)
PIECES_F32 = ((PIECES * PIECE, LANES), F32)


def finish_kernel(flags, kept, received, evolved):
    order = order_matrix(flags[0] == 1)
    rest = jnp.dot(order, received[...], preferred_element_type=F32)
    mine = kept[...]
    half = flags[3]
    evolved[:, 0, :LANES] = jnp.where(half == 0, mine, rest)[:ROWS]
    evolved[:, 0, LANES:] = jnp.where(half == 0, rest, mine)[:ROWS]


def place(rows, columns, wanted):
    return (lax.broadcasted_iota(jnp.int32, (rows, columns), 0) == wanted[None, :]).astype(BF16)


def chosen(left, right):
    return jnp.dot(left, right, preferred_element_type=BF16)


def column_half(wide, block):
    column = lax.iota(jnp.int32, PAD)
    inside = column < ROWS
    start_a, start_b = 640 * block, jnp.where(block == 1, 1280, 2048)
    part_a = lax.dynamic_slice(wide, (0, start_a), (wide.shape[0], 768))
    part_b = lax.dynamic_slice(wide, (0, start_b), (wide.shape[0], 896))
    wanted_a = jnp.where(inside, ROWS * block + column - start_a, -1)
    wanted_b = jnp.where(inside, 4 * ROWS - 1 - ROWS * block - column - start_b, -1)
    halves = chosen(part_a, place(768, PAD, wanted_a)), chosen(part_b, place(896, PAD, wanted_b))
    return halves


def padded_columns(matrix):
    return jnp.pad(matrix, ((0, 0), (0, 2944 - matrix.shape[1])))


def per_device(populations, solid_mask, collision):
    cell, vel = lax.axis_index("cells"), lax.axis_index("vel")
    low = (vel < 2).astype(jnp.int32)
    core, line, odd = cell % 2, cell // 32, cell // 2 % 2
    pieces = [2 * ((line + step) % 4) + (odd ^ other) for step in (0, 3, 1, 2) for other in range(2)]
    block = jnp.minimum(vel, 3 - vel)
    half = (1 - low) ^ (cell // RING % 2)
    needing = (cell + 1 - 2 * low) % 128
    straight_half = (1 - low) ^ (needing // RING % 2)
    same = (low != core).astype(jnp.int32)
    flags = jnp.stack([low, 1 - core, block, half, same, straight_half, *pieces])
    flags = flags.astype(jnp.int32)

    first_row = PIECE * pieces[0]
    row = first_row + lax.iota(jnp.int32, PIECE)
    start = jnp.clip(jnp.where(low == 1, first_row, ROWS - PIECE - first_row), 0, ROWS - PIECE)
    wanted = jnp.where(row < ROWS, jnp.where(low == 1, row, ROWS - 1 - row) - start, -1)
    window = lax.dynamic_slice(collision, (start, 0), (PIECE, collision.shape[1]))
    window = padded_columns(chosen(place(PIECE, PIECE, wanted).T, window))
    piece = jnp.concatenate(column_half(window, core), axis=1)
    populations, piece = lax.optimization_barrier((populations, piece))
    piece = to_mirror(piece)
    padded = jnp.pad(populations[:, 0, :], ((0, PAD - ROWS), (0, 0)))
    rows = (PAD, LANES)
    own, own_edge, message, straight, turned, masks, factors = call(
        prepare_kernel,
        [(rows, F32), ((CHUNK, LANES), F32), ((PAD + EDGE, LANES), BF16),
         ((PAD + 16, LANES), BF16), ((PAD + 16, LANES), BF16), ((8, LANES), F32), ((3, *rows), F32)],
        flags, padded, solid_mask, flops=2 * 3 * PAD * PAD * 256,
    )
    received = to_mirror(message)
    piece, straight, turned = lax.optimization_barrier((piece, straight, turned))
    pair = jnp.concatenate([piece, to_next_z(piece)], axis=0)
    straight, turned = to_layer(straight, False), to_layer(turned, True)

    row = lax.iota(jnp.int32, PAD)
    wanted = jnp.where(row < ROWS, jnp.where(low == 1, row, ROWS - 1 - row), -1)
    piece, collision = lax.optimization_barrier((piece, collision))
    ordered = padded_columns(chosen(place(ROWS, PAD, wanted).T, collision))

    pair, ordered = lax.optimization_barrier((pair, ordered))
    below, above = along_x(pair, 1), along_x(pair, -1)
    matrix = *column_half(ordered, 0), *column_half(ordered, 1)
    turned, *matrix = lax.optimization_barrier((turned, *matrix))
    lowered, masks, bands = call(
        first_kernel,
        [((2 * PAD, LANES), BF16), ((8, LANES), F32), ((BAND, LANES), BF16)],
        flags, own, own_edge, received, straight, turned, masks, factors, flops=100 * PAD * 256,
    )
    edges_shape = ((2 * EDGE, LANES), BF16)
    sends = [(rows, F32)] * 2 + [(rows, BF16)] * 2 + [edges_shape]
    multiply = 2 * PAD * 4 * PAD * LANES
    work = 100 * PAD * LANES

    below, above, lowered = lax.optimization_barrier((below, above, lowered))
    beyond = along_x(below[:PIECE], 1), along_x(above[PIECE:], -1)
    other = to_side(lowered)
    bands = to_mirror(bands), to_opposite(bands)
    wide = ((4 * PAD, LANES), BF16)
    own, own_packed, all_rows, all_bands = call(
        collide_kernel, [(rows, F32), ((EDGE, LANES), BF16), wide, wide],
        flags, lowered, other, *bands, factors, *matrix, flops=2 * multiply,
    )
    *beyond, own = lax.optimization_barrier((*beyond, own))
    mine = jnp.concatenate([pair, below, above, *beyond], axis=0)
    theirs = to_sibling(mine)
    near, far, for_sibling, for_neighbour, edges = call(
        collide_partner_kernel, sends,
        flags, own, own_packed, all_rows, all_bands, factors, mine, theirs,
        flops=2 * multiply, scratch=[((PIECES * PIECE, 2 * LANES), F32)],
    )

    for step in range(1, STEPS):
        neighbour, sibling = to_neighbour(for_neighbour), with_sibling(for_sibling)
        new_near, for_neighbour, packed = call(
            between_near_kernel, [(rows, F32), (rows, BF16), ((EDGE, LANES), BF16)],
            flags, near, far, sibling, edges, masks, factors, flops=work,
        )
        new_far, for_sibling, edges = call(
            between_far_kernel, [(rows, F32), (rows, BF16), edges_shape],
            flags, near, far, neighbour, edges, masks, factors, packed, flops=work,
        )
        near, far = new_near, new_far
        neighbour, edges = to_neighbour(for_neighbour), to_mirror(edges)
        sibling = with_sibling(for_sibling)
        (lowered,) = call(
            lower_kernel, [((2 * PAD, LANES), BF16)],
            flags, near, far, sibling, neighbour, edges, masks, factors, flops=work,
        )
        other = to_side(lowered)
        early = call(
            early_kernel, [ROWS_F32, PIECES_F32], flags, lowered, *matrix, mine, theirs, flops=multiply
        )
        near, far, for_sibling, for_neighbour, edges = call(
            late_kernel, sends, flags, other, *early, factors, *matrix, mine, theirs,
            flops=multiply, scratch=[ROWS_F32, PIECES_F32],
        )

    neighbour, edges = to_neighbour(for_neighbour), to_mirror(edges)
    sibling = with_sibling(for_sibling)
    last = flags, near, far, sibling, neighbour, edges, masks, factors
    (message,) = call(functools.partial(last_kernel, True), [(rows, BF16)], *last, flops=work)
    received = to_mirror(message)
    (kept,) = call(functools.partial(last_kernel, False), [(rows, F32)], *last, flops=multiply)
    (evolved,) = call(
        finish_kernel, [((ROWS, 1, 2 * LANES), F32)], flags, kept, received, flops=2 * PAD * PAD * LANES
    )
    return evolved


def solution(mesh):
    in_specs = (P("vel", "cells", None), P("cells", None), P("vel", None))
    out_specs = P("vel", "cells", None)
    return jax.shard_map(
        per_device, mesh=mesh, in_specs=in_specs, out_specs=out_specs, check_vma=False
    )
```

```python
import functools
import math

import jax
import jax.numpy as jnp
from jax import lax
from jax.experimental import pallas as pl
from jax.experimental.pallas import tpu as pltpu
from jax.sharding import PartitionSpec as P


K = 14
STEPS = 2
NZ = 16
BOTH = ("cells", "vel")
ROWS = 686
PAD = 704
CHUNK = 88
PART = 2 * CHUNK
EDGE = 96
LANES = 128
BAND = 4 * CHUNK
RING = 16
F32 = jnp.float32
BF16 = jnp.bfloat16
PARAMS = pltpu.CompilerParams(vmem_limit_bytes=20 * 1024 * 1024)


def pairs_of(target):
    pairs = []
    for cell in range(128):
        for part in range(4):
            to_cell, to_part = target(cell, part)
            pairs.append((cell * 4 + part, to_cell * 4 + to_part))
    return pairs


def with_sibling(array):
    groups = [[cell, cell + 1] for cell in range(0, 128, 2)]
    return lax.all_gather(array, "cells", axis=0, tiled=True, axis_index_groups=groups)


def to_layer(array, turned):
    def target(cell, part):
        return (cell - 1 if part < 2 else cell + 1) % 128, 3 - part if turned else part

    return lax.ppermute(array, BOTH, pairs_of(target))


def neighbour_of(cell, part):
    other = (cell - 1 if cell % 2 == 0 else cell + 1) % 128
    return other, part if (other // RING) % 2 == (cell // RING) % 2 else 3 - part


def to_neighbour(array):
    return lax.ppermute(array, BOTH, pairs_of(neighbour_of))


def to_mirror(array):
    return lax.ppermute(array, "vel", [(i, 3 - i) for i in range(4)])


def to_opposite(array):
    return lax.ppermute(array, "vel", [(i, i ^ 2) for i in range(4)])


def to_side(array):
    return lax.ppermute(array, "vel", [(i, i ^ 1) for i in range(4)])


def call(kernel, outs, flags, *arrays, flops=0, stay=0, scratch=(), leave=False):
    moved = sum(x.size * x.dtype.itemsize for x in arrays)
    moved += sum(math.prod(shape) * jnp.dtype(dtype).itemsize for shape, dtype in outs)
    vmem, hbm = (pl.BlockSpec(memory_space=space) for space in (pltpu.VMEM, pltpu.HBM))
    count = len(arrays) - stay
    specs = [vmem] * count + [hbm] * stay
    arrays = *arrays[:count], *(pltpu.with_memory_space_constraint(x, pltpu.HBM) for x in arrays[count:])
    return pl.pallas_call(
        kernel,
        out_shape=[(pltpu.HBM if leave else jax.ShapeDtypeStruct)(shape, dtype) for shape, dtype in outs],
        in_specs=[pl.BlockSpec(memory_space=pltpu.SMEM)] + specs,
        out_specs=[vmem] * len(outs),
        scratch_shapes=scratch,
        compiler_params=PARAMS,
        cost_estimate=pl.CostEstimate(flops=flops, bytes_accessed=moved, transcendentals=0),
    )(flags, *arrays)


def roll(values, shift):
    return pltpu.roll(values, shift % values.shape[1], 1)


def order_matrix(low):
    row = lax.broadcasted_iota(jnp.int32, (PAD, PAD), 0)
    column = lax.broadcasted_iota(jnp.int32, (PAD, PAD), 1)
    wanted = jnp.where(low, row, ROWS - 1 - row)
    return jnp.where((column == wanted) & (row < ROWS), 1.0, 0.0).astype(BF16)


def reordered(order, values):
    total = jnp.zeros(values.shape, F32)
    for _ in range(3):
        part = values.astype(BF16)
        total += jnp.dot(order, part, preferred_element_type=F32)
        values = values - part.astype(F32)
    return total


def signed_factors(block, chunk):
    row = CHUNK * chunk + lax.broadcasted_iota(jnp.int32, (CHUNK, LANES), 0)
    ids = ROWS * block + row
    upper = (ids * 4682) >> 16
    k_z = ids - K * upper
    k_x = (upper * 4682) >> 16
    k_y = upper - K * k_x
    centre = (K - 1) / 2.0
    x, y, z = ((k.astype(F32) - centre) * (0.3 / centre) for k in (k_x, k_y, k_z))
    return jnp.abs(x), y, z


def lanes_of(rows):
    return lax.broadcasted_iota(jnp.int32, (rows, LANES), 1)


def lower_z(values):
    z_place = lax.broadcasted_iota(jnp.int32, values.shape, 1) % NZ
    return jnp.where(z_place == 0, roll(values, 1 - NZ), roll(values, 1))


def upper_z(values):
    z_place = lax.broadcasted_iota(jnp.int32, values.shape, 1) % NZ
    return jnp.where(z_place == NZ - 1, roll(values, NZ - 1), roll(values, -1))


def picked(values, lanes):
    return jnp.take_along_axis(values, lanes, axis=1, mode="promise_in_bounds")


def pack_edge(packed, values, positive, chunk, lane):
    place = lane & (NZ - 1)
    edge = picked(values, jnp.where(positive, place + LANES - NZ, place))
    return jnp.where((lane >> 4) == chunk, edge, packed)


def edge_block(packed):
    return jnp.concatenate([packed, jnp.zeros((EDGE - CHUNK, LANES), F32)], axis=0).astype(BF16)


def prepare_kernel(
    flags, populations, solid, own, own_edge, message, straight, turned, masks, factors
):
    low, block, half = flags[0] == 1, flags[2], flags[3]
    ordered = reordered(order_matrix(low), populations[...])
    left, right = ordered[:, :LANES], ordered[:, LANES:]
    mine = jnp.where(half == 0, left, right)
    rest = jnp.where(half == 0, right, left)
    own[...] = mine
    edges = jnp.zeros((CHUNK, LANES), F32)
    sent = jnp.zeros((CHUNK, LANES), F32)
    lane = lanes_of(CHUNK)
    for chunk in range(PAD // CHUNK):
        rows = slice(CHUNK * chunk, CHUNK * (chunk + 1))
        x, y, z = signed_factors(block, chunk)
        factors[0, rows], factors[1, rows], factors[2, rows] = x, y, z
        positive = jnp.where(low, y, -y) > 0
        edges = pack_edge(edges, rest[rows], positive, chunk, lane)
        sent = pack_edge(sent, mine[rows], positive, chunk, lane)
    own_edge[...] = edges
    message[:PAD] = rest.astype(BF16)
    message[PAD:] = edge_block(sent)
    fluid = jnp.where(jnp.broadcast_to(solid[...], (8, 2 * LANES)) == 0, 1.0, 0.0)
    place = lax.broadcasted_iota(jnp.int32, (8, 2 * LANES), 0)
    found = jnp.zeros((8, 2 * LANES), F32)
    near = (fluid, roll(fluid, NZ), roll(fluid, -NZ), lower_z(fluid), upper_z(fluid))
    for index, value in enumerate(near):
        found = jnp.where(place == index, value, found)
    masks[...] = jnp.where(half == 0, found[:, :LANES], found[:, LANES:])
    row = lax.broadcasted_iota(jnp.int32, (16, LANES), 0)
    halves = []
    for side in range(2):
        cells = slice(LANES * side, LANES * (side + 1))
        open_cells = jnp.where(row == 0, jnp.broadcast_to(fluid[:1, cells], (16, LANES)), 0.0)
        halves.append((ordered[:, cells].astype(BF16), open_cells.astype(BF16)))
    for place, target in ((flags[5], straight), (1 - flags[5], turned)):
        for rows, low_value, high_value in zip((slice(0, PAD), slice(PAD, PAD + 16)), *halves):
            target[rows] = jnp.where(place == 0, low_value, high_value)


def rows_of(index, size):
    return slice(size * index, size * (index + 1))


def stream_part(part, sign, values, mirror, layer, edge, masks, open_x, factors):
    fluid, below_open_y, above_open_y, below_open_z, above_open_z = (
        jnp.broadcast_to(masks[i : i + 1], (CHUNK, LANES)) for i in range(5)
    )
    open_x = jnp.broadcast_to(open_x, (CHUNK, LANES))
    lane = lanes_of(CHUNK)
    z_place = lane & (NZ - 1)
    below_z = jnp.where(z_place == 0, lane + NZ - 1, lane - 1)
    above_z = jnp.where(z_place == NZ - 1, lane + 1 - NZ, lane + 1)
    below_y, above_y = (lane + LANES - NZ) & (LANES - 1), (lane + NZ) & (LANES - 1)
    results = []
    for index in range(2):
        chunk = 2 * part + index
        x, y, z = (factors[i, rows_of(chunk, CHUNK)] for i in range(3))
        up_y, up_z = y * sign > 0, z * sign > 0
        here, back = values[rows_of(index, CHUNK)], mirror[rows_of(index, CHUNK)]
        at_edge = jnp.where(up_y, lane, lane + NZ)
        put = picked(edge, (at_edge + NZ * chunk) & (LANES - 1))
        outside = (up_y & (lane < NZ)) | (~up_y & (lane >= LANES - NZ))
        near_y = jnp.where(outside, put, picked(here, jnp.where(up_y, below_y, above_y)))
        near_z = picked(here, jnp.where(up_z, below_z, above_z))
        upwind_x = jnp.where(open_x > 0, layer[rows_of(index, CHUNK)], back)
        upwind_y = jnp.where(jnp.where(up_y, below_open_y, above_open_y) > 0, near_y, back)
        upwind_z = jnp.where(jnp.where(up_z, below_open_z, above_open_z) > 0, near_z, back)
        outflow = x * (here - upwind_x)
        outflow += jnp.abs(y) * (here - upwind_y)
        outflow += jnp.abs(z) * (here - upwind_z)
        results.append((here - outflow) * fluid)
    return jnp.concatenate(results, axis=0)


def pack_part(packed, part, sign, values, factors):
    lane = lanes_of(CHUNK)
    for index in range(2):
        chunk = 2 * part + index
        positive = factors[1, rows_of(chunk, CHUNK)] * sign > 0
        packed = pack_edge(packed, values[rows_of(index, CHUNK)], positive, chunk, lane)
    return packed


def signs(flags):
    near = jnp.where(flags[1] == 1, 1.0, -1.0)
    return near, -near


def place_of_near(flags):
    return pl.multiple_of(PAD * (1 - flags[1]), 16), pl.multiple_of(PAD * flags[1], 16)


def first_kernel(
    flags, own, own_edge, received, straight, turned, masks_in, factors, lowered, masks_out, bands
):
    same = flags[4] == 1
    place = lax.broadcasted_iota(jnp.int32, (8, LANES), 0)
    open_own = straight[PAD:].astype(F32)[:1]
    open_other = turned[PAD:].astype(F32)[:1]
    masks = masks_in[...]
    masks = jnp.where(place == 5, jnp.where(same, open_own, open_other), masks)
    masks = jnp.where(place == 6, jnp.where(same, open_other, open_own), masks)
    masks_out[...] = masks
    edge_own, edge_other = own_edge[...], received[PAD:].astype(F32)[:CHUNK]
    sign = jnp.where(flags[0] == 1, 1.0, -1.0)
    low = flags[0] == 1
    group = lanes_of(PART) >> 5
    packed = [jnp.zeros((PART, LANES), F32)] * 2
    for part in range(PAD // PART):
        span = rows_of(part, PART)
        mine, theirs = own[span], received[span].astype(F32)
        new_own = stream_part(
            part, sign, mine, theirs, straight[span].astype(F32), edge_own, masks, open_own, factors
        )
        new_other = stream_part(
            part, -sign, theirs, mine, turned[span].astype(F32), edge_other, masks, open_other, factors
        )
        rows_a, rows_b = jnp.where(low, new_own, new_other), jnp.where(low, new_other, new_own)
        for index, rows in enumerate((rows_a, rows_b)):
            lowered[PAD * index + PART * part : PAD * index + PART * (part + 1)] = rows.astype(BF16)
            place = 2 * index + part // 2
            edge = roll(rows, NZ + 2 * NZ * place)
            packed[part % 2] = jnp.where(group == place, edge, packed[part % 2])
    for index in range(2):
        bands[rows_of(index, PART)] = packed[index].astype(BF16)


def streamed(flags, near, far, sibling, neighbour, edges, masks, factors):
    values = masks[...]
    edge_near, edge_far = (edges[rows_of(i, EDGE)].astype(F32)[:CHUNK] for i in range(2))
    sign_near, sign_far = signs(flags)
    start = pl.multiple_of(PAD * flags[1], 16)
    for part in range(PAD // PART):
        span = rows_of(part, PART)
        rows_near, rows_far = near[span], far[span]
        layer = sibling[pl.ds(start + PART * part, PART)].astype(F32)
        new_near = stream_part(
            part, sign_near, rows_near, rows_far, layer, edge_near, values, values[5:6], factors
        )
        layer = neighbour[span].astype(F32)
        new_far = stream_part(
            part, sign_far, rows_far, rows_near, layer, edge_far, values, values[6:7], factors
        )
        yield part, span, new_near, new_far


def between_near_kernel(flags, near, far, sibling, edges, masks, factors, rows_out, sent, packed_out):
    values = masks[...]
    sign = signs(flags)[0]
    start = pl.multiple_of(PAD * flags[1], 16)
    edge = edges[:EDGE].astype(F32)[:CHUNK]
    packed = jnp.zeros((CHUNK, LANES), F32)
    for part in range(PAD // PART):
        span = rows_of(part, PART)
        layer = sibling[pl.ds(start + PART * part, PART)].astype(F32)
        rows = stream_part(
            part, sign, near[span], far[span], layer, edge, values, values[5:6], factors
        )
        rows_out[span] = rows
        sent[span] = rows.astype(BF16)
        packed = pack_part(packed, part, sign, rows, factors)
    packed_out[...] = edge_block(packed)


def between_far_kernel(
    flags, near, far, neighbour, edges, masks, factors, packed_near, rows_out, sent, packed_out
):
    values = masks[...]
    sign = signs(flags)[1]
    edge = edges[EDGE:].astype(F32)[:CHUNK]
    packed = jnp.zeros((CHUNK, LANES), F32)
    for part in range(PAD // PART):
        span = rows_of(part, PART)
        layer = neighbour[span].astype(F32)
        rows = stream_part(
            part, sign, far[span], near[span], layer, edge, values, values[6:7], factors
        )
        rows_out[span] = rows
        sent[span] = rows.astype(BF16)
        packed = pack_part(packed, part, sign, rows, factors)
    packed_out[:EDGE] = packed_near[...]
    packed_out[EDGE:] = edge_block(packed)


def lower_kernel(flags, near, far, sibling, neighbour, edges, masks, factors, lowered):
    at_near, at_far = place_of_near(flags)
    for part, span, new_near, new_far in streamed(
        flags, near, far, sibling, neighbour, edges, masks, factors
    ):
        lowered[pl.ds(at_near + PART * part, PART)] = new_near.astype(BF16)
        lowered[pl.ds(at_far + PART * part, PART)] = new_far.astype(BF16)


def last_kernel(given, flags, near, far, sibling, neighbour, edges, masks, factors, out):
    same = (flags[4] == 1) != given
    values = masks[...]
    edge_near, edge_far = (edges[rows_of(i, EDGE)].astype(F32)[:CHUNK] for i in range(2))
    edge, open_x = jnp.where(same, edge_near, edge_far), jnp.where(same, values[5:6], values[6:7])
    sign = jnp.where((flags[0] == 1) != given, 1.0, -1.0)
    start = pl.multiple_of(PAD * flags[1], 16)
    results = []
    for part in range(PAD // PART):
        span = rows_of(part, PART)
        rows_near, rows_far = near[span], far[span]
        layer_near = sibling[pl.ds(start + PART * part, PART)].astype(F32)
        layer = jnp.where(same, layer_near, neighbour[span].astype(F32))
        rows, mirror = jnp.where(same, rows_near, rows_far), jnp.where(same, rows_far, rows_near)
        results.append(stream_part(part, sign, rows, mirror, layer, edge, values, open_x, factors))
    results = jnp.concatenate(results, axis=0)
    if given:
        out[...] = results.astype(BF16)
    else:
        out[...] = reordered(order_matrix(flags[0] == 1), results)


def dot(left, right):
    return jnp.dot(left, right, preferred_element_type=F32)


def pack_other(packed, part, sign, values, factors):
    lane = lanes_of(CHUNK)
    place = lane & (NZ - 1)
    for index in range(2):
        chunk = 2 * part + index
        positive = factors[1, rows_of(chunk, CHUNK)] * sign > 0
        edge = picked(values[rows_of(index, CHUNK)], jnp.where(positive, place, place + NZ))
        packed = jnp.where((lane >> 4) == chunk, edge, packed)
    return packed


def unpacked(bands):
    values = bands.astype(F32)
    return jnp.concatenate([roll(values, -2 * NZ * group) for group in range(4)], axis=0).astype(BF16)


def collide_kernel(
    flags, lowered, other, bands, other_bands, factors, m0, m1, m2, m3, rows_out, packed_out, all_rows, all_bands
):
    swapped = flags[2] == 1
    for index, right in enumerate((swapped, ~swapped)):
        all_rows[rows_of(index, 2 * PAD)] = jnp.where(right, other[...], lowered[...])
        all_bands[rows_of(index, BAND)] = jnp.where(right, other_bands[...], bands[...])
    values = []
    for index in range(2):
        rows, band = all_rows[rows_of(index, 2 * PAD)], unpacked(all_bands[rows_of(index, BAND)])
        for side in range(2):
            span = rows_of(side, PAD)
            values.append(jnp.concatenate([rows[span], band[span]], axis=1))
    sign = jnp.where(flags[0] == 1, 1.0, -1.0)
    packed = jnp.zeros((CHUNK, LANES), F32)
    for part in range(PAD // PART):
        span = rows_of(part, PART)
        total = sum(dot(m[span], v) for m, v in zip((m0, m1, m2, m3), values))
        rows_out[span] = total[:, :LANES]
        packed = pack_other(packed, part, sign, total[:, LANES:], factors)
    packed_out[...] = edge_block(packed)


def give_rows(flags, part, rows_near, rows_far, factors, packed, outs):
    near, far, to_other_core, to_neighbour_chip = outs
    span = rows_of(part, PART)
    near[span], far[span] = rows_near, rows_far
    to_neighbour_chip[span] = rows_near.astype(BF16)
    to_other_core[span] = rows_far.astype(BF16)
    sign_near, sign_far = signs(flags)
    return (
        pack_part(packed[0], part, sign_near, rows_near, factors),
        pack_part(packed[1], part, sign_far, rows_far, factors),
    )


def give_product(flags, part, own, partner, factors, packed, outs):
    same = flags[4] == 1
    near, far = jnp.where(same, own, partner), jnp.where(same, partner, own)
    return give_rows(flags, part, near, far, factors, packed, outs)


def collide_partner_kernel(
    flags, factors, own_packed, all_rows, all_bands, own, matrix,
    near, far, for_sibling, for_neighbour, edges,
    held, held_rows, held_bands, held_own, held_packed, done,
):
    small = [
        pltpu.make_async_copy(source, target, done.at[index])
        for index, (source, target) in enumerate(
            ((all_rows, held_rows), (all_bands, held_bands), (own, held_own), (own_packed, held_packed))
        )
    ]
    parts = PAD // PART
    pieces = [
        [
            pltpu.make_async_copy(
                matrix.at[rows_of(parts * half + part, PART)],
                held.at[rows_of(parts * half + part, PART)],
                done.at[4 + parts * half + part],
            )
            for half in range(2)
        ]
        for part in range(parts)
    ]
    for copy in small[:2] + sum(pieces, []) + small[2:]:
        copy.start()
    for copy in small[:2]:
        copy.wait()
    low, same = flags[0] == 1, flags[4] == 1
    values = []
    for index in range(2):
        band = unpacked(held_bands[rows_of(index, BAND)])
        values.append(jnp.concatenate([held_rows[rows_of(index, 2 * PAD)], band], axis=1))
    sign = jnp.where(low, -1.0, 1.0)
    packed = jnp.zeros((CHUNK, LANES), F32)
    for part in range(parts):
        span = rows_of(part, PART)
        total = 0.0
        for half in range(2):
            pieces[part][half].wait()
            total += dot(held[rows_of(parts * half + part, PART)], values[half])
        if part == 0:
            for copy in small[2:]:
                copy.wait()
        mine, theirs = held_own[span], total[:, :LANES]
        rows_near, rows_far = jnp.where(same, mine, theirs), jnp.where(same, theirs, mine)
        near[span], far[span] = rows_near, rows_far
        for_neighbour[span] = rows_near.astype(BF16)
        for_sibling[span] = rows_far.astype(BF16)
        packed = pack_other(packed, part, sign, total[:, LANES:], factors)
    mine, theirs = held_packed[...], edge_block(packed)
    edges[:EDGE] = jnp.where(same, mine, theirs)
    edges[EDGE:] = jnp.where(same, theirs, mine)


def early_kernel(
    flags, lowered, m0, m1, m2, m3, matrix, own_out, partner_out, next_own, next_partner,
    held_own, held_partner, done,
):
    values = lowered[...]
    parts = m0, m1, m2, m3
    for half in range(2):

        @pl.when(flags[2] == half)
        def _():
            copies = [
                pltpu.make_async_copy(
                    matrix.at[rows_of(half, PAD)], held_partner, done.at[0]
                )
            ]
            for i in range(2):
                copies.append(pltpu.make_async_copy(parts[2 * half + i], held_own.at[i], done.at[1 + i]))
            copies.append(
                pltpu.make_async_copy(matrix.at[rows_of(1 - half, PAD)], next_partner, done.at[3])
            )
            for i in range(2):
                source = parts[2 * (1 - half) + i]
                copies.append(pltpu.make_async_copy(source, next_own.at[i], done.at[4 + i]))
            for copy in copies:
                copy.start()
            copies[0].wait()
            for part in range(PAD // PART):
                span = rows_of(part, PART)
                partner_out[span] = dot(held_partner[span], values)
            copies[1].wait()
            copies[2].wait()
            for part in range(PAD // PART):
                span = rows_of(part, PART)
                own_out[span] = dot(held_own[0, span], values[:PAD]) + dot(held_own[1, span], values[PAD:])
            for copy in copies[3:]:
                copy.wait()


def late_kernel(flags, other, own, partner, factors, matrix_own, matrix_partner, *outs):
    values = other[...]
    packed = (jnp.zeros((CHUNK, LANES), F32),) * 2
    for part in range(PAD // PART):
        span = rows_of(part, PART)
        more_own = dot(matrix_own[0, span], values[:PAD]) + dot(matrix_own[1, span], values[PAD:])
        more_partner = dot(matrix_partner[span], values)
        packed = give_product(
            flags, part, own[span] + more_own, partner[span] + more_partner, factors, packed, outs[:4]
        )
    outs[4][:EDGE], outs[4][EDGE:] = edge_block(packed[0]), edge_block(packed[1])


ROWS_F32 = ((PAD, LANES), F32)
PARTNER_SCRATCH = [
    pltpu.VMEM((2 * PAD, 2 * PAD), BF16),
    pltpu.VMEM((4 * PAD, LANES), BF16),
    pltpu.VMEM((2 * BAND, LANES), BF16),
    pltpu.VMEM((PAD, LANES), F32),
    pltpu.VMEM((EDGE, LANES), BF16),
    pltpu.SemaphoreType.DMA((12,)),
]
HELD = [pltpu.VMEM((2, PAD, PAD), BF16), pltpu.VMEM((PAD, 2 * PAD), BF16)]
EARLY = [ROWS_F32, ROWS_F32, ((2, PAD, PAD), BF16), ((PAD, 2 * PAD), BF16)]
EARLY_SCRATCH = HELD + [pltpu.SemaphoreType.DMA((6,))]


def finish_kernel(flags, kept, received, evolved):
    order = order_matrix(flags[0] == 1)
    rest = jnp.dot(order, received[...], preferred_element_type=F32)
    mine = kept[...]
    half = flags[3]
    evolved[:, 0, :LANES] = jnp.where(half == 0, mine, rest)[:ROWS]
    evolved[:, 0, LANES:] = jnp.where(half == 0, rest, mine)[:ROWS]


def place(rows, columns, wanted):
    return (lax.broadcasted_iota(jnp.int32, (rows, columns), 0) == wanted[None, :]).astype(BF16)


def chosen(left, right):
    return jnp.dot(left, right, preferred_element_type=BF16)


def column_half(wide, block):
    column = lax.iota(jnp.int32, PAD)
    inside = column < ROWS
    start_a, start_b = 640 * block, jnp.where(block == 1, 1280, 2048)
    part_a = lax.dynamic_slice(wide, (0, start_a), (wide.shape[0], 768))
    part_b = lax.dynamic_slice(wide, (0, start_b), (wide.shape[0], 896))
    wanted_a = jnp.where(inside, ROWS * block + column - start_a, -1)
    wanted_b = jnp.where(inside, 4 * ROWS - 1 - ROWS * block - column - start_b, -1)
    halves = chosen(part_a, place(768, PAD, wanted_a)), chosen(part_b, place(896, PAD, wanted_b))
    return halves


def padded_columns(matrix):
    return jnp.pad(matrix, ((0, 0), (0, 2944 - matrix.shape[1])))


def per_device(populations, solid_mask, collision):
    cell, vel = lax.axis_index("cells"), lax.axis_index("vel")
    low = (vel < 2).astype(jnp.int32)
    core, ring_place = cell % 2, cell // 32 + 4 * (cell // 2 % 2)
    block = jnp.minimum(vel, 3 - vel)
    half = (1 - low) ^ (cell // RING % 2)
    needing = (cell + 1 - 2 * low) % 128
    straight_half = (1 - low) ^ (needing // RING % 2)
    same = (low != core).astype(jnp.int32)
    flags = jnp.stack([low, 1 - core, block, half, same, straight_half])
    flags = flags.astype(jnp.int32)

    first_row = CHUNK * ring_place
    row = first_row + lax.iota(jnp.int32, CHUNK)
    start = jnp.clip(jnp.where(low == 1, first_row, ROWS - CHUNK - first_row), 0, ROWS - CHUNK)
    wanted = jnp.where(row < ROWS, jnp.where(low == 1, row, ROWS - 1 - row) - start, -1)
    window = lax.dynamic_slice(collision, (start, 0), (CHUNK, collision.shape[1]))
    window = padded_columns(chosen(place(CHUNK, CHUNK, wanted).T, window))
    piece = jnp.concatenate(column_half(window, core), axis=1)
    populations, piece = lax.optimization_barrier((populations, piece))
    piece = to_mirror(piece)

    padded = jnp.pad(populations[:, 0, :], ((0, PAD - ROWS), (0, 0)))
    rows = (PAD, LANES)
    own, own_edge, message, straight, turned, masks, factors = call(
        prepare_kernel,
        [(rows, F32), ((CHUNK, LANES), F32), ((PAD + EDGE, LANES), BF16),
         ((PAD + 16, LANES), BF16), ((PAD + 16, LANES), BF16), ((8, LANES), F32), ((3, *rows), F32)],
        flags, padded, solid_mask, flops=2 * 3 * PAD * PAD * 256,
    )
    piece, _ = lax.optimization_barrier((piece, message))
    groups = [
        [x * 32 + y * 16 + 4 * pair + 2 * odd + side for side in range(2) for odd in range(2) for x in range(4)]
        for y in range(2)
        for pair in range(4)
    ]
    partner_matrix = lax.all_gather(piece, "cells", axis=0, tiled=True, axis_index_groups=groups)
    turned = to_layer(turned, True)
    received = to_mirror(message)

    row = lax.iota(jnp.int32, PAD)
    wanted = jnp.where(row < ROWS, jnp.where(low == 1, row, ROWS - 1 - row), -1)
    message, collision = lax.optimization_barrier((message, collision))
    ordered = padded_columns(chosen(place(ROWS, PAD, wanted).T, collision))

    straight, ordered = lax.optimization_barrier((straight, ordered))
    straight = to_layer(straight, False)
    matrix = *column_half(ordered, 0), *column_half(ordered, 1)
    turned, *matrix = lax.optimization_barrier((turned, *matrix))
    lowered, masks, bands = call(
        first_kernel,
        [((2 * PAD, LANES), BF16), ((8, LANES), F32), ((BAND, LANES), BF16)],
        flags, own, own_edge, received, straight, turned, masks, factors, flops=100 * PAD * 256,
    )
    edges_shape = ((2 * EDGE, LANES), BF16)
    sends = [(rows, F32)] * 2 + [(rows, BF16)] * 2 + [edges_shape]
    multiply = 2 * PAD * 4 * PAD * LANES
    work = 100 * PAD * LANES

    other = to_side(lowered)
    bands = to_mirror(bands), to_opposite(bands)
    own, own_packed, all_rows, all_bands = call(
        collide_kernel,
        [(rows, F32), ((EDGE, LANES), BF16), ((4 * PAD, LANES), BF16), ((2 * BAND, LANES), BF16)],
        flags, lowered, other, *bands, factors, *matrix, flops=2 * multiply, leave=True,
    )
    partner_matrix, own = lax.optimization_barrier((partner_matrix, own))
    near, far, for_sibling, for_neighbour, edges = call(
        collide_partner_kernel, sends, flags, factors, own_packed, all_rows, all_bands, own, partner_matrix,
        flops=2 * multiply, stay=5, scratch=PARTNER_SCRATCH,
    )

    for step in range(1, STEPS):
        neighbour, sibling = to_neighbour(for_neighbour), with_sibling(for_sibling)
        new_near, for_neighbour, packed = call(
            between_near_kernel, [(rows, F32), (rows, BF16), ((EDGE, LANES), BF16)],
            flags, near, far, sibling, edges, masks, factors, flops=work,
        )
        new_far, for_sibling, edges = call(
            between_far_kernel, [(rows, F32), (rows, BF16), edges_shape],
            flags, near, far, neighbour, edges, masks, factors, packed, flops=work,
        )
        near, far = new_near, new_far
        neighbour, edges = to_neighbour(for_neighbour), to_mirror(edges)
        sibling = with_sibling(for_sibling)
        (lowered,) = call(
            lower_kernel, [((2 * PAD, LANES), BF16)],
            flags, near, far, sibling, neighbour, edges, masks, factors, flops=work,
        )
        other = to_side(lowered)
        early = call(
            early_kernel, EARLY, flags, lowered, *matrix, partner_matrix,
            flops=multiply, stay=5, scratch=EARLY_SCRATCH,
        )
        near, far, for_sibling, for_neighbour, edges = call(
            late_kernel, sends, flags, other, *early[:2], factors, *early[2:], flops=multiply
        )

    neighbour, edges = to_neighbour(for_neighbour), to_mirror(edges)
    sibling = with_sibling(for_sibling)
    last = flags, near, far, sibling, neighbour, edges, masks, factors
    (message,) = call(functools.partial(last_kernel, True), [(rows, BF16)], *last, flops=work)
    received = to_mirror(message)
    (kept,) = call(functools.partial(last_kernel, False), [(rows, F32)], *last, flops=multiply)
    (evolved,) = call(
        finish_kernel, [((ROWS, 1, 2 * LANES), F32)], flags, kept, received, flops=2 * PAD * PAD * LANES
    )
    return evolved


def solution(mesh):
    in_specs = (P("vel", "cells", None), P("cells", None), P("vel", None))
    out_specs = P("vel", "cells", None)
    return jax.shard_map(
        per_device, mesh=mesh, in_specs=in_specs, out_specs=out_specs, check_vma=False
    )
```

```python
import functools
import math

import jax
import jax.numpy as jnp
from jax import lax
from jax.experimental import pallas as pl
from jax.experimental.pallas import tpu as pltpu
from jax.sharding import PartitionSpec as P


K = 14
STEPS = 2
NZ = 16
BOTH = ("cells", "vel")
ROWS = 686
PAD = 704
CHUNK = 88
PART = 2 * CHUNK
EDGE = 96
LANES = 128
BAND = 4 * CHUNK
RING = 16
F32 = jnp.float32
BF16 = jnp.bfloat16
PARAMS = pltpu.CompilerParams(vmem_limit_bytes=20 * 1024 * 1024)


def pairs_of(target):
    pairs = []
    for cell in range(128):
        for part in range(4):
            to_cell, to_part = target(cell, part)
            pairs.append((cell * 4 + part, to_cell * 4 + to_part))
    return pairs


def with_sibling(array):
    groups = [[cell, cell + 1] for cell in range(0, 128, 2)]
    return lax.all_gather(array, "cells", axis=0, tiled=True, axis_index_groups=groups)


def to_layer(array, turned):
    def target(cell, part):
        return (cell - 1 if part < 2 else cell + 1) % 128, 3 - part if turned else part

    return lax.ppermute(array, BOTH, pairs_of(target))


def neighbour_of(cell, part):
    other = (cell - 1 if cell % 2 == 0 else cell + 1) % 128
    return other, part if (other // RING) % 2 == (cell // RING) % 2 else 3 - part


def to_neighbour(array):
    return lax.ppermute(array, BOTH, pairs_of(neighbour_of))


def to_mirror(array):
    return lax.ppermute(array, "vel", [(i, 3 - i) for i in range(4)])


def to_opposite(array):
    return lax.ppermute(array, "vel", [(i, i ^ 2) for i in range(4)])


def to_side(array):
    return lax.ppermute(array, "vel", [(i, i ^ 1) for i in range(4)])


def call(kernel, outs, flags, *arrays, flops=0, stay=0, scratch=(), leave=False):
    moved = sum(x.size * x.dtype.itemsize for x in arrays)
    moved += sum(math.prod(shape) * jnp.dtype(dtype).itemsize for shape, dtype in outs)
    vmem, hbm = (pl.BlockSpec(memory_space=space) for space in (pltpu.VMEM, pltpu.HBM))
    count = len(arrays) - stay
    specs = [vmem] * count + [hbm] * stay
    arrays = *arrays[:count], *(pltpu.with_memory_space_constraint(x, pltpu.HBM) for x in arrays[count:])
    return pl.pallas_call(
        kernel,
        out_shape=[(pltpu.HBM if leave else jax.ShapeDtypeStruct)(shape, dtype) for shape, dtype in outs],
        in_specs=[pl.BlockSpec(memory_space=pltpu.SMEM)] + specs,
        out_specs=[vmem] * len(outs),
        scratch_shapes=scratch,
        compiler_params=PARAMS,
        cost_estimate=pl.CostEstimate(flops=flops, bytes_accessed=moved, transcendentals=0),
    )(flags, *arrays)


def roll(values, shift):
    return pltpu.roll(values, shift % values.shape[1], 1)


def order_matrix(low):
    row = lax.broadcasted_iota(jnp.int32, (PAD, PAD), 0)
    column = lax.broadcasted_iota(jnp.int32, (PAD, PAD), 1)
    wanted = jnp.where(low, row, ROWS - 1 - row)
    return jnp.where((column == wanted) & (row < ROWS), 1.0, 0.0).astype(BF16)


def reordered(order, values):
    total = jnp.zeros(values.shape, F32)
    for _ in range(3):
        part = values.astype(BF16)
        total += jnp.dot(order, part, preferred_element_type=F32)
        values = values - part.astype(F32)
    return total


def signed_factors(block, chunk):
    row = CHUNK * chunk + lax.broadcasted_iota(jnp.int32, (CHUNK, LANES), 0)
    ids = ROWS * block + row
    upper = (ids * 4682) >> 16
    k_z = ids - K * upper
    k_x = (upper * 4682) >> 16
    k_y = upper - K * k_x
    centre = (K - 1) / 2.0
    x, y, z = ((k.astype(F32) - centre) * (0.3 / centre) for k in (k_x, k_y, k_z))
    return jnp.abs(x), y, z


def lanes_of(rows):
    return lax.broadcasted_iota(jnp.int32, (rows, LANES), 1)


def lower_z(values):
    z_place = lax.broadcasted_iota(jnp.int32, values.shape, 1) % NZ
    return jnp.where(z_place == 0, roll(values, 1 - NZ), roll(values, 1))


def upper_z(values):
    z_place = lax.broadcasted_iota(jnp.int32, values.shape, 1) % NZ
    return jnp.where(z_place == NZ - 1, roll(values, NZ - 1), roll(values, -1))


def picked(values, lanes):
    return jnp.take_along_axis(values, lanes, axis=1, mode="promise_in_bounds")


def pack_edge(packed, values, positive, chunk, lane):
    place = lane & (NZ - 1)
    edge = picked(values, jnp.where(positive, place + LANES - NZ, place))
    return jnp.where((lane >> 4) == chunk, edge, packed)


def edge_block(packed):
    return jnp.concatenate([packed, jnp.zeros((EDGE - CHUNK, LANES), F32)], axis=0).astype(BF16)


def prepare_kernel(
    flags, populations, solid, own, own_edge, message, straight, turned, masks, factors
):
    low, block, half = flags[0] == 1, flags[2], flags[3]
    ordered = reordered(order_matrix(low), populations[...])
    left, right = ordered[:, :LANES], ordered[:, LANES:]
    mine = jnp.where(half == 0, left, right)
    rest = jnp.where(half == 0, right, left)
    own[...] = mine
    edges = jnp.zeros((CHUNK, LANES), F32)
    sent = jnp.zeros((CHUNK, LANES), F32)
    lane = lanes_of(CHUNK)
    for chunk in range(PAD // CHUNK):
        rows = slice(CHUNK * chunk, CHUNK * (chunk + 1))
        x, y, z = signed_factors(block, chunk)
        factors[0, rows], factors[1, rows], factors[2, rows] = x, y, z
        positive = jnp.where(low, y, -y) > 0
        edges = pack_edge(edges, rest[rows], positive, chunk, lane)
        sent = pack_edge(sent, mine[rows], positive, chunk, lane)
    own_edge[...] = edges
    message[:PAD] = rest.astype(BF16)
    message[PAD:] = edge_block(sent)
    fluid = jnp.where(jnp.broadcast_to(solid[...], (8, 2 * LANES)) == 0, 1.0, 0.0)
    place = lax.broadcasted_iota(jnp.int32, (8, 2 * LANES), 0)
    found = jnp.zeros((8, 2 * LANES), F32)
    near = (fluid, roll(fluid, NZ), roll(fluid, -NZ), lower_z(fluid), upper_z(fluid))
    for index, value in enumerate(near):
        found = jnp.where(place == index, value, found)
    masks[...] = jnp.where(half == 0, found[:, :LANES], found[:, LANES:])
    row = lax.broadcasted_iota(jnp.int32, (16, LANES), 0)
    halves = []
    for side in range(2):
        cells = slice(LANES * side, LANES * (side + 1))
        open_cells = jnp.where(row == 0, jnp.broadcast_to(fluid[:1, cells], (16, LANES)), 0.0)
        halves.append((ordered[:, cells].astype(BF16), open_cells.astype(BF16)))
    for place, target in ((flags[5], straight), (1 - flags[5], turned)):
        for rows, low_value, high_value in zip((slice(0, PAD), slice(PAD, PAD + 16)), *halves):
            target[rows] = jnp.where(place == 0, low_value, high_value)


def rows_of(index, size):
    return slice(size * index, size * (index + 1))


def stream_part(part, sign, values, mirror, layer, edge, masks, open_x, factors):
    fluid, below_open_y, above_open_y, below_open_z, above_open_z = (
        jnp.broadcast_to(masks[i : i + 1], (CHUNK, LANES)) for i in range(5)
    )
    open_x = jnp.broadcast_to(open_x, (CHUNK, LANES))
    lane = lanes_of(CHUNK)
    z_place = lane & (NZ - 1)
    below_z = jnp.where(z_place == 0, lane + NZ - 1, lane - 1)
    above_z = jnp.where(z_place == NZ - 1, lane + 1 - NZ, lane + 1)
    below_y, above_y = (lane + LANES - NZ) & (LANES - 1), (lane + NZ) & (LANES - 1)
    results = []
    for index in range(2):
        chunk = 2 * part + index
        x, y, z = (factors[i, rows_of(chunk, CHUNK)] for i in range(3))
        up_y, up_z = y * sign > 0, z * sign > 0
        here, back = values[rows_of(index, CHUNK)], mirror[rows_of(index, CHUNK)]
        at_edge = jnp.where(up_y, lane, lane + NZ)
        put = picked(edge, (at_edge + NZ * chunk) & (LANES - 1))
        outside = (up_y & (lane < NZ)) | (~up_y & (lane >= LANES - NZ))
        near_y = jnp.where(outside, put, picked(here, jnp.where(up_y, below_y, above_y)))
        near_z = picked(here, jnp.where(up_z, below_z, above_z))
        upwind_x = jnp.where(open_x > 0, layer[rows_of(index, CHUNK)], back)
        upwind_y = jnp.where(jnp.where(up_y, below_open_y, above_open_y) > 0, near_y, back)
        upwind_z = jnp.where(jnp.where(up_z, below_open_z, above_open_z) > 0, near_z, back)
        outflow = x * (here - upwind_x)
        outflow += jnp.abs(y) * (here - upwind_y)
        outflow += jnp.abs(z) * (here - upwind_z)
        results.append((here - outflow) * fluid)
    return jnp.concatenate(results, axis=0)


def pack_part(packed, part, sign, values, factors):
    lane = lanes_of(CHUNK)
    for index in range(2):
        chunk = 2 * part + index
        positive = factors[1, rows_of(chunk, CHUNK)] * sign > 0
        packed = pack_edge(packed, values[rows_of(index, CHUNK)], positive, chunk, lane)
    return packed


def signs(flags):
    near = jnp.where(flags[1] == 1, 1.0, -1.0)
    return near, -near


def place_of_near(flags):
    return pl.multiple_of(PAD * (1 - flags[1]), 16), pl.multiple_of(PAD * flags[1], 16)


def first_kernel(
    flags, own, own_edge, received, straight, turned, masks_in, factors, lowered, masks_out, bands
):
    same = flags[4] == 1
    place = lax.broadcasted_iota(jnp.int32, (8, LANES), 0)
    open_own = straight[PAD:].astype(F32)[:1]
    open_other = turned[PAD:].astype(F32)[:1]
    masks = masks_in[...]
    masks = jnp.where(place == 5, jnp.where(same, open_own, open_other), masks)
    masks = jnp.where(place == 6, jnp.where(same, open_other, open_own), masks)
    masks_out[...] = masks
    edge_own, edge_other = own_edge[...], received[PAD:].astype(F32)[:CHUNK]
    sign = jnp.where(flags[0] == 1, 1.0, -1.0)
    low = flags[0] == 1
    group = lanes_of(PART) >> 5
    packed = [jnp.zeros((PART, LANES), F32)] * 2
    for part in range(PAD // PART):
        span = rows_of(part, PART)
        mine, theirs = own[span], received[span].astype(F32)
        new_own = stream_part(
            part, sign, mine, theirs, straight[span].astype(F32), edge_own, masks, open_own, factors
        )
        new_other = stream_part(
            part, -sign, theirs, mine, turned[span].astype(F32), edge_other, masks, open_other, factors
        )
        rows_a, rows_b = jnp.where(low, new_own, new_other), jnp.where(low, new_other, new_own)
        for index, rows in enumerate((rows_a, rows_b)):
            lowered[PAD * index + PART * part : PAD * index + PART * (part + 1)] = rows.astype(BF16)
            place = 2 * index + part // 2
            edge = roll(rows, NZ + 2 * NZ * place)
            packed[part % 2] = jnp.where(group == place, edge, packed[part % 2])
    for index in range(2):
        bands[rows_of(index, PART)] = packed[index].astype(BF16)


def streamed(flags, near, far, sibling, neighbour, edges, masks, factors):
    values = masks[...]
    edge_near, edge_far = (edges[rows_of(i, EDGE)].astype(F32)[:CHUNK] for i in range(2))
    sign_near, sign_far = signs(flags)
    start = pl.multiple_of(PAD * flags[1], 16)
    for part in range(PAD // PART):
        span = rows_of(part, PART)
        rows_near, rows_far = near[span], far[span]
        layer = sibling[pl.ds(start + PART * part, PART)].astype(F32)
        new_near = stream_part(
            part, sign_near, rows_near, rows_far, layer, edge_near, values, values[5:6], factors
        )
        layer = neighbour[span].astype(F32)
        new_far = stream_part(
            part, sign_far, rows_far, rows_near, layer, edge_far, values, values[6:7], factors
        )
        yield part, span, new_near, new_far


def between_near_kernel(flags, near, far, sibling, edges, masks, factors, rows_out, sent, packed_out):
    values = masks[...]
    sign = signs(flags)[0]
    start = pl.multiple_of(PAD * flags[1], 16)
    edge = edges[:EDGE].astype(F32)[:CHUNK]
    packed = jnp.zeros((CHUNK, LANES), F32)
    for part in range(PAD // PART):
        span = rows_of(part, PART)
        layer = sibling[pl.ds(start + PART * part, PART)].astype(F32)
        rows = stream_part(
            part, sign, near[span], far[span], layer, edge, values, values[5:6], factors
        )
        rows_out[span] = rows
        sent[span] = rows.astype(BF16)
        packed = pack_part(packed, part, sign, rows, factors)
    packed_out[...] = edge_block(packed)


def between_far_kernel(
    flags, near, far, neighbour, edges, masks, factors, packed_near, rows_out, sent, packed_out
):
    values = masks[...]
    sign = signs(flags)[1]
    edge = edges[EDGE:].astype(F32)[:CHUNK]
    packed = jnp.zeros((CHUNK, LANES), F32)
    for part in range(PAD // PART):
        span = rows_of(part, PART)
        layer = neighbour[span].astype(F32)
        rows = stream_part(
            part, sign, far[span], near[span], layer, edge, values, values[6:7], factors
        )
        rows_out[span] = rows
        sent[span] = rows.astype(BF16)
        packed = pack_part(packed, part, sign, rows, factors)
    packed_out[:EDGE] = packed_near[...]
    packed_out[EDGE:] = edge_block(packed)


def lower_kernel(flags, near, far, sibling, neighbour, edges, masks, factors, lowered):
    at_near, at_far = place_of_near(flags)
    for part, span, new_near, new_far in streamed(
        flags, near, far, sibling, neighbour, edges, masks, factors
    ):
        lowered[pl.ds(at_near + PART * part, PART)] = new_near.astype(BF16)
        lowered[pl.ds(at_far + PART * part, PART)] = new_far.astype(BF16)


def last_kernel(given, flags, near, far, sibling, neighbour, edges, masks, factors, out):
    same = (flags[4] == 1) != given
    values = masks[...]
    edge_near, edge_far = (edges[rows_of(i, EDGE)].astype(F32)[:CHUNK] for i in range(2))
    edge, open_x = jnp.where(same, edge_near, edge_far), jnp.where(same, values[5:6], values[6:7])
    sign = jnp.where((flags[0] == 1) != given, 1.0, -1.0)
    start = pl.multiple_of(PAD * flags[1], 16)
    results = []
    for part in range(PAD // PART):
        span = rows_of(part, PART)
        rows_near, rows_far = near[span], far[span]
        layer_near = sibling[pl.ds(start + PART * part, PART)].astype(F32)
        layer = jnp.where(same, layer_near, neighbour[span].astype(F32))
        rows, mirror = jnp.where(same, rows_near, rows_far), jnp.where(same, rows_far, rows_near)
        results.append(stream_part(part, sign, rows, mirror, layer, edge, values, open_x, factors))
    results = jnp.concatenate(results, axis=0)
    if given:
        out[...] = results.astype(BF16)
    else:
        out[...] = reordered(order_matrix(flags[0] == 1), results)


def dot(left, right):
    return jnp.dot(left, right, preferred_element_type=F32)


def pack_other(packed, part, sign, values, factors):
    lane = lanes_of(CHUNK)
    place = lane & (NZ - 1)
    for index in range(2):
        chunk = 2 * part + index
        positive = factors[1, rows_of(chunk, CHUNK)] * sign > 0
        edge = picked(values[rows_of(index, CHUNK)], jnp.where(positive, place, place + NZ))
        packed = jnp.where((lane >> 4) == chunk, edge, packed)
    return packed


def unpacked(bands):
    values = bands.astype(F32)
    return jnp.concatenate([roll(values, -2 * NZ * group) for group in range(4)], axis=0).astype(BF16)


def collide_kernel(
    flags, lowered, other, bands, other_bands, factors, m0, m1, m2, m3, rows_out, packed_out, all_rows, all_bands
):
    swapped = flags[2] == 1
    for index, right in enumerate((swapped, ~swapped)):
        all_rows[rows_of(index, 2 * PAD)] = jnp.where(right, other[...], lowered[...])
        all_bands[rows_of(index, BAND)] = jnp.where(right, other_bands[...], bands[...])
    values = []
    for index in range(2):
        rows, band = all_rows[rows_of(index, 2 * PAD)], unpacked(all_bands[rows_of(index, BAND)])
        for side in range(2):
            span = rows_of(side, PAD)
            values.append(jnp.concatenate([rows[span], band[span]], axis=1))
    sign = jnp.where(flags[0] == 1, 1.0, -1.0)
    packed = jnp.zeros((CHUNK, LANES), F32)
    for part in range(PAD // PART):
        span = rows_of(part, PART)
        total = sum(dot(m[span], v) for m, v in zip((m0, m1, m2, m3), values))
        rows_out[span] = total[:, :LANES]
        packed = pack_other(packed, part, sign, total[:, LANES:], factors)
    packed_out[...] = edge_block(packed)


def give_rows(flags, part, rows_near, rows_far, factors, packed, outs):
    near, far, to_other_core, to_neighbour_chip = outs
    span = rows_of(part, PART)
    near[span], far[span] = rows_near, rows_far
    to_neighbour_chip[span] = rows_near.astype(BF16)
    to_other_core[span] = rows_far.astype(BF16)
    sign_near, sign_far = signs(flags)
    return (
        pack_part(packed[0], part, sign_near, rows_near, factors),
        pack_part(packed[1], part, sign_far, rows_far, factors),
    )


def give_product(flags, part, own, partner, factors, packed, outs):
    same = flags[4] == 1
    near, far = jnp.where(same, own, partner), jnp.where(same, partner, own)
    return give_rows(flags, part, near, far, factors, packed, outs)


def collide_partner_kernel(
    flags, factors, own_packed, all_rows, all_bands, own, matrix,
    near, far, for_sibling, for_neighbour, edges,
    held, held_rows, held_bands, held_own, held_packed, done,
):
    small = [
        pltpu.make_async_copy(source, target, done.at[index])
        for index, (source, target) in enumerate(
            ((all_rows, held_rows), (all_bands, held_bands), (own, held_own), (own_packed, held_packed))
        )
    ]
    parts = PAD // PART
    pieces = [
        [
            pltpu.make_async_copy(
                matrix.at[rows_of(parts * half + part, PART)],
                held.at[rows_of(parts * half + part, PART)],
                done.at[4 + parts * half + part],
            )
            for half in range(2)
        ]
        for part in range(parts)
    ]
    for copy in small[:2] + sum(pieces, []) + small[2:]:
        copy.start()
    for copy in small[:2]:
        copy.wait()
    low, same = flags[0] == 1, flags[4] == 1
    values = []
    for index in range(2):
        band = unpacked(held_bands[rows_of(index, BAND)])
        values.append(jnp.concatenate([held_rows[rows_of(index, 2 * PAD)], band], axis=1))
    sign = jnp.where(low, -1.0, 1.0)
    packed = jnp.zeros((CHUNK, LANES), F32)
    for part in range(parts):
        span = rows_of(part, PART)
        total = 0.0
        for half in range(2):
            pieces[part][half].wait()
            total += dot(held[rows_of(parts * half + part, PART)], values[half])
        if part == 0:
            for copy in small[2:]:
                copy.wait()
        mine, theirs = held_own[span], total[:, :LANES]
        rows_near, rows_far = jnp.where(same, mine, theirs), jnp.where(same, theirs, mine)
        near[span], far[span] = rows_near, rows_far
        for_neighbour[span] = rows_near.astype(BF16)
        for_sibling[span] = rows_far.astype(BF16)
        packed = pack_other(packed, part, sign, total[:, LANES:], factors)
    mine, theirs = held_packed[...], edge_block(packed)
    edges[:EDGE] = jnp.where(same, mine, theirs)
    edges[EDGE:] = jnp.where(same, theirs, mine)


def early_kernel(
    flags, lowered, m0, m1, m2, m3, matrix, own_out, partner_out, next_own, next_partner,
    held_own, held_partner, done,
):
    values = lowered[...]
    parts = m0, m1, m2, m3
    for half in range(2):

        @pl.when(flags[2] == half)
        def _():
            copies = [
                pltpu.make_async_copy(
                    matrix.at[rows_of(half, PAD)], held_partner, done.at[0]
                )
            ]
            for i in range(2):
                copies.append(pltpu.make_async_copy(parts[2 * half + i], held_own.at[i], done.at[1 + i]))
            copies.append(
                pltpu.make_async_copy(matrix.at[rows_of(1 - half, PAD)], next_partner, done.at[3])
            )
            for i in range(2):
                source = parts[2 * (1 - half) + i]
                copies.append(pltpu.make_async_copy(source, next_own.at[i], done.at[4 + i]))
            for copy in copies:
                copy.start()
            copies[0].wait()
            for part in range(PAD // PART):
                span = rows_of(part, PART)
                partner_out[span] = dot(held_partner[span], values)
            copies[1].wait()
            copies[2].wait()
            for part in range(PAD // PART):
                span = rows_of(part, PART)
                own_out[span] = dot(held_own[0, span], values[:PAD]) + dot(held_own[1, span], values[PAD:])
            for copy in copies[3:]:
                copy.wait()


def late_kernel(flags, other, own, partner, factors, matrix_own, matrix_partner, *outs):
    values = other[...]
    packed = (jnp.zeros((CHUNK, LANES), F32),) * 2
    for part in range(PAD // PART):
        span = rows_of(part, PART)
        more_own = dot(matrix_own[0, span], values[:PAD]) + dot(matrix_own[1, span], values[PAD:])
        more_partner = dot(matrix_partner[span], values)
        packed = give_product(
            flags, part, own[span] + more_own, partner[span] + more_partner, factors, packed, outs[:4]
        )
    outs[4][:EDGE], outs[4][EDGE:] = edge_block(packed[0]), edge_block(packed[1])


ROWS_F32 = ((PAD, LANES), F32)
PARTNER_SCRATCH = [
    pltpu.VMEM((2 * PAD, 2 * PAD), BF16),
    pltpu.VMEM((4 * PAD, LANES), BF16),
    pltpu.VMEM((2 * BAND, LANES), BF16),
    pltpu.VMEM((PAD, LANES), F32),
    pltpu.VMEM((EDGE, LANES), BF16),
    pltpu.SemaphoreType.DMA((12,)),
]
HELD = [pltpu.VMEM((2, PAD, PAD), BF16), pltpu.VMEM((PAD, 2 * PAD), BF16)]
EARLY = [ROWS_F32, ROWS_F32, ((2, PAD, PAD), BF16), ((PAD, 2 * PAD), BF16)]
EARLY_SCRATCH = HELD + [pltpu.SemaphoreType.DMA((6,))]


def finish_kernel(flags, kept, received, evolved):
    order = order_matrix(flags[0] == 1)
    rest = jnp.dot(order, received[...], preferred_element_type=F32)
    mine = kept[...]
    half = flags[3]
    evolved[:, 0, :LANES] = jnp.where(half == 0, mine, rest)[:ROWS]
    evolved[:, 0, LANES:] = jnp.where(half == 0, rest, mine)[:ROWS]


def place(rows, columns, wanted):
    return (lax.broadcasted_iota(jnp.int32, (rows, columns), 0) == wanted[None, :]).astype(BF16)


def chosen(left, right):
    return jnp.dot(left, right, preferred_element_type=BF16)


def column_half(wide, block):
    column = lax.iota(jnp.int32, PAD)
    inside = column < ROWS
    start_a, start_b = 640 * block, jnp.where(block == 1, 1280, 2048)
    part_a = lax.dynamic_slice(wide, (0, start_a), (wide.shape[0], 768))
    part_b = lax.dynamic_slice(wide, (0, start_b), (wide.shape[0], 896))
    wanted_a = jnp.where(inside, ROWS * block + column - start_a, -1)
    wanted_b = jnp.where(inside, 4 * ROWS - 1 - ROWS * block - column - start_b, -1)
    halves = chosen(part_a, place(768, PAD, wanted_a)), chosen(part_b, place(896, PAD, wanted_b))
    return halves


def padded_columns(matrix):
    return jnp.pad(matrix, ((0, 0), (0, 2944 - matrix.shape[1])))


def per_device(populations, solid_mask, collision):
    cell, vel = lax.axis_index("cells"), lax.axis_index("vel")
    low = (vel < 2).astype(jnp.int32)
    core, ring_place = cell % 2, cell // 32 + 4 * (cell // 2 % 2)
    block = jnp.minimum(vel, 3 - vel)
    half = (1 - low) ^ (cell // RING % 2)
    needing = (cell + 1 - 2 * low) % 128
    straight_half = (1 - low) ^ (needing // RING % 2)
    same = (low != core).astype(jnp.int32)
    flags = jnp.stack([low, 1 - core, block, half, same, straight_half])
    flags = flags.astype(jnp.int32)

    first_row = CHUNK * ring_place
    row = first_row + lax.iota(jnp.int32, CHUNK)
    start = jnp.clip(jnp.where(low == 1, first_row, ROWS - CHUNK - first_row), 0, ROWS - CHUNK)
    wanted = jnp.where(row < ROWS, jnp.where(low == 1, row, ROWS - 1 - row) - start, -1)
    window = lax.dynamic_slice(collision, (start, 0), (CHUNK, collision.shape[1]))
    window = padded_columns(chosen(place(CHUNK, CHUNK, wanted).T, window))
    piece = jnp.concatenate(column_half(window, core), axis=1)
    populations, piece = lax.optimization_barrier((populations, piece))
    piece = to_mirror(piece)

    padded = jnp.pad(populations[:, 0, :], ((0, PAD - ROWS), (0, 0)))
    rows = (PAD, LANES)
    own, own_edge, message, straight, turned, masks, factors = call(
        prepare_kernel,
        [(rows, F32), ((CHUNK, LANES), F32), ((PAD + EDGE, LANES), BF16),
         ((PAD + 16, LANES), BF16), ((PAD + 16, LANES), BF16), ((8, LANES), F32), ((3, *rows), F32)],
        flags, padded, solid_mask, flops=2 * 3 * PAD * PAD * 256,
    )
    piece, _ = lax.optimization_barrier((piece, message))
    groups = [
        [x * 32 + y * 16 + 4 * pair + 2 * odd + side for side in range(2) for odd in range(2) for x in range(4)]
        for y in range(2)
        for pair in range(4)
    ]
    partner_matrix = lax.all_gather(piece, "cells", axis=0, tiled=True, axis_index_groups=groups)
    turned = to_layer(turned, True)
    received = to_mirror(message)

    row = lax.iota(jnp.int32, PAD)
    wanted = jnp.where(row < ROWS, jnp.where(low == 1, row, ROWS - 1 - row), -1)
    message, collision = lax.optimization_barrier((message, collision))
    ordered = padded_columns(chosen(place(ROWS, PAD, wanted).T, collision))

    straight, ordered = lax.optimization_barrier((straight, ordered))
    straight = to_layer(straight, False)
    lowered, masks, bands = call(
        first_kernel,
        [((2 * PAD, LANES), BF16), ((8, LANES), F32), ((BAND, LANES), BF16)],
        flags, own, own_edge, received, straight, turned, masks, factors, flops=100 * PAD * 256,
    )
    edges_shape = ((2 * EDGE, LANES), BF16)
    sends = [(rows, F32)] * 2 + [(rows, BF16)] * 2 + [edges_shape]
    multiply = 2 * PAD * 4 * PAD * LANES
    work = 100 * PAD * LANES

    lowered, bands, ordered = lax.optimization_barrier((lowered, bands, ordered))
    matrix = *column_half(ordered, 0), *column_half(ordered, 1)
    other = to_side(lowered)
    bands = to_mirror(bands), to_opposite(bands)
    own, own_packed, all_rows, all_bands = call(
        collide_kernel,
        [(rows, F32), ((EDGE, LANES), BF16), ((4 * PAD, LANES), BF16), ((2 * BAND, LANES), BF16)],
        flags, lowered, other, *bands, factors, *matrix, flops=2 * multiply, leave=True,
    )
    partner_matrix, own = lax.optimization_barrier((partner_matrix, own))
    near, far, for_sibling, for_neighbour, edges = call(
        collide_partner_kernel, sends, flags, factors, own_packed, all_rows, all_bands, own, partner_matrix,
        flops=2 * multiply, stay=5, scratch=PARTNER_SCRATCH,
    )

    for step in range(1, STEPS):
        neighbour, sibling = to_neighbour(for_neighbour), with_sibling(for_sibling)
        new_near, for_neighbour, packed = call(
            between_near_kernel, [(rows, F32), (rows, BF16), ((EDGE, LANES), BF16)],
            flags, near, far, sibling, edges, masks, factors, flops=work,
        )
        new_far, for_sibling, edges = call(
            between_far_kernel, [(rows, F32), (rows, BF16), edges_shape],
            flags, near, far, neighbour, edges, masks, factors, packed, flops=work,
        )
        near, far = new_near, new_far
        neighbour, edges = to_neighbour(for_neighbour), to_mirror(edges)
        sibling = with_sibling(for_sibling)
        (lowered,) = call(
            lower_kernel, [((2 * PAD, LANES), BF16)],
            flags, near, far, sibling, neighbour, edges, masks, factors, flops=work,
        )
        other = to_side(lowered)
        early = call(
            early_kernel, EARLY, flags, lowered, *matrix, partner_matrix,
            flops=multiply, stay=5, scratch=EARLY_SCRATCH,
        )
        near, far, for_sibling, for_neighbour, edges = call(
            late_kernel, sends, flags, other, *early[:2], factors, *early[2:], flops=multiply
        )

    neighbour, edges = to_neighbour(for_neighbour), to_mirror(edges)
    sibling = with_sibling(for_sibling)
    last = flags, near, far, sibling, neighbour, edges, masks, factors
    (message,) = call(functools.partial(last_kernel, True), [(rows, BF16)], *last, flops=work)
    received = to_mirror(message)
    (kept,) = call(functools.partial(last_kernel, False), [(rows, F32)], *last, flops=multiply)
    (evolved,) = call(
        finish_kernel, [((ROWS, 1, 2 * LANES), F32)], flags, kept, received, flops=2 * PAD * PAD * LANES
    )
    return evolved


def solution(mesh):
    in_specs = (P("vel", "cells", None), P("cells", None), P("vel", None))
    out_specs = P("vel", "cells", None)
    return jax.shard_map(
        per_device, mesh=mesh, in_specs=in_specs, out_specs=out_specs, check_vma=False
    )
```

```python
import functools
import math

import jax
import jax.numpy as jnp
from jax import lax
from jax.experimental import pallas as pl
from jax.experimental.pallas import tpu as pltpu
from jax.sharding import PartitionSpec as P


K = 14
STEPS = 2
NZ = 16
BOTH = ("cells", "vel")
ROWS = 686
PAD = 704
CHUNK = 88
PART = 2 * CHUNK
EDGE = 96
LANES = 128
BAND = 4 * CHUNK
RING = 16
F32 = jnp.float32
BF16 = jnp.bfloat16
PARAMS = pltpu.CompilerParams(vmem_limit_bytes=20 * 1024 * 1024)


def pairs_of(target):
    pairs = []
    for cell in range(128):
        for part in range(4):
            to_cell, to_part = target(cell, part)
            pairs.append((cell * 4 + part, to_cell * 4 + to_part))
    return pairs


def with_sibling(array):
    groups = [[cell, cell + 1] for cell in range(0, 128, 2)]
    return lax.all_gather(array, "cells", axis=0, tiled=True, axis_index_groups=groups)


def to_layer(array, turned):
    def target(cell, part):
        return (cell - 1 if part < 2 else cell + 1) % 128, 3 - part if turned else part

    return lax.ppermute(array, BOTH, pairs_of(target))


def neighbour_of(cell, part):
    other = (cell - 1 if cell % 2 == 0 else cell + 1) % 128
    return other, part if (other // RING) % 2 == (cell // RING) % 2 else 3 - part


def to_neighbour(array):
    return lax.ppermute(array, BOTH, pairs_of(neighbour_of))


def to_mirror(array):
    return lax.ppermute(array, "vel", [(i, 3 - i) for i in range(4)])


def to_opposite(array):
    return lax.ppermute(array, "vel", [(i, i ^ 2) for i in range(4)])


def to_side(array):
    return lax.ppermute(array, "vel", [(i, i ^ 1) for i in range(4)])


def call(kernel, outs, flags, *arrays, flops=0, stay=0, scratch=(), leave=False):
    moved = sum(x.size * x.dtype.itemsize for x in arrays)
    moved += sum(math.prod(shape) * jnp.dtype(dtype).itemsize for shape, dtype in outs)
    vmem, hbm = (pl.BlockSpec(memory_space=space) for space in (pltpu.VMEM, pltpu.HBM))
    count = len(arrays) - stay
    specs = [vmem] * count + [hbm] * stay
    arrays = *arrays[:count], *(pltpu.with_memory_space_constraint(x, pltpu.HBM) for x in arrays[count:])
    return pl.pallas_call(
        kernel,
        out_shape=[(pltpu.HBM if leave else jax.ShapeDtypeStruct)(shape, dtype) for shape, dtype in outs],
        in_specs=[pl.BlockSpec(memory_space=pltpu.SMEM)] + specs,
        out_specs=[vmem] * len(outs),
        scratch_shapes=scratch,
        compiler_params=PARAMS,
        cost_estimate=pl.CostEstimate(flops=flops, bytes_accessed=moved, transcendentals=0),
    )(flags, *arrays)


def roll(values, shift):
    return pltpu.roll(values, shift % values.shape[1], 1)


def order_matrix(low):
    row = lax.broadcasted_iota(jnp.int32, (PAD, PAD), 0)
    column = lax.broadcasted_iota(jnp.int32, (PAD, PAD), 1)
    wanted = jnp.where(low, row, ROWS - 1 - row)
    return jnp.where((column == wanted) & (row < ROWS), 1.0, 0.0).astype(BF16)


def reordered(order, values):
    total = jnp.zeros(values.shape, F32)
    for _ in range(3):
        part = values.astype(BF16)
        total += jnp.dot(order, part, preferred_element_type=F32)
        values = values - part.astype(F32)
    return total


def signed_factors(block, chunk):
    row = CHUNK * chunk + lax.broadcasted_iota(jnp.int32, (CHUNK, LANES), 0)
    ids = ROWS * block + row
    upper = (ids * 4682) >> 16
    k_z = ids - K * upper
    k_x = (upper * 4682) >> 16
    k_y = upper - K * k_x
    centre = (K - 1) / 2.0
    x, y, z = ((k.astype(F32) - centre) * (0.3 / centre) for k in (k_x, k_y, k_z))
    return jnp.abs(x), y, z


def lanes_of(rows):
    return lax.broadcasted_iota(jnp.int32, (rows, LANES), 1)


def lower_z(values):
    z_place = lax.broadcasted_iota(jnp.int32, values.shape, 1) % NZ
    return jnp.where(z_place == 0, roll(values, 1 - NZ), roll(values, 1))


def upper_z(values):
    z_place = lax.broadcasted_iota(jnp.int32, values.shape, 1) % NZ
    return jnp.where(z_place == NZ - 1, roll(values, NZ - 1), roll(values, -1))


def picked(values, lanes):
    return jnp.take_along_axis(values, lanes, axis=1, mode="promise_in_bounds")


def pack_edge(packed, values, positive, chunk, lane):
    place = lane & (NZ - 1)
    edge = picked(values, jnp.where(positive, place + LANES - NZ, place))
    return jnp.where((lane >> 4) == chunk, edge, packed)


def edge_block(packed):
    return jnp.concatenate([packed, jnp.zeros((EDGE - CHUNK, LANES), F32)], axis=0).astype(BF16)


def prepare_kernel(
    flags, populations, solid, own, own_edge, message, straight, turned, masks, factors
):
    low, block, half = flags[0] == 1, flags[2], flags[3]
    ordered = reordered(order_matrix(low), populations[...])
    left, right = ordered[:, :LANES], ordered[:, LANES:]
    mine = jnp.where(half == 0, left, right)
    rest = jnp.where(half == 0, right, left)
    own[...] = mine
    edges = jnp.zeros((CHUNK, LANES), F32)
    sent = jnp.zeros((CHUNK, LANES), F32)
    lane = lanes_of(CHUNK)
    for chunk in range(PAD // CHUNK):
        rows = slice(CHUNK * chunk, CHUNK * (chunk + 1))
        x, y, z = signed_factors(block, chunk)
        factors[0, rows], factors[1, rows], factors[2, rows] = x, y, z
        positive = jnp.where(low, y, -y) > 0
        edges = pack_edge(edges, rest[rows], positive, chunk, lane)
        sent = pack_edge(sent, mine[rows], positive, chunk, lane)
    own_edge[...] = edges
    message[:PAD] = rest.astype(BF16)
    message[PAD:] = edge_block(sent)
    fluid = jnp.where(jnp.broadcast_to(solid[...], (8, 2 * LANES)) == 0, 1.0, 0.0)
    place = lax.broadcasted_iota(jnp.int32, (8, 2 * LANES), 0)
    found = jnp.zeros((8, 2 * LANES), F32)
    near = (fluid, roll(fluid, NZ), roll(fluid, -NZ), lower_z(fluid), upper_z(fluid))
    for index, value in enumerate(near):
        found = jnp.where(place == index, value, found)
    masks[...] = jnp.where(half == 0, found[:, :LANES], found[:, LANES:])
    row = lax.broadcasted_iota(jnp.int32, (16, LANES), 0)
    halves = []
    for side in range(2):
        cells = slice(LANES * side, LANES * (side + 1))
        open_cells = jnp.where(row == 0, jnp.broadcast_to(fluid[:1, cells], (16, LANES)), 0.0)
        halves.append((ordered[:, cells].astype(BF16), open_cells.astype(BF16)))
    for place, target in ((flags[5], straight), (1 - flags[5], turned)):
        for rows, low_value, high_value in zip((slice(0, PAD), slice(PAD, PAD + 16)), *halves):
            target[rows] = jnp.where(place == 0, low_value, high_value)


def rows_of(index, size):
    return slice(size * index, size * (index + 1))


def stream_part(part, sign, values, mirror, layer, edge, masks, open_x, factors):
    fluid, below_open_y, above_open_y, below_open_z, above_open_z = (
        jnp.broadcast_to(masks[i : i + 1], (CHUNK, LANES)) for i in range(5)
    )
    open_x = jnp.broadcast_to(open_x, (CHUNK, LANES))
    lane = lanes_of(CHUNK)
    z_place = lane & (NZ - 1)
    below_z = jnp.where(z_place == 0, lane + NZ - 1, lane - 1)
    above_z = jnp.where(z_place == NZ - 1, lane + 1 - NZ, lane + 1)
    below_y, above_y = (lane + LANES - NZ) & (LANES - 1), (lane + NZ) & (LANES - 1)
    results = []
    for index in range(2):
        chunk = 2 * part + index
        x, y, z = (factors[i, rows_of(chunk, CHUNK)] for i in range(3))
        up_y, up_z = y * sign > 0, z * sign > 0
        here, back = values[rows_of(index, CHUNK)], mirror[rows_of(index, CHUNK)]
        at_edge = jnp.where(up_y, lane, lane + NZ)
        put = picked(edge, (at_edge + NZ * chunk) & (LANES - 1))
        outside = (up_y & (lane < NZ)) | (~up_y & (lane >= LANES - NZ))
        near_y = jnp.where(outside, put, picked(here, jnp.where(up_y, below_y, above_y)))
        near_z = picked(here, jnp.where(up_z, below_z, above_z))
        upwind_x = jnp.where(open_x > 0, layer[rows_of(index, CHUNK)], back)
        upwind_y = jnp.where(jnp.where(up_y, below_open_y, above_open_y) > 0, near_y, back)
        upwind_z = jnp.where(jnp.where(up_z, below_open_z, above_open_z) > 0, near_z, back)
        outflow = x * (here - upwind_x)
        outflow += jnp.abs(y) * (here - upwind_y)
        outflow += jnp.abs(z) * (here - upwind_z)
        results.append((here - outflow) * fluid)
    return jnp.concatenate(results, axis=0)


def pack_part(packed, part, sign, values, factors):
    lane = lanes_of(CHUNK)
    for index in range(2):
        chunk = 2 * part + index
        positive = factors[1, rows_of(chunk, CHUNK)] * sign > 0
        packed = pack_edge(packed, values[rows_of(index, CHUNK)], positive, chunk, lane)
    return packed


def signs(flags):
    near = jnp.where(flags[1] == 1, 1.0, -1.0)
    return near, -near


def place_of_near(flags):
    return pl.multiple_of(PAD * (1 - flags[1]), 16), pl.multiple_of(PAD * flags[1], 16)


def first_kernel(
    flags, own, own_edge, received, straight, turned, masks_in, factors, lowered, masks_out, bands
):
    same = flags[4] == 1
    place = lax.broadcasted_iota(jnp.int32, (8, LANES), 0)
    open_own = straight[PAD:].astype(F32)[:1]
    open_other = turned[PAD:].astype(F32)[:1]
    masks = masks_in[...]
    masks = jnp.where(place == 5, jnp.where(same, open_own, open_other), masks)
    masks = jnp.where(place == 6, jnp.where(same, open_other, open_own), masks)
    masks_out[...] = masks
    edge_own, edge_other = own_edge[...], received[PAD:].astype(F32)[:CHUNK]
    sign = jnp.where(flags[0] == 1, 1.0, -1.0)
    low = flags[0] == 1
    group = lanes_of(PART) >> 5
    packed = [jnp.zeros((PART, LANES), F32)] * 2
    for part in range(PAD // PART):
        span = rows_of(part, PART)
        mine, theirs = own[span], received[span].astype(F32)
        new_own = stream_part(
            part, sign, mine, theirs, straight[span].astype(F32), edge_own, masks, open_own, factors
        )
        new_other = stream_part(
            part, -sign, theirs, mine, turned[span].astype(F32), edge_other, masks, open_other, factors
        )
        rows_a, rows_b = jnp.where(low, new_own, new_other), jnp.where(low, new_other, new_own)
        for index, rows in enumerate((rows_a, rows_b)):
            lowered[PAD * index + PART * part : PAD * index + PART * (part + 1)] = rows.astype(BF16)
            place = 2 * index + part // 2
            edge = roll(rows, NZ + 2 * NZ * place)
            packed[part % 2] = jnp.where(group == place, edge, packed[part % 2])
    for index in range(2):
        bands[rows_of(index, PART)] = packed[index].astype(BF16)


def streamed(flags, near, far, sibling, neighbour, edges, masks, factors):
    values = masks[...]
    edge_near, edge_far = (edges[rows_of(i, EDGE)].astype(F32)[:CHUNK] for i in range(2))
    sign_near, sign_far = signs(flags)
    start = pl.multiple_of(PAD * flags[1], 16)
    for part in range(PAD // PART):
        span = rows_of(part, PART)
        rows_near, rows_far = near[span], far[span]
        layer = sibling[pl.ds(start + PART * part, PART)].astype(F32)
        new_near = stream_part(
            part, sign_near, rows_near, rows_far, layer, edge_near, values, values[5:6], factors
        )
        layer = neighbour[span].astype(F32)
        new_far = stream_part(
            part, sign_far, rows_far, rows_near, layer, edge_far, values, values[6:7], factors
        )
        yield part, span, new_near, new_far


def between_near_kernel(flags, near, far, sibling, edges, masks, factors, rows_out, sent, packed_out):
    values = masks[...]
    sign = signs(flags)[0]
    start = pl.multiple_of(PAD * flags[1], 16)
    edge = edges[:EDGE].astype(F32)[:CHUNK]
    packed = jnp.zeros((CHUNK, LANES), F32)
    for part in range(PAD // PART):
        span = rows_of(part, PART)
        layer = sibling[pl.ds(start + PART * part, PART)].astype(F32)
        rows = stream_part(
            part, sign, near[span], far[span], layer, edge, values, values[5:6], factors
        )
        rows_out[span] = rows
        sent[span] = rows.astype(BF16)
        packed = pack_part(packed, part, sign, rows, factors)
    packed_out[...] = edge_block(packed)


def between_far_kernel(
    flags, near, far, neighbour, edges, masks, factors, packed_near, rows_out, sent, packed_out
):
    values = masks[...]
    sign = signs(flags)[1]
    edge = edges[EDGE:].astype(F32)[:CHUNK]
    packed = jnp.zeros((CHUNK, LANES), F32)
    for part in range(PAD // PART):
        span = rows_of(part, PART)
        layer = neighbour[span].astype(F32)
        rows = stream_part(
            part, sign, far[span], near[span], layer, edge, values, values[6:7], factors
        )
        rows_out[span] = rows
        sent[span] = rows.astype(BF16)
        packed = pack_part(packed, part, sign, rows, factors)
    packed_out[:EDGE] = packed_near[...]
    packed_out[EDGE:] = edge_block(packed)


def lower_kernel(flags, near, far, sibling, neighbour, edges, masks, factors, lowered):
    at_near, at_far = place_of_near(flags)
    for part, span, new_near, new_far in streamed(
        flags, near, far, sibling, neighbour, edges, masks, factors
    ):
        lowered[pl.ds(at_near + PART * part, PART)] = new_near.astype(BF16)
        lowered[pl.ds(at_far + PART * part, PART)] = new_far.astype(BF16)


def last_kernel(given, flags, near, far, sibling, neighbour, edges, masks, factors, out):
    same = (flags[4] == 1) != given
    values = masks[...]
    edge_near, edge_far = (edges[rows_of(i, EDGE)].astype(F32)[:CHUNK] for i in range(2))
    edge, open_x = jnp.where(same, edge_near, edge_far), jnp.where(same, values[5:6], values[6:7])
    sign = jnp.where((flags[0] == 1) != given, 1.0, -1.0)
    start = pl.multiple_of(PAD * flags[1], 16)
    results = []
    for part in range(PAD // PART):
        span = rows_of(part, PART)
        rows_near, rows_far = near[span], far[span]
        layer_near = sibling[pl.ds(start + PART * part, PART)].astype(F32)
        layer = jnp.where(same, layer_near, neighbour[span].astype(F32))
        rows, mirror = jnp.where(same, rows_near, rows_far), jnp.where(same, rows_far, rows_near)
        results.append(stream_part(part, sign, rows, mirror, layer, edge, values, open_x, factors))
    results = jnp.concatenate(results, axis=0)
    if given:
        out[...] = results.astype(BF16)
    else:
        out[...] = reordered(order_matrix(flags[0] == 1), results)


def dot(left, right):
    return jnp.dot(left, right, preferred_element_type=F32)


def pack_other(packed, part, sign, values, factors):
    lane = lanes_of(CHUNK)
    place = lane & (NZ - 1)
    for index in range(2):
        chunk = 2 * part + index
        positive = factors[1, rows_of(chunk, CHUNK)] * sign > 0
        edge = picked(values[rows_of(index, CHUNK)], jnp.where(positive, place, place + NZ))
        packed = jnp.where((lane >> 4) == chunk, edge, packed)
    return packed


def unpacked(bands):
    values = bands.astype(F32)
    return jnp.concatenate([roll(values, -2 * NZ * group) for group in range(4)], axis=0).astype(BF16)


def collide_kernel(
    flags, lowered, other, bands, other_bands, factors, m0, m1, m2, m3, rows_out, packed_out, all_rows, all_bands
):
    swapped = flags[2] == 1
    for index, right in enumerate((swapped, ~swapped)):
        all_rows[rows_of(index, 2 * PAD)] = jnp.where(right, other[...], lowered[...])
        all_bands[rows_of(index, BAND)] = jnp.where(right, other_bands[...], bands[...])
    values = []
    for index in range(2):
        rows, band = all_rows[rows_of(index, 2 * PAD)], unpacked(all_bands[rows_of(index, BAND)])
        for side in range(2):
            span = rows_of(side, PAD)
            values.append(jnp.concatenate([rows[span], band[span]], axis=1))
    sign = jnp.where(flags[0] == 1, 1.0, -1.0)
    packed = jnp.zeros((CHUNK, LANES), F32)
    for part in range(PAD // PART):
        span = rows_of(part, PART)
        total = sum(dot(m[span], v) for m, v in zip((m0, m1, m2, m3), values))
        rows_out[span] = total[:, :LANES]
        packed = pack_other(packed, part, sign, total[:, LANES:], factors)
    packed_out[...] = edge_block(packed)


def give_rows(flags, part, rows_near, rows_far, factors, packed, outs):
    near, far, to_other_core, to_neighbour_chip = outs
    span = rows_of(part, PART)
    near[span], far[span] = rows_near, rows_far
    to_neighbour_chip[span] = rows_near.astype(BF16)
    to_other_core[span] = rows_far.astype(BF16)
    sign_near, sign_far = signs(flags)
    return (
        pack_part(packed[0], part, sign_near, rows_near, factors),
        pack_part(packed[1], part, sign_far, rows_far, factors),
    )


def give_product(flags, part, own, partner, factors, packed, outs):
    same = flags[4] == 1
    near, far = jnp.where(same, own, partner), jnp.where(same, partner, own)
    return give_rows(flags, part, near, far, factors, packed, outs)


def collide_partner_kernel(
    flags, factors, own_packed, all_rows, all_bands, own, matrix,
    near, far, for_sibling, for_neighbour, edges,
    held, held_rows, held_bands, held_own, held_packed, done,
):
    small = [
        pltpu.make_async_copy(source, target, done.at[index])
        for index, (source, target) in enumerate(
            ((all_rows, held_rows), (all_bands, held_bands), (own, held_own), (own_packed, held_packed))
        )
    ]
    parts = PAD // PART
    pieces = [
        [
            pltpu.make_async_copy(
                matrix.at[rows_of(parts * half + part, PART)],
                held.at[rows_of(parts * half + part, PART)],
                done.at[4 + parts * half + part],
            )
            for half in range(2)
        ]
        for part in range(parts)
    ]
    for copy in small[:2] + sum(pieces, []) + small[2:]:
        copy.start()
    for copy in small[:2]:
        copy.wait()
    low, same = flags[0] == 1, flags[4] == 1
    values = []
    for index in range(2):
        band = unpacked(held_bands[rows_of(index, BAND)])
        values.append(jnp.concatenate([held_rows[rows_of(index, 2 * PAD)], band], axis=1))
    sign = jnp.where(low, -1.0, 1.0)
    packed = jnp.zeros((CHUNK, LANES), F32)
    for part in range(parts):
        span = rows_of(part, PART)
        total = 0.0
        for half in range(2):
            pieces[part][half].wait()
            total += dot(held[rows_of(parts * half + part, PART)], values[half])
        if part == 0:
            for copy in small[2:]:
                copy.wait()
        mine, theirs = held_own[span], total[:, :LANES]
        rows_near, rows_far = jnp.where(same, mine, theirs), jnp.where(same, theirs, mine)
        near[span], far[span] = rows_near, rows_far
        for_neighbour[span] = rows_near.astype(BF16)
        for_sibling[span] = rows_far.astype(BF16)
        packed = pack_other(packed, part, sign, total[:, LANES:], factors)
    mine, theirs = held_packed[...], edge_block(packed)
    edges[:EDGE] = jnp.where(same, mine, theirs)
    edges[EDGE:] = jnp.where(same, theirs, mine)


def early_kernel(
    flags, lowered, m0, m1, m2, m3, matrix, own_out, partner_out, next_own, next_partner,
    held_own, held_partner, done,
):
    values = lowered[...]
    parts = m0, m1, m2, m3
    for half in range(2):

        @pl.when(flags[2] == half)
        def _():
            copies = [
                pltpu.make_async_copy(
                    matrix.at[rows_of(half, PAD)], held_partner, done.at[0]
                )
            ]
            for i in range(2):
                copies.append(pltpu.make_async_copy(parts[2 * half + i], held_own.at[i], done.at[1 + i]))
            copies.append(
                pltpu.make_async_copy(matrix.at[rows_of(1 - half, PAD)], next_partner, done.at[3])
            )
            for i in range(2):
                source = parts[2 * (1 - half) + i]
                copies.append(pltpu.make_async_copy(source, next_own.at[i], done.at[4 + i]))
            for copy in copies:
                copy.start()
            copies[0].wait()
            for part in range(PAD // PART):
                span = rows_of(part, PART)
                partner_out[span] = dot(held_partner[span], values)
            copies[1].wait()
            copies[2].wait()
            for part in range(PAD // PART):
                span = rows_of(part, PART)
                own_out[span] = dot(held_own[0, span], values[:PAD]) + dot(held_own[1, span], values[PAD:])
            for copy in copies[3:]:
                copy.wait()


def late_kernel(flags, other, own, partner, factors, matrix_own, matrix_partner, *outs):
    values = other[...]
    packed = (jnp.zeros((CHUNK, LANES), F32),) * 2
    for part in range(PAD // PART):
        span = rows_of(part, PART)
        more_own = dot(matrix_own[0, span], values[:PAD]) + dot(matrix_own[1, span], values[PAD:])
        more_partner = dot(matrix_partner[span], values)
        packed = give_product(
            flags, part, own[span] + more_own, partner[span] + more_partner, factors, packed, outs[:4]
        )
    outs[4][:EDGE], outs[4][EDGE:] = edge_block(packed[0]), edge_block(packed[1])


ROWS_F32 = ((PAD, LANES), F32)
PARTNER_SCRATCH = [
    pltpu.VMEM((2 * PAD, 2 * PAD), BF16),
    pltpu.VMEM((4 * PAD, LANES), BF16),
    pltpu.VMEM((2 * BAND, LANES), BF16),
    pltpu.VMEM((PAD, LANES), F32),
    pltpu.VMEM((EDGE, LANES), BF16),
    pltpu.SemaphoreType.DMA((12,)),
]
HELD = [pltpu.VMEM((2, PAD, PAD), BF16), pltpu.VMEM((PAD, 2 * PAD), BF16)]
EARLY = [ROWS_F32, ROWS_F32, ((2, PAD, PAD), BF16), ((PAD, 2 * PAD), BF16)]
EARLY_SCRATCH = HELD + [pltpu.SemaphoreType.DMA((6,))]


def finish_kernel(flags, kept, received, evolved):
    order = order_matrix(flags[0] == 1)
    rest = jnp.dot(order, received[...], preferred_element_type=F32)
    mine = kept[...]
    half = flags[3]
    evolved[:, 0, :LANES] = jnp.where(half == 0, mine, rest)[:ROWS]
    evolved[:, 0, LANES:] = jnp.where(half == 0, rest, mine)[:ROWS]


def place(rows, columns, wanted):
    return (lax.broadcasted_iota(jnp.int32, (rows, columns), 0) == wanted[None, :]).astype(BF16)


def chosen(left, right):
    return jnp.dot(left, right, preferred_element_type=BF16)


def column_half(wide, block):
    column = lax.iota(jnp.int32, PAD)
    inside = column < ROWS
    start_a, start_b = 640 * block, jnp.where(block == 1, 1280, 2048)
    part_a = lax.dynamic_slice(wide, (0, start_a), (wide.shape[0], 768))
    part_b = lax.dynamic_slice(wide, (0, start_b), (wide.shape[0], 896))
    wanted_a = jnp.where(inside, ROWS * block + column - start_a, -1)
    wanted_b = jnp.where(inside, 4 * ROWS - 1 - ROWS * block - column - start_b, -1)
    halves = chosen(part_a, place(768, PAD, wanted_a)), chosen(part_b, place(896, PAD, wanted_b))
    return halves


def padded_columns(matrix):
    return jnp.pad(matrix, ((0, 0), (0, 2944 - matrix.shape[1])))


def per_device(populations, solid_mask, collision):
    cell, vel = lax.axis_index("cells"), lax.axis_index("vel")
    low = (vel < 2).astype(jnp.int32)
    core, ring_place = cell % 2, cell // 32 + 4 * (cell // 2 % 2)
    block = jnp.minimum(vel, 3 - vel)
    half = (1 - low) ^ (cell // RING % 2)
    needing = (cell + 1 - 2 * low) % 128
    straight_half = (1 - low) ^ (needing // RING % 2)
    same = (low != core).astype(jnp.int32)
    flags = jnp.stack([low, 1 - core, block, half, same, straight_half])
    flags = flags.astype(jnp.int32)

    first_row = CHUNK * ring_place
    row = first_row + lax.iota(jnp.int32, CHUNK)
    start = jnp.clip(jnp.where(low == 1, first_row, ROWS - CHUNK - first_row), 0, ROWS - CHUNK)
    wanted = jnp.where(row < ROWS, jnp.where(low == 1, row, ROWS - 1 - row) - start, -1)
    window = lax.dynamic_slice(collision, (start, 0), (CHUNK, collision.shape[1]))
    window = padded_columns(chosen(place(CHUNK, CHUNK, wanted).T, window))
    piece = jnp.concatenate(column_half(window, core), axis=1)
    populations, piece = lax.optimization_barrier((populations, piece))
    piece = to_mirror(piece)

    padded = jnp.pad(populations[:, 0, :], ((0, PAD - ROWS), (0, 0)))
    rows = (PAD, LANES)
    own, own_edge, message, straight, turned, masks, factors = call(
        prepare_kernel,
        [(rows, F32), ((CHUNK, LANES), F32), ((PAD + EDGE, LANES), BF16),
         ((PAD + 16, LANES), BF16), ((PAD + 16, LANES), BF16), ((8, LANES), F32), ((3, *rows), F32)],
        flags, padded, solid_mask, flops=2 * 3 * PAD * PAD * 256,
    )
    piece, straight, turned = lax.optimization_barrier((piece, straight, turned))
    groups = [
        [x * 32 + y * 16 + 4 * pair + 2 * odd + side for side in range(2) for odd in range(2) for x in range(4)]
        for y in range(2)
        for pair in range(4)
    ]
    partner_matrix = lax.all_gather(piece, "cells", axis=0, tiled=True, axis_index_groups=groups)
    turned = to_layer(turned, True)
    received = to_mirror(message)

    row = lax.iota(jnp.int32, PAD)
    wanted = jnp.where(row < ROWS, jnp.where(low == 1, row, ROWS - 1 - row), -1)
    message, collision = lax.optimization_barrier((message, collision))
    ordered = padded_columns(chosen(place(ROWS, PAD, wanted).T, collision))

    straight, ordered = lax.optimization_barrier((straight, ordered))
    straight = to_layer(straight, False)
    matrix = *column_half(ordered, 0), *column_half(ordered, 1)
    turned, *matrix = lax.optimization_barrier((turned, *matrix))
    lowered, masks, bands = call(
        first_kernel,
        [((2 * PAD, LANES), BF16), ((8, LANES), F32), ((BAND, LANES), BF16)],
        flags, own, own_edge, received, straight, turned, masks, factors, flops=100 * PAD * 256,
    )
    edges_shape = ((2 * EDGE, LANES), BF16)
    sends = [(rows, F32)] * 2 + [(rows, BF16)] * 2 + [edges_shape]
    multiply = 2 * PAD * 4 * PAD * LANES
    work = 100 * PAD * LANES

    other = to_side(lowered)
    bands = to_mirror(bands), to_opposite(bands)
    own, own_packed, all_rows, all_bands = call(
        collide_kernel,
        [(rows, F32), ((EDGE, LANES), BF16), ((4 * PAD, LANES), BF16), ((2 * BAND, LANES), BF16)],
        flags, lowered, other, *bands, factors, *matrix, flops=2 * multiply, leave=True,
    )
    partner_matrix, own = lax.optimization_barrier((partner_matrix, own))
    near, far, for_sibling, for_neighbour, edges = call(
        collide_partner_kernel, sends, flags, factors, own_packed, all_rows, all_bands, own, partner_matrix,
        flops=2 * multiply, stay=5, scratch=PARTNER_SCRATCH,
    )

    for step in range(1, STEPS):
        neighbour, sibling = to_neighbour(for_neighbour), with_sibling(for_sibling)
        new_near, for_neighbour, packed = call(
            between_near_kernel, [(rows, F32), (rows, BF16), ((EDGE, LANES), BF16)],
            flags, near, far, sibling, edges, masks, factors, flops=work,
        )
        new_far, for_sibling, edges = call(
            between_far_kernel, [(rows, F32), (rows, BF16), edges_shape],
            flags, near, far, neighbour, edges, masks, factors, packed, flops=work,
        )
        near, far = new_near, new_far
        neighbour, edges = to_neighbour(for_neighbour), to_mirror(edges)
        sibling = with_sibling(for_sibling)
        (lowered,) = call(
            lower_kernel, [((2 * PAD, LANES), BF16)],
            flags, near, far, sibling, neighbour, edges, masks, factors, flops=work,
        )
        other = to_side(lowered)
        early = call(
            early_kernel, EARLY, flags, lowered, *matrix, partner_matrix,
            flops=multiply, stay=5, scratch=EARLY_SCRATCH,
        )
        near, far, for_sibling, for_neighbour, edges = call(
            late_kernel, sends, flags, other, *early[:2], factors, *early[2:], flops=multiply
        )

    neighbour, edges = to_neighbour(for_neighbour), to_mirror(edges)
    sibling = with_sibling(for_sibling)
    last = flags, near, far, sibling, neighbour, edges, masks, factors
    (message,) = call(functools.partial(last_kernel, True), [(rows, BF16)], *last, flops=work)
    received = to_mirror(message)
    (kept,) = call(functools.partial(last_kernel, False), [(rows, F32)], *last, flops=multiply)
    (evolved,) = call(
        finish_kernel, [((ROWS, 1, 2 * LANES), F32)], flags, kept, received, flops=2 * PAD * PAD * LANES
    )
    return evolved


def solution(mesh):
    in_specs = (P("vel", "cells", None), P("cells", None), P("vel", None))
    out_specs = P("vel", "cells", None)
    return jax.shard_map(
        per_device, mesh=mesh, in_specs=in_specs, out_specs=out_specs, check_vma=False
    )
```
